256 devices in a mesh: dom: 32 (over x, y, core), row: 8 (over z).
Axes of the slice: x: 4, y: 4, z: 8, core: 2. Of those that a mesh axis runs over, the one named last changes fastest.
Arguments:
- basis: float32 [16, 1048576], P(None, ('dom', 'row')), may hold values from -6 to 6
- previous: float32 [16, 1048576], P(None, ('dom', 'row')), may hold values from -3 to 3
- previous_image: float32 [16, 1048576], P(None, ('dom', 'row')), may hold values from -12 to 12
- degree: float32 [1048576], P(('dom', 'row')), may hold values from 1 to 8
- coupling: bfloat16 [65536, 128, 128], P(('dom', 'row')), may hold values from -0.1875 to 0.1875
- slot_row: int32 [65536], P(('dom', 'row')), may hold values from 0 to 31
- slot_column: int32 [65536], P(('dom', 'row')), may hold values from 0 to 511
- send_lists: int32 [32, 32, 8], P('dom'), may hold values from 0 to 255
- live_slots: int32 [256], P(('dom', 'row')), may hold values from 32 to 256, as said below
Outputs:
- new_basis: float32 [16, 1048576], P(None, ('dom', 'row'))
- new_image: float32 [16, 1048576], P(None, ('dom', 'row'))
The draws below stay inside these ranges and needn't reach their ends.
Inputs may be any that keep to these rules, and one draw needn't show every extreme that they name: `live_slots`: each device has a block count; some device uses all 256 of its slots and some device uses 256 // 8.
All inputs are finite; a program needn't handle non-finite values. Where the reference program divides by a largest or mean magnitude, that divisor is 1e-20 or more.
Results may differ from the reference program's by a relative error of at most 0.002.
Values may be sent and summed in bfloat16 or wider, within the bound.
No kernel may reach another device: no remote copies, remote signals or barrier semaphores. Data moves between devices by JAX's collectives and lax.ppermute only.
A program may use at most 64 MiB of HBM per device.

```python
import math
import jax
import jax.numpy as jnp
from jax import lax

K = 16
BS = 128
SLOTS = 8
SEND = 8
RB = 32
BLK_DEV = 256
GROUP_DEVS = 8
PARTS_SIZE = 32
PART = 256
HALO = 256
NB = 8192
BLK_ALL = 65536
NROWS = 1048576
N_DOM = 32
N_ROW = 8


def draw_live_slots(key, part):
    key = jax.random.fold_in(key, 7)
    first, second = jax.random.split(key, 2)
    devices = PARTS_SIZE * GROUP_DEVS
    divisors = jnp.array([1, 2, 4, 8], dtype=jnp.int32)
    picks = jax.random.randint(first, (devices,), 0, 4)
    counts = BLK_DEV // divisors[picks]
    chosen = jax.random.permutation(second, devices)
    counts = counts.at[chosen[0]].set(BLK_DEV)
    counts = counts.at[chosen[1]].set(BLK_DEV // 8)
    return counts.astype(jnp.int32)


def draw_basis(key, part):
    key = jax.random.fold_in(key, 11)
    sign_key, level_key, noise_key = jax.random.split(key, 3)
    signs = jnp.where(jax.random.bernoulli(sign_key, 0.5, (K, 1)), 1.0, -1.0).astype(jnp.float32)
    ramp = 0.6 + 1.2 * jnp.arange(NROWS, dtype=jnp.float32) / NROWS
    level = jax.random.uniform(level_key, (K, 1), jnp.float32, 0.7, 1.2)
    noise = jnp.clip(jax.random.normal(noise_key, (K, NROWS), jnp.float32), -3.8, 3.8)
    return (signs * level * ramp[None, :] + noise).astype(jnp.float32)


def draw_coupling(key, part):
    key = jax.random.fold_in(key, 13)
    fan_scale = (SLOTS * BS) ** (-0.5)
    shape = (BLK_ALL, BS, BS)
    noise = jnp.clip(jax.random.normal(key, shape, jnp.float32), -5.0, 5.0)
    values = noise * fan_scale + fan_scale * fan_scale
    return values.astype(jnp.bfloat16)


def touch_ends(values, own_key, smallest, top_value):
    shape = values.shape
    index_at = [jax.random.randint(jax.random.fold_in(own_key, axis), (), 0, shape[axis]) for axis in range(len(shape))]
    values = values.at[tuple(index_at)].set(smallest)
    longest = shape.index(max(shape))
    index_at[longest] = (index_at[longest] + 1) % shape[longest]
    return values.at[tuple(index_at)].set(top_value)


def level_of(key, dims, pieces, smallest, largest):
    factor_of, own = 1.0, jax.random.fold_in(key, 6)
    for dim, parts in pieces:
        heights = jnp.exp(jax.random.uniform(jax.random.fold_in(own, dim), (parts,), jnp.float32, smallest / len(pieces), largest / len(pieces)))
        factor_of = factor_of * jnp.repeat(heights, dims[dim] // parts).reshape([-1 if axis == dim else 1 for axis in range(len(dims))])
    return factor_of


def scatter_about(key, shape, scale, most, cuts=(), kind=jnp.bfloat16):
    values = jax.random.normal(key, shape, jnp.float32) * scale
    if len(cuts) > 0:
        values = level_of(key, shape, cuts, -0.22, 0.18) * values
    return jnp.clip(values, min=-most, max=most).astype(kind)


def setup_inputs(seed: int = 0) -> dict:
    key_list = jax.random.split(jax.random.key(seed), 10)
    basis = draw_basis(jax.random.fold_in(key_list[9], 71), 0)
    previous = scatter_about(key_list[1], (K, NROWS), 0.5, 3.0, ((1, 256),), jnp.float32)
    previous_image = scatter_about(key_list[2], (K, NROWS), 2.0, 12.0, ((1, 256),), jnp.float32)
    degree = jnp.clip(jnp.exp(math.log(8.0) - 2.0794415 * jax.random.uniform(key_list[3], (NROWS,), jnp.float32) ** level_of(key_list[3], (NROWS,), ((0, 256),), -0.2, 0.2)), 1.0, 8.0)
    coupling = draw_coupling(jax.random.fold_in(key_list[9], 71), 0)
    slot_row = touch_ends(jax.random.randint(key_list[5], (BLK_ALL,), 0, RB), jax.random.fold_in(key_list[5], 1), 0, RB - 1).astype(jnp.int32)
    slot_column = touch_ends(jax.random.randint(key_list[6], (BLK_ALL,), 0, PART + HALO), jax.random.fold_in(key_list[6], 1), 0, (PART + HALO) - 1).astype(jnp.int32)
    send_lists = touch_ends(jax.random.randint(key_list[7], (PARTS_SIZE, PARTS_SIZE, SEND), 0, PART), jax.random.fold_in(key_list[7], 1), 0, PART - 1).astype(jnp.int32)
    live_slots = draw_live_slots(jax.random.fold_in(key_list[9], 71), 0)
    return dict(basis=basis, previous=previous, previous_image=previous_image, degree=degree, coupling=coupling, slot_row=slot_row, slot_column=slot_column, send_lists=send_lists, live_slots=live_slots)


def couple_device(lookup, dev_coupling, dev_rows, dev_cols, dev_live):
    picked = lookup[dev_cols].astype(jnp.float32)
    product = jnp.einsum('skc,sjc->skj', picked, dev_coupling.astype(jnp.float32))
    live_mask = jnp.arange(dev_rows.shape[0], dtype=jnp.int32) < dev_live
    product = jnp.where(live_mask[:, None, None], product, jnp.float32(0.0))
    return jax.ops.segment_sum(product, dev_rows, num_segments=RB)

def couple(field_half, coupling, slot_row, slot_column, send_lists, live_slots):
    devices = N_DOM * N_ROW
    tile_rows = field_half.reshape(K, NB, BS).transpose(1, 0, 2)
    grouped = coupling.reshape(devices, BLK_DEV, BS, BS)
    slot_rows = slot_row.reshape(devices, BLK_DEV)
    slot_cols = slot_column.reshape(devices, BLK_DEV)

    def per_device(operands):
        device_id, dev_coupling, dev_rows, dev_cols, dev_live = operands
        partition = device_id // N_ROW
        own_part = lax.dynamic_slice_in_dim(tile_rows, (partition * PART).astype(jnp.int32), PART, 0)
        sources = (jnp.arange(N_DOM, dtype=jnp.int32)[:, None] * PART + send_lists[:, partition, :]).reshape(-1)
        lookup = jnp.concatenate([own_part, tile_rows[sources]], axis=0)
        return couple_device(lookup, dev_coupling, dev_rows, dev_cols, dev_live)
    result = lax.map(per_device, (jnp.arange(devices, dtype=jnp.int32), grouped, slot_rows, slot_cols, live_slots))
    return result.transpose(2, 0, 1, 3).reshape(K, NB * BS)

def ritz(gram_a, gram_b, count):
    highest = lax.Precision.HIGHEST
    symmetric = 0.5 * (gram_a + gram_a.T)
    factor = jnp.linalg.cholesky(gram_b)
    partial_solve = lax.linalg.triangular_solve(factor, symmetric, left_side=True, lower=True)
    reduced = lax.linalg.triangular_solve(factor, partial_solve.T, left_side=True, lower=True)
    reduced = 0.5 * (reduced + reduced.T)
    spread = jnp.max(lax.optimization_barrier(jnp.sum(jnp.abs(reduced), axis=1)))
    dimension = reduced.shape[0]
    filter_mat = (spread * jnp.eye(dimension, dtype=jnp.float32) - reduced) / (2.0 * spread)
    subspace = jnp.eye(dimension, count, dtype=jnp.float32)
    for repeat in range(4):
        subspace = jnp.dot(filter_mat.astype(jnp.float32), subspace.astype(jnp.float32), precision=highest, preferred_element_type=jnp.float32)
    inner_gram = jnp.dot(subspace.T.astype(jnp.float32), subspace.astype(jnp.float32), precision=highest, preferred_element_type=jnp.float32)
    sub_factor = jnp.linalg.cholesky(inner_gram)
    orthonormal = lax.linalg.triangular_solve(sub_factor, subspace.T, left_side=True, lower=True).T
    return lax.linalg.triangular_solve(factor, orthonormal, left_side=True, lower=True, transpose_a=True)

def reference(basis, previous, previous_image, degree, coupling, slot_row, slot_column, send_lists, live_slots):
    highest = lax.Precision.HIGHEST
    basis_half = basis.astype(jnp.bfloat16)
    image = degree * basis - couple(basis_half, coupling, slot_row, slot_column, send_lists, live_slots)
    theta = lax.optimization_barrier(jnp.sum(basis * image, axis=1)) / lax.optimization_barrier(jnp.sum(basis * basis, axis=1))
    residual = (image - theta[:, None] * basis) / degree
    residual_half = residual.astype(jnp.bfloat16)
    residual_image = degree * residual - couple(residual_half, coupling, slot_row, slot_column, send_lists, live_slots)
    stacked = jnp.concatenate([basis, residual, previous], axis=0)
    stacked_image = jnp.concatenate([image, residual_image, previous_image], axis=0)
    gram_b = jnp.dot(stacked.astype(jnp.float32), stacked.T.astype(jnp.float32), precision=highest, preferred_element_type=jnp.float32)
    gram_a = jnp.dot(stacked.astype(jnp.float32), stacked_image.T.astype(jnp.float32), precision=highest, preferred_element_type=jnp.float32)
    coeff = ritz(gram_a, gram_b, K)
    root_rows = math.sqrt(NROWS)
    new_basis = root_rows * jnp.dot(coeff.T.astype(jnp.float32), stacked.astype(jnp.float32), precision=highest, preferred_element_type=jnp.float32)
    new_image = root_rows * jnp.dot(coeff.T.astype(jnp.float32), stacked_image.astype(jnp.float32), precision=highest, preferred_element_type=jnp.float32)
    return (new_basis, new_image)
```

```python
import functools
import math

import jax
import jax.numpy as jnp
from jax import lax
from jax.experimental import pallas as pl
from jax.experimental.pallas import tpu as pltpu
from jax.sharding import PartitionSpec as P

K = 16
BS = 128
RB = 32
SLOTS = 256
SEND = 8
LEN = SLOTS + 8
F32 = jnp.float32
BF16 = jnp.bfloat16
HIGHEST = lax.Precision.HIGHEST
VMEM_LIMIT = 48 * 1024 * 1024
SMEM = pl.BlockSpec(memory_space=pltpu.SMEM)
HBM = pl.BlockSpec(memory_space=pl.ANY)
VMEM = pl.BlockSpec(memory_space=pltpu.VMEM)


def call(kernel, out_shape, in_specs, out_specs, scratch=(), flops=0, moved=0):
    return pl.pallas_call(
        kernel,
        out_shape=out_shape,
        in_specs=in_specs,
        out_specs=out_specs,
        scratch_shapes=scratch,
        compiler_params=pltpu.CompilerParams(vmem_limit_bytes=VMEM_LIMIT),
        cost_estimate=pl.CostEstimate(flops=flops, bytes_accessed=moved, transcendentals=0),
    )


def shaped(shape, dtype):
    return jax.ShapeDtypeStruct(shape, dtype)


def dot_nt(left, right, precision=None):
    return lax.dot_general(
        left, right, (((1,), (1,)), ((), ())), precision=precision, preferred_element_type=F32
    )


def dot_nn(left, right, precision=None):
    return lax.dot_general(
        left, right, (((1,), (0,)), ((), ())), precision=precision, preferred_element_type=F32
    )


def columns(block):
    return slice(block * BS, (block + 1) * BS)


def list_kernel(part, row_ref, column_ref, live_ref, own_ref, halo_ref, count_ref):
    live = live_ref[0]

    def step(slot, counts):
        n_own, n_halo = counts
        column = column_ref[slot]
        row = row_ref[slot]
        own_ref[0, n_own] = slot
        own_ref[1, n_own] = column
        own_ref[2, n_own] = row
        halo_ref[0, n_halo] = slot
        halo_ref[1, n_halo] = column - part
        halo_ref[2, n_halo] = row
        used = slot < live
        is_own = column < part
        n_own = n_own + jnp.where(used & is_own, 1, 0)
        n_halo = n_halo + jnp.where(used & (column >= part), 1, 0)
        return n_own, n_halo

    n_own, n_halo = lax.fori_loop(0, SLOTS, step, (jnp.int32(0), jnp.int32(0)))
    for ref, count in ((own_ref, n_own), (halo_ref, n_halo)):
        for extra in range(8):
            ref[0, count + extra] = 0
            ref[1, count + extra] = 0
            ref[2, count + extra] = RB
    count_ref[0] = n_own
    count_ref[1] = n_halo


def make_lists(slot_row, slot_column, live_slots, part):
    return call(
        functools.partial(list_kernel, part),
        (shaped((3, LEN), jnp.int32), shaped((3, LEN), jnp.int32), shaped((2,), jnp.int32)),
        [SMEM, SMEM, SMEM],
        (SMEM, SMEM, SMEM),
        moved=20000,
    )(slot_row, slot_column, live_slots)


def cast_kernel(field_ref, tiles_ref):
    for block in range(RB):
        tiles_ref[block] = field_ref[:, columns(block)].astype(BF16)


def cast_tiles(field):
    return call(cast_kernel, shaped((RB, K, BS), BF16), [VMEM], VMEM, moved=400000)(field)


def gather_row(tiles, n_row):
    up = [(i, (i + 1) % n_row) for i in range(n_row)]
    down = [(i, (i - 1) % n_row) for i in range(n_row)]
    pieces = [(0, tiles)]
    from_below = from_above = tiles
    for step in range(1, n_row // 2):
        from_below = lax.ppermute(from_below, "row", up)
        from_above = lax.ppermute(from_above, "row", down)
        pieces += [(-step, from_below), (step, from_above)]
    half = RB // 2
    far_low = lax.ppermute(from_below[:half], "row", up)
    far_high = lax.ppermute(from_above[half:], "row", down)
    return pieces, far_low, far_high


def select_kernel(offsets, n_row, place_ref, send_ref, *refs):
    pieces, (far_low, far_high, part_ref, chosen_ref) = refs[: len(offsets)], refs[len(offsets) :]
    place = place_ref[0]
    half = RB // 2
    for offset, piece in zip(offsets, pieces):
        owner = lax.rem(place + offset + n_row, n_row)
        part_ref[pl.ds(owner * RB, RB)] = piece[...]
    owner = lax.rem(place + n_row // 2, n_row)
    part_ref[pl.ds(owner * RB, half)] = far_low[...]
    part_ref[pl.ds(owner * RB + half, half)] = far_high[...]

    def step(group, carry):
        for j in range(8):
            chosen_ref[group * 8 + j] = part_ref[send_ref[group * 8 + j]]
        return carry

    lax.fori_loop(0, chosen_ref.shape[0] // 8, step, 0)


def select(gathered, place, send_list, n_row):
    pieces, far_low, far_high = gathered
    offsets = [offset for offset, _ in pieces]
    count = send_list.shape[0]
    return call(
        functools.partial(select_kernel, offsets, n_row),
        (shaped((n_row * RB, K, BS), BF16), shaped((count, K, BS), BF16)),
        [SMEM, SMEM] + [VMEM] * (len(pieces) + 2),
        (VMEM, VMEM),
        moved=3000000,
    )(place, send_list, *[piece for _, piece in pieces], far_low, far_high)


def apply_list(count, list_ref, lookup_ref, coupling_ref, held, sems, acc_ref):
    groups = lax.div(count + 7, 8)

    def issue(group, carry):
        for j in range(8):
            at = group * 8 + j
            pltpu.make_async_copy(
                coupling_ref.at[list_ref[0, at]], held.at[at], sems.at[group]
            ).start()
        return carry

    lax.fori_loop(0, groups, issue, 0)

    def work(group, carry):
        base = group * 8
        pltpu.make_async_copy(
            coupling_ref.at[pl.ds(0, 8)], held.at[pl.ds(base, 8)], sems.at[group]
        ).wait()
        products = [
            dot_nt(lookup_ref[list_ref[1, base + j]], held[base + j]) for j in range(8)
        ]
        for j in range(8):
            row = list_ref[2, base + j]
            acc_ref[row] = acc_ref[row] + products[j]
        return carry

    lax.fori_loop(0, groups, work, 0)


HELD = (pltpu.VMEM((SLOTS, BS, BS), BF16), pltpu.SemaphoreType.DMA((SLOTS // 8,)))


def own_kernel(list_ref, count_ref, lookup_ref, coupling_ref, acc_ref, held, sems):
    acc_ref[...] = jnp.zeros_like(acc_ref)
    apply_list(count_ref[0], list_ref, lookup_ref, coupling_ref, held, sems, acc_ref)


def couple_own(own_list, counts, part_tiles, coupling):
    return call(
        own_kernel,
        shaped((RB + 1, K, BS), F32),
        [SMEM, SMEM, VMEM, HBM],
        VMEM,
        HELD,
        flops=2 * SLOTS * K * BS * BS,
        moved=8000000,
    )(own_list, counts, part_tiles, coupling)


def image_kernel(
    list_ref, count_ref, lookup_ref, coupling_ref, own_ref, basis_ref, degree_ref,
    image_ref, sums_ref, acc_ref, held, sems,
):
    acc_ref[...] = own_ref[...]
    apply_list(count_ref[1], list_ref, lookup_ref, coupling_ref, held, sems, acc_ref)
    top = jnp.zeros((K, BS), F32)
    bottom = jnp.zeros((K, BS), F32)
    for block in range(RB):
        at = columns(block)
        basis = basis_ref[:, at]
        image = degree_ref[:, at] * basis - acc_ref[block]
        image_ref[:, at] = image
        top = top + basis * image
        bottom = bottom + basis * basis
    lane = lax.broadcasted_iota(jnp.int32, (K, BS), 1)
    sums = jnp.where(
        lane == 0, jnp.sum(top, axis=1, keepdims=True), jnp.sum(bottom, axis=1, keepdims=True)
    )
    for peer in range(sums_ref.shape[0]):
        sums_ref[peer] = sums


def make_image(halo_list, counts, halo_tiles, coupling, own, basis, degree, n_dom):
    return call(
        image_kernel,
        (shaped(basis.shape, F32), shaped((n_dom, K, BS), F32)),
        [SMEM, SMEM, VMEM, HBM, VMEM, VMEM, VMEM],
        (VMEM, VMEM),
        (pltpu.VMEM((RB + 1, K, BS), F32),) + HELD,
        flops=2 * SLOTS * K * BS * BS,
        moved=8000000,
    )(halo_list, counts, halo_tiles, coupling, own, basis, degree)


def spread_kernel(taken_ref, given_ref):
    total = taken_ref[0]
    for peer in range(1, taken_ref.shape[0]):
        total = total + taken_ref[peer]
    for peer in range(given_ref.shape[0]):
        given_ref[peer] = total


def add_and_repeat(taken, peers):
    return call(
        spread_kernel, shaped((peers,) + taken.shape[1:], F32), [VMEM], VMEM, moved=400000
    )(taken)


def residual_kernel(sums_ref, basis_ref, image_ref, degree_ref, residual_ref, tiles_ref):
    sums = sums_ref[0]
    for peer in range(1, sums_ref.shape[0]):
        sums = sums + sums_ref[peer]
    theta = sums[:, 0:1] / sums[:, 1:2]
    for block in range(RB):
        at = columns(block)
        residual = (image_ref[:, at] - theta * basis_ref[:, at]) / degree_ref[:, at]
        residual_ref[:, at] = residual
        tiles_ref[block] = residual.astype(BF16)


def make_residual(sums, basis, image, degree):
    return call(
        residual_kernel,
        (shaped(basis.shape, F32), shaped((RB, K, BS), BF16)),
        [VMEM] * 4,
        (VMEM, VMEM),
        moved=1000000,
    )(sums, basis, image, degree)


def iota2(shape, axis):
    return lax.broadcasted_iota(jnp.int32, shape, axis)


def square(value, wide_ref):
    rows, cols = value.shape
    wide_ref[...] = jnp.zeros_like(wide_ref)
    wide_ref[0:rows, 0:cols] = value
    return wide_ref[...]


def pack_grams(gram_b, gram_a, wide_ref):
    wide_a = square(gram_a, wide_ref)
    both = 0.5 * (wide_a + wide_a.T)
    wide_b = square(gram_b, wide_ref)
    row = iota2((BS, BS), 0)
    lane = iota2((BS, BS), 1)
    packed = jnp.where(row <= lane, wide_b, both)
    diagonal = jnp.sum(jnp.where(row == lane, both, 0.0), axis=1, keepdims=True)
    low, high = packed[0:24], pltpu.roll(packed[24:48], 48, 1)
    at = iota2((24, BS), 1)
    out = jnp.where(at < 48, low, high)
    out = jnp.where(at == 96, diagonal[0:24], out)
    return jnp.where(at == 97, diagonal[24:48], out)


def unpack_grams(packed, wide_ref):
    wide_ref[...] = jnp.zeros_like(wide_ref)
    at = iota2((24, BS), 1)
    wide_ref[0:24] = jnp.where(at < 48, packed, 0.0)
    wide_ref[24:48] = jnp.where(at < 48, pltpu.roll(packed, 80, 1), 0.0)
    wide = wide_ref[...]
    flipped = wide.T
    row = iota2((48, BS), 0)
    lane = iota2((48, BS), 1)
    wide, flipped = wide[0:48], flipped[0:48]
    diagonal = jnp.concatenate([packed[:, 96:97], packed[:, 97:98]], axis=0)
    gram_b = jnp.where(row <= lane, wide, flipped)
    gram_a = jnp.where(row == lane, diagonal, jnp.where(row > lane, wide, flipped))
    return gram_b, gram_a


def gram_kernel(
    list_ref, count_ref, lookup_ref, coupling_ref, own_ref, basis_ref, image_ref, residual_ref, degree_ref,
    previous_ref, previous_image_ref, residual_image_ref, packed_ref, acc_ref, held, sems, stacked, stacked_image,
    wide_ref,
):
    acc_ref[...] = own_ref[...]
    apply_list(count_ref[1], list_ref, lookup_ref, coupling_ref, held, sems, acc_ref)
    stacked[0:16] = basis_ref[...]
    stacked[16:32] = residual_ref[...]
    stacked[32:48] = previous_ref[...]
    stacked_image[0:16] = image_ref[...]
    stacked_image[32:48] = previous_image_ref[...]
    for block in range(RB):
        at = columns(block)
        value = degree_ref[:, at] * residual_ref[:, at] - acc_ref[block]
        residual_image_ref[:, at] = value
        stacked_image[16:32, at] = value
    gram_b = dot_nt(stacked[...], stacked[...], HIGHEST)
    gram_a = dot_nt(stacked[...], stacked_image[...], HIGHEST)
    packed = pack_grams(gram_b, gram_a, wide_ref)
    for peer in range(packed_ref.shape[0]):
        packed_ref[peer] = packed


def make_grams(
    halo_list, counts, halo_tiles, coupling, own, basis, image, residual, degree, previous, previous_image, n_dom
):
    width = basis.shape[1]
    return call(
        gram_kernel,
        (shaped(basis.shape, F32), shaped((n_dom, 24, BS), F32)),
        [SMEM, SMEM, VMEM, HBM] + [VMEM] * 7,
        (VMEM, VMEM),
        (pltpu.VMEM((RB + 1, K, BS), F32),)
        + HELD
        + (pltpu.VMEM((48, width), F32), pltpu.VMEM((48, width), F32), pltpu.VMEM((BS, BS), F32)),
        flops=2 * SLOTS * K * BS * BS,
        moved=10000000,
    )(halo_list, counts, halo_tiles, coupling, own, basis, image, residual, degree, previous, previous_image)


def inverse_factor(gram, n):
    row = iota2((n, BS), 0)
    lane = iota2((n, BS), 1)
    work = jnp.where(lane < n, gram, jnp.where(lane == row + n, 1.0, 0.0))
    for j in range(n):
        column = work[:, j : j + 1]
        pivot = work[j : j + 1, :]
        scale = lax.rsqrt(work[j : j + 1, j : j + 1])
        scaled = pivot * scale
        below = jnp.where(row[:, 0:1] > j, column * scale, 0.0)
        work = jnp.where(row == j, scaled, work - below * scaled)
    return pltpu.roll(work, BS - n, 1)


def final_kernel(
    root_rows, taken_ref, basis_ref, residual_ref, previous_ref, image_ref, residual_image_ref, previous_image_ref,
    new_basis_ref, new_image_ref, wide_ref, stacked,
):
    packed = taken_ref[0]
    for peer in range(1, taken_ref.shape[0]):
        packed = packed + taken_ref[peer]
    gram_b, gram_a = unpack_grams(packed, wide_ref)
    inverse = inverse_factor(gram_b, 48)[:, 0:48]
    symmetric = gram_a[:, 0:48]
    reduced = dot_nt(dot_nn(inverse, symmetric, HIGHEST), inverse, HIGHEST)
    wide = square(reduced, wide_ref)
    reduced = 0.5 * (wide + wide.T)[0:48, 0:48]
    spread = jnp.max(jnp.sum(jnp.abs(reduced), axis=1, keepdims=True), axis=0, keepdims=True)
    row = iota2((48, 48), 0)
    lane = iota2((48, 48), 1)
    filter_mat = (jnp.where(row == lane, spread, 0.0) - reduced) / (2.0 * spread)
    subspace = filter_mat[:, 0:16]
    for repeat in range(3):
        subspace = dot_nn(filter_mat, subspace, HIGHEST)
    wide_ref[...] = jnp.zeros_like(wide_ref)
    wide_ref[0:48, 0:16] = subspace
    turned = wide_ref[...].T[0:16, 0:48]
    inner = dot_nt(turned, turned, HIGHEST)
    wide_ref[...] = jnp.zeros_like(wide_ref)
    wide_ref[0:16, 0:16] = inner
    sub_inverse = inverse_factor(wide_ref[0:16, :], 16)[:, 0:16]
    coeff = dot_nn(dot_nn(sub_inverse, turned, HIGHEST), inverse, HIGHEST) * root_rows
    stacked[0:16] = basis_ref[...]
    stacked[16:32] = residual_ref[...]
    stacked[32:48] = previous_ref[...]
    new_basis_ref[...] = dot_nn(coeff, stacked[...], HIGHEST)
    stacked[0:16] = image_ref[...]
    stacked[16:32] = residual_image_ref[...]
    stacked[32:48] = previous_image_ref[...]
    new_image_ref[...] = dot_nn(coeff, stacked[...], HIGHEST)


def finish(root_rows, packed, basis, residual, previous, image, residual_image, previous_image):
    return call(
        functools.partial(final_kernel, root_rows),
        (shaped(basis.shape, F32), shaped(basis.shape, F32)),
        [VMEM] * 7,
        (VMEM, VMEM),
        (pltpu.VMEM((BS, BS), F32), pltpu.VMEM((48, basis.shape[1]), F32)),
        flops=1000000,
        moved=3000000,
    )(packed, basis, residual, previous, image, residual_image, previous_image)


def to_all(value, axis):
    return lax.all_to_all(value, axis, split_axis=0, concat_axis=0, tiled=True)


def body(
    n_dom, n_row,
    basis, previous, previous_image, degree, coupling, slot_row, slot_column, send_lists, live_slots,
):
    part = n_row * RB
    place = lax.axis_index("row").astype(jnp.int32).reshape(1)
    send_list = send_lists.reshape(n_dom * SEND)
    degree = degree.reshape(1, -1)
    own_list, halo_list, counts = make_lists(slot_row, slot_column, live_slots, part)

    part_tiles, chosen = select(gather_row(cast_tiles(basis), n_row), place, send_list, n_row)
    halo_tiles = to_all(chosen, "dom")
    own = couple_own(own_list, counts, part_tiles, coupling)
    image, sums = make_image(halo_list, counts, halo_tiles, coupling, own, basis, degree, n_dom)
    sums = to_all(add_and_repeat(to_all(sums, "dom"), n_row), "row")
    residual, tiles = make_residual(sums, basis, image, degree)

    part_tiles, chosen = select(gather_row(tiles, n_row), place, send_list, n_row)
    halo_tiles = to_all(chosen, "dom")
    own = couple_own(own_list, counts, part_tiles, coupling)
    residual_image, packed = make_grams(
        halo_list, counts, halo_tiles, coupling, own, basis, image, residual, degree, previous, previous_image, n_dom
    )
    packed = to_all(add_and_repeat(to_all(packed, "dom"), n_row), "row")
    root_rows = math.sqrt(basis.shape[1] * n_dom * n_row)
    return finish(root_rows, packed, basis, residual, previous, image, residual_image, previous_image)


def solution(mesh):
    split = P(None, ("dom", "row"))
    flat = P(("dom", "row"))
    return jax.shard_map(
        functools.partial(body, mesh.shape["dom"], mesh.shape["row"]),
        mesh=mesh,
        in_specs=(
            split, split, split, flat, P(("dom", "row"), None, None), flat, flat, P("dom", None, None), flat,
        ),
        out_specs=(split, split),
        check_vma=False,
    )
```

```python
import functools
import math

import jax
import jax.numpy as jnp
from jax import lax
from jax.experimental import pallas as pl
from jax.experimental.pallas import tpu as pltpu
from jax.sharding import PartitionSpec as P

K = 16
BS = 128
RB = 32
SLOTS = 256
SEND = 8
HALF = RB // 2
EXTRA = SEND + 1
LEN = SLOTS + 8
F32 = jnp.float32
BF16 = jnp.bfloat16
HIGHEST = lax.Precision.HIGHEST
VMEM_LIMIT = 48 * 1024 * 1024
SMEM = pl.BlockSpec(memory_space=pltpu.SMEM)
HBM = pl.BlockSpec(memory_space=pl.ANY)
VMEM = pl.BlockSpec(memory_space=pltpu.VMEM)


def call(kernel, out_shape, in_specs, out_specs, scratch=(), flops=0, moved=0):
    return pl.pallas_call(
        kernel,
        out_shape=out_shape,
        in_specs=in_specs,
        out_specs=out_specs,
        scratch_shapes=scratch,
        compiler_params=pltpu.CompilerParams(vmem_limit_bytes=VMEM_LIMIT),
        cost_estimate=pl.CostEstimate(flops=flops, bytes_accessed=moved, transcendentals=0),
    )


def shaped(shape, dtype):
    return jax.ShapeDtypeStruct(shape, dtype)


def dot_nt(left, right, precision=None):
    return lax.dot_general(
        left, right, (((1,), (1,)), ((), ())), precision=precision, preferred_element_type=F32
    )


def dot_nn(left, right, precision=None):
    return lax.dot_general(
        left, right, (((1,), (0,)), ((), ())), precision=precision, preferred_element_type=F32
    )


def columns(block):
    return slice(block * BS, (block + 1) * BS)


def iota2(shape, axis):
    return lax.broadcasted_iota(jnp.int32, shape, axis)


def list_kernel(part, row_ref, column_ref, live_ref, own_ref, halo_ref, count_ref):
    live = live_ref[0]

    def step(slot, counts):
        n_own, n_halo = counts
        column = column_ref[slot]
        row = row_ref[slot]
        received = jnp.maximum(column - part, 0)
        own_ref[0, n_own] = slot
        own_ref[1, n_own] = jnp.minimum(column, part - 1)
        own_ref[2, n_own] = row
        own_ref[3, n_own] = jnp.minimum(column, part - 1) >> 5
        halo_ref[0, n_halo] = slot
        halo_ref[1, n_halo] = received + (received >> 3)
        halo_ref[2, n_halo] = row
        halo_ref[3, n_halo] = received
        used = slot < live
        n_own = n_own + jnp.where(used & (column < part), 1, 0)
        n_halo = n_halo + jnp.where(used & (column >= part), 1, 0)
        return n_own, n_halo

    n_own, n_halo = lax.fori_loop(0, SLOTS, step, (jnp.int32(0), jnp.int32(0)))
    for ref, count in ((own_ref, n_own), (halo_ref, n_halo)):
        for extra in range(8):
            ref[0, count + extra] = 0
            ref[1, count + extra] = 0
            ref[2, count + extra] = RB
            ref[3, count + extra] = 0
    count_ref[0] = n_own
    count_ref[1] = n_halo


def make_lists(slot_row, slot_column, live_slots, part):
    return call(
        functools.partial(list_kernel, part),
        (shaped((4, LEN), jnp.int32), shaped((4, LEN), jnp.int32), shaped((2,), jnp.int32)),
        [SMEM, SMEM, SMEM],
        (SMEM, SMEM, SMEM),
        moved=20000,
    )(slot_row, slot_column, live_slots)


def split3(value):
    high = value.astype(BF16).astype(F32)
    rest = value - high
    middle = rest.astype(BF16).astype(F32)
    return high, middle, (rest - middle).astype(BF16).astype(F32)


def cast_kernel(field_ref, degree_ref, tiles_ref):
    for block in range(RB):
        tiles_ref[block + 2 * (block // HALF)] = field_ref[:, columns(block)].astype(BF16)
    for half in range(2):
        inverse = 1.0 / degree_ref[half * HALF : (half + 1) * HALF]
        high = inverse.astype(BF16)
        at = half * (HALF + 2) + HALF
        tiles_ref[at] = high
        tiles_ref[at + 1] = (inverse - high.astype(F32)).astype(BF16)


def cast_tiles(field, degree):
    return call(
        cast_kernel, shaped((RB + 4, K, BS), BF16), [VMEM, VMEM], VMEM, moved=400000
    )(field, degree)


def gather_row(tiles, n_row, half):
    up = [(i, (i + 1) % n_row) for i in range(n_row)]
    down = [(i, (i - 1) % n_row) for i in range(n_row)]
    pieces = [(0, tiles)]
    from_below = from_above = tiles
    for step in range(1, n_row // 2):
        from_below = lax.ppermute(from_below, "row", up)
        from_above = lax.ppermute(from_above, "row", down)
        pieces += [(-step, from_below), (step, from_above)]
    far_low = lax.ppermute(from_below[:half], "row", up)
    far_high = lax.ppermute(from_above[half:], "row", down)
    return pieces, far_low, far_high


def halves(offsets, pieces, half, n_row, place):
    parts = []
    for offset, piece in zip(offsets, pieces):
        owner = lax.rem(place + offset + n_row, n_row)
        parts += [(owner, 0, piece, 0), (owner, 1, piece, half)]
    owner = lax.rem(place + n_row // 2, n_row)
    return parts + [(owner, 0, pieces[-2], 0), (owner, 1, pieces[-1], 0)]


def first_select_kernel(offsets, n_row, place_ref, send_ref, *refs):
    pieces, (part_ref, inverse_ref, chosen_ref, rows_ref) = refs[:-4], refs[-4:]
    for owner, half, piece, start in halves(offsets, pieces, HALF + 2, n_row, place_ref[0]):
        at = owner * RB + half * HALF
        part_ref[pl.ds(at, HALF)] = piece[start : start + HALF]
        inverse_ref[pl.ds(pl.multiple_of(at, HALF), HALF), :] = (
            piece[start + HALF].astype(F32) + piece[start + HALF + 1].astype(F32)
        )

    def step(peer, carry):
        for j in range(SEND):
            block = send_ref[peer * SEND + j]
            chosen_ref[peer * EXTRA + j] = part_ref[block]
            rows_ref[j : j + 1, :] = inverse_ref[pl.ds(block, 1), :]
        rows = rows_ref[...]
        high = rows.astype(BF16).astype(F32)
        chosen_ref[peer * EXTRA + SEND] = jnp.concatenate([high, rows - high], axis=0).astype(BF16)
        return carry

    lax.fori_loop(0, chosen_ref.shape[0] // EXTRA, step, 0)


def first_select(gathered, place, send_list, n_row):
    pieces, far_low, far_high = gathered
    part = n_row * RB
    peers = send_list.shape[0] // SEND
    return call(
        functools.partial(first_select_kernel, [offset for offset, _ in pieces], n_row),
        (shaped((part, K, BS), BF16), shaped((part, BS), F32), shaped((peers * EXTRA, K, BS), BF16)),
        [SMEM, SMEM] + [VMEM] * (len(pieces) + 2),
        (VMEM, VMEM, VMEM),
        (pltpu.VMEM((SEND, BS), F32),),
        moved=3000000,
    )(place, send_list, *[piece for _, piece in pieces], far_low, far_high)


def second_select_kernel(offsets, n_row, place_ref, send_ref, pick_ref, *refs):
    pieces, (part_ref, chosen_ref, table_ref) = refs[:-3], refs[-3:]
    lane = iota2((K, BS), 1)
    table = jnp.zeros((K, BS), F32)
    side_sum = jnp.zeros((K, BS), F32)
    for owner, half, piece, start in halves(offsets, pieces, HALF, n_row, place_ref[0]):
        part_ref[pl.ds(owner * RB + half * HALF, HALF)] = piece[start : start + HALF]
        if half == 1:
            side = piece[start + HALF].astype(F32)
            table = jnp.where(lane == owner, side[:, 0:1], table)
            side_sum = side_sum + side
    top = jnp.sum(jnp.where((lane >= 1) & (lane <= 3), side_sum, 0.0), axis=1, keepdims=True)
    bottom = jnp.sum(jnp.where((lane >= 4) & (lane <= 6), side_sum, 0.0), axis=1, keepdims=True)
    for at, value in enumerate(split3(top) + split3(bottom)):
        table = jnp.where(lane == 8 + at, value, table)
    table = table.astype(BF16)
    table_ref[...] = table
    sides = dot_nn(table, pick_ref[...])
    for peer in range(chosen_ref.shape[0] // EXTRA):
        chosen_ref[peer * EXTRA + SEND] = sides[:, columns(peer)].astype(BF16)

    def step(peer, carry):
        for j in range(SEND):
            chosen_ref[peer * EXTRA + j] = part_ref[send_ref[peer * SEND + j]]
        return carry

    lax.fori_loop(0, chosen_ref.shape[0] // EXTRA, step, 0)


def second_select(gathered, place, send_list, pick, n_row):
    pieces, far_low, far_high = gathered
    peers = send_list.shape[0] // SEND
    return call(
        functools.partial(second_select_kernel, [offset for offset, _ in pieces], n_row),
        (shaped((n_row * RB, K, BS), BF16), shaped((peers * EXTRA, K, BS), BF16), shaped((K, BS), BF16)),
        [SMEM, SMEM] + [VMEM] * (len(pieces) + 3),
        (VMEM, VMEM, VMEM),
        moved=3000000,
    )(place, send_list, pick, *[piece for _, piece in pieces], far_low, far_high)


def picks(send_list):
    peers = send_list.shape[0] // SEND
    owner = (send_list >> 5).reshape(peers, SEND)
    lane = jnp.broadcast_to(jnp.arange(BS, dtype=jnp.int32)[None, :], (peers, BS))
    target = jnp.where(lane < 14, lane, -1)
    target = jnp.concatenate([owner, target[:, SEND:]], axis=1).reshape(-1)
    return (jnp.arange(BS, dtype=jnp.int32)[:, None] == target[None, :]).astype(BF16)


def issue(count, list_ref, coupling_ref, held, sems):
    def step(group, carry):
        for j in range(8):
            at = group * 8 + j
            pltpu.make_async_copy(
                coupling_ref.at[list_ref[0, at]], held.at[at], sems.at[group]
            ).start()
        return carry

    lax.fori_loop(0, lax.div(count + 7, 8), step, 0)


def work(count, list_ref, coupling_ref, held, sems, multiply, add):
    def step(group, carry):
        base = group * 8
        pltpu.make_async_copy(
            coupling_ref.at[pl.ds(0, 8)], held.at[pl.ds(base, 8)], sems.at[group]
        ).wait()
        products = [
            multiply(list_ref[1, base + j], list_ref[3, base + j], held[base + j]) for j in range(8)
        ]
        for j in range(8):
            add(base + j, list_ref[2, base + j], list_ref[3, base + j], products[j])
        return carry

    lax.fori_loop(0, lax.div(count + 7, 8), step, 0)


HELD = (pltpu.VMEM((SLOTS, BS, BS), BF16), pltpu.SemaphoreType.DMA((SLOTS // 8,)))
ROWS = shaped((RB + 1, K, BS), F32)
PRODUCTS = shaped((SLOTS, K, BS), F32)


def scale_block(block, inverse):
    return (block.astype(F32) * inverse).astype(BF16)


def first_own_kernel(
    list_ref, count_ref, part_ref, inverse_ref, coupling_ref, acc_ref, scaled_ref, kept_ref, held, sems
):
    issue(count_ref[0], list_ref, coupling_ref, held, sems)
    acc_ref[...] = jnp.zeros_like(acc_ref)
    scaled_ref[...] = jnp.zeros_like(scaled_ref)

    def multiply(tile, side, weights):
        block = part_ref[tile]
        scaled = scale_block(block, inverse_ref[pl.ds(tile, 1), :])
        return dot_nt(jnp.concatenate([block, scaled], axis=0), weights)

    def add(at, row, side, product):
        acc_ref[row] = acc_ref[row] + product[0:K]
        scaled_ref[row] = scaled_ref[row] + product[K:]
        kept_ref[at] = product[K:]

    work(count_ref[0], list_ref, coupling_ref, held, sems, multiply, add)


def first_own(own_list, counts, part_tiles, inverse, coupling):
    return call(
        first_own_kernel,
        (ROWS, ROWS, PRODUCTS),
        [SMEM, SMEM, VMEM, VMEM, HBM],
        (VMEM, VMEM, VMEM),
        HELD,
        flops=2 * SLOTS * K * BS * BS,
        moved=10000000,
    )(own_list, counts, part_tiles, inverse, coupling)


def image_kernel(
    list_ref, count_ref, halo_ref, coupling_ref, own_ref, basis_ref, degree_ref, image_ref, tiles_ref, acc_ref, held,
    sems,
):
    issue(count_ref[1], list_ref, coupling_ref, held, sems)
    acc_ref[...] = own_ref[...]

    def multiply(tile, side, weights):
        return dot_nt(halo_ref[tile], weights)

    def add(at, row, side, product):
        acc_ref[row] = acc_ref[row] + product

    work(count_ref[1], list_ref, coupling_ref, held, sems, multiply, add)
    top = jnp.zeros((K, BS), F32)
    bottom = jnp.zeros((K, BS), F32)
    for block in range(RB):
        at = columns(block)
        basis = basis_ref[:, at]
        image = degree_ref[block : block + 1, :] * basis - acc_ref[block]
        image_ref[:, at] = image
        top = top + basis * image
        bottom = bottom + basis * basis
    top = jnp.sum(top, axis=1, keepdims=True)
    bottom = jnp.sum(bottom, axis=1, keepdims=True)
    usable = bottom > 1e-30
    quotient = jnp.where(usable, top / jnp.where(usable, bottom, 1.0), 0.0).astype(BF16).astype(F32)
    for block in range(RB):
        at = columns(block)
        residual = (image_ref[:, at] - quotient * basis_ref[:, at]) / degree_ref[block : block + 1, :]
        tiles_ref[block] = residual.astype(BF16)
    lane = iota2((K, BS), 1)
    side = jnp.where(lane == 0, quotient, 0.0)
    for at, value in enumerate(split3(top) + split3(bottom)):
        side = jnp.where(lane == 1 + at, value, side)
    tiles_ref[RB] = side.astype(BF16)


def make_image(halo_list, counts, halo_tiles, coupling, own, basis, degree):
    return call(
        image_kernel,
        (shaped(basis.shape, F32), shaped((RB + 1, K, BS), BF16)),
        [SMEM, SMEM, VMEM, HBM, VMEM, VMEM, VMEM],
        (VMEM, VMEM),
        (pltpu.VMEM((RB + 1, K, BS), F32),) + HELD,
        flops=2 * SLOTS * K * BS * BS,
        moved=8000000,
    )(halo_list, counts, halo_tiles, coupling, own, basis, degree)


def second_own_kernel(
    own_list, halo_list, count_ref, part_ref, table_ref, own_kept_ref, own_scaled_ref, halo_ref, coupling_ref,
    acc_ref, scaled_ref, kept_ref, held, sems, halo_held, halo_sems, quotient_ref, inverse_ref,
):
    issue(count_ref[0], own_list, coupling_ref, held, sems)
    issue(count_ref[1], halo_list, coupling_ref, halo_held, halo_sems)
    acc_ref[...] = jnp.zeros_like(acc_ref)
    scaled_ref[...] = own_scaled_ref[...]
    table = table_ref[...].astype(F32)
    lane = iota2((K, BS), 1)
    for owner in range(quotient_ref.shape[0]):
        quotient_ref[owner] = jnp.broadcast_to(table[:, owner : owner + 1], (K, BS))
    for peer in range(halo_ref.shape[0] // EXTRA):
        side = halo_ref[peer * EXTRA + SEND].astype(F32)
        inverse_ref[peer * SEND : (peer + 1) * SEND, :] = side[0:SEND] + side[SEND:]

    def multiply(tile, side, weights):
        return dot_nt(part_ref[tile], weights)

    def add(at, row, side, product):
        acc_ref[row] = acc_ref[row] + (product + quotient_ref[side] * own_kept_ref[at])

    work(count_ref[0], own_list, coupling_ref, held, sems, multiply, add)

    def multiply_halo(tile, side, weights):
        return dot_nt(scale_block(halo_ref[tile], inverse_ref[pl.ds(side, 1), :]), weights)

    def add_halo(at, row, side, product):
        scaled_ref[row] = scaled_ref[row] + product
        kept_ref[at] = product

    work(count_ref[1], halo_list, coupling_ref, halo_held, halo_sems, multiply_halo, add_halo)


def second_own(
    own_list, halo_list, counts, part_tiles, table, own_kept, own_scaled, halo_tiles, coupling, n_row
):
    return call(
        second_own_kernel,
        (ROWS, ROWS, PRODUCTS),
        [SMEM, SMEM, SMEM] + [VMEM] * 5 + [HBM],
        (VMEM, VMEM, VMEM),
        HELD
        + HELD
        + (pltpu.VMEM((n_row, K, BS), F32), pltpu.VMEM((halo_tiles.shape[0] // EXTRA * SEND, BS), F32)),
        flops=4 * SLOTS * K * BS * BS,
        moved=10000000,
    )(own_list, halo_list, counts, part_tiles, table, own_kept, own_scaled, halo_tiles, coupling)


def spread_kernel(taken_ref, given_ref):
    total = taken_ref[0]
    for peer in range(1, taken_ref.shape[0]):
        total = total + taken_ref[peer]
    for peer in range(given_ref.shape[0]):
        given_ref[peer] = total


def add_and_repeat(taken, peers):
    return call(
        spread_kernel, shaped((peers,) + taken.shape[1:], F32), [VMEM], VMEM, moved=400000
    )(taken)


def square(value, wide_ref):
    rows, cols = value.shape
    wide_ref[...] = jnp.zeros_like(wide_ref)
    wide_ref[0:rows, 0:cols] = value
    return wide_ref[...]


def pack_grams(gram_b, gram_a, wide_ref):
    wide_a = square(gram_a, wide_ref)
    both = 0.5 * (wide_a + wide_a.T)
    wide_b = square(gram_b, wide_ref)
    row = iota2((BS, BS), 0)
    lane = iota2((BS, BS), 1)
    packed = jnp.where(row <= lane, wide_b, both)
    diagonal = jnp.sum(jnp.where(row == lane, both, 0.0), axis=1, keepdims=True)
    low, high = packed[0:24], pltpu.roll(packed[24:48], 48, 1)
    at = iota2((24, BS), 1)
    out = jnp.where(at < 48, low, high)
    out = jnp.where(at == 96, diagonal[0:24], out)
    return jnp.where(at == 97, diagonal[24:48], out)


def unpack_grams(packed, wide_ref):
    wide_ref[...] = jnp.zeros_like(wide_ref)
    at = iota2((24, BS), 1)
    wide_ref[0:24] = jnp.where(at < 48, packed, 0.0)
    wide_ref[24:48] = jnp.where(at < 48, pltpu.roll(packed, 80, 1), 0.0)
    wide = wide_ref[...]
    flipped = wide.T
    row = iota2((48, BS), 0)
    lane = iota2((48, BS), 1)
    wide, flipped = wide[0:48], flipped[0:48]
    diagonal = jnp.concatenate([packed[:, 96:97], packed[:, 97:98]], axis=0)
    gram_b = jnp.where(row <= lane, wide, flipped)
    gram_a = jnp.where(row == lane, diagonal, jnp.where(row > lane, wide, flipped))
    return gram_b, gram_a


def gram_kernel(
    list_ref, count_ref, halo_ref, coupling_ref, own_ref, scaled_ref, kept_ref, basis_ref, image_ref, degree_ref,
    previous_ref, previous_image_ref, residual_ref, residual_image_ref, packed_ref, acc_ref, held, sems, side_ref,
    quotient_ref, stacked, stacked_image, wide_ref,
):
    issue(count_ref[1], list_ref, coupling_ref, held, sems)
    acc_ref[...] = own_ref[...]
    peers = halo_ref.shape[0] // EXTRA
    total = jnp.zeros((K, BS), F32)
    for peer in range(peers):
        side = halo_ref[peer * EXTRA + SEND]
        side_ref[peer * K : (peer + 1) * K, :] = side
        total = total + side.astype(F32)
    side = side_ref[...]
    for j in range(SEND):
        spread = (iota2((BS, BS), 0) == j).astype(F32).astype(BF16)
        quotient_ref[j] = dot_nn(side, spread).reshape(peers, K, BS)
    lane = iota2((K, BS), 1)
    top = jnp.sum(jnp.where((lane >= 8) & (lane <= 10), total, 0.0), axis=1, keepdims=True)
    bottom = jnp.sum(jnp.where((lane >= 11) & (lane <= 13), total, 0.0), axis=1, keepdims=True)
    theta = top / bottom

    def multiply(tile, side, weights):
        return dot_nt(halo_ref[tile], weights)

    def add(at, row, side, product):
        acc_ref[row] = acc_ref[row] + (product + quotient_ref[side & 7, side >> 3] * kept_ref[at])

    work(count_ref[1], list_ref, coupling_ref, held, sems, multiply, add)
    stacked[0:16] = basis_ref[...]
    stacked[32:48] = previous_ref[...]
    stacked_image[0:16] = image_ref[...]
    stacked_image[32:48] = previous_image_ref[...]
    for block in range(RB):
        at = columns(block)
        degree = degree_ref[block : block + 1, :]
        residual = (image_ref[:, at] - theta * basis_ref[:, at]) / degree
        residual_ref[:, at] = residual
        stacked[16:32, at] = residual
        value = degree * residual - (acc_ref[block] - theta * scaled_ref[block])
        residual_image_ref[:, at] = value
        stacked_image[16:32, at] = value
    gram_b = dot_nt(stacked[...], stacked[...], HIGHEST)
    gram_a = dot_nt(stacked[...], stacked_image[...], HIGHEST)
    packed = pack_grams(gram_b, gram_a, wide_ref)
    for peer in range(packed_ref.shape[0]):
        packed_ref[peer] = packed


def make_grams(
    halo_list, counts, halo_tiles, coupling, own, scaled, kept, basis, image, degree, previous, previous_image, n_dom
):
    width = basis.shape[1]
    return call(
        gram_kernel,
        (shaped(basis.shape, F32), shaped(basis.shape, F32), shaped((n_dom, 24, BS), F32)),
        [SMEM, SMEM, VMEM, HBM] + [VMEM] * 8,
        (VMEM, VMEM, VMEM),
        (pltpu.VMEM((RB + 1, K, BS), F32),)
        + HELD
        + (
            pltpu.VMEM((n_dom * K, BS), BF16),
            pltpu.VMEM((SEND, n_dom, K, BS), F32),
            pltpu.VMEM((48, width), F32),
            pltpu.VMEM((48, width), F32),
            pltpu.VMEM((BS, BS), F32),
        ),
        flops=2 * SLOTS * K * BS * BS,
        moved=10000000,
    )(halo_list, counts, halo_tiles, coupling, own, scaled, kept, basis, image, degree, previous, previous_image)


def inverse_factor(gram, n):
    row = iota2((n, BS), 0)
    lane = iota2((n, BS), 1)
    work = jnp.where(lane < n, gram, jnp.where(lane == row + n, 1.0, 0.0))
    for j in range(n):
        column = work[:, j : j + 1]
        pivot = work[j : j + 1, :]
        scale = lax.rsqrt(work[j : j + 1, j : j + 1])
        scaled = pivot * scale
        below = jnp.where(row[:, 0:1] > j, column * scale, 0.0)
        work = jnp.where(row == j, scaled, work - below * scaled)
    return pltpu.roll(work, BS - n, 1)


def final_kernel(
    root_rows, taken_ref, basis_ref, residual_ref, previous_ref, image_ref, residual_image_ref, previous_image_ref,
    new_basis_ref, new_image_ref, wide_ref, stacked,
):
    packed = taken_ref[0]
    for peer in range(1, taken_ref.shape[0]):
        packed = packed + taken_ref[peer]
    gram_b, gram_a = unpack_grams(packed, wide_ref)
    inverse = inverse_factor(gram_b, 48)[:, 0:48]
    symmetric = gram_a[:, 0:48]
    reduced = dot_nt(dot_nn(inverse, symmetric, HIGHEST), inverse, HIGHEST)
    wide = square(reduced, wide_ref)
    reduced = 0.5 * (wide + wide.T)[0:48, 0:48]
    spread = jnp.max(jnp.sum(jnp.abs(reduced), axis=1, keepdims=True), axis=0, keepdims=True)
    row = iota2((48, 48), 0)
    lane = iota2((48, 48), 1)
    filter_mat = (jnp.where(row == lane, spread, 0.0) - reduced) / (2.0 * spread)
    subspace = filter_mat[:, 0:16]
    for repeat in range(3):
        subspace = dot_nn(filter_mat, subspace, HIGHEST)
    wide_ref[...] = jnp.zeros_like(wide_ref)
    wide_ref[0:48, 0:16] = subspace
    turned = wide_ref[...].T[0:16, 0:48]
    inner = dot_nt(turned, turned, HIGHEST)
    wide_ref[...] = jnp.zeros_like(wide_ref)
    wide_ref[0:16, 0:16] = inner
    sub_inverse = inverse_factor(wide_ref[0:16, :], 16)[:, 0:16]
    coeff = dot_nn(dot_nn(sub_inverse, turned, HIGHEST), inverse, HIGHEST) * root_rows
    stacked[0:16] = basis_ref[...]
    stacked[16:32] = residual_ref[...]
    stacked[32:48] = previous_ref[...]
    new_basis_ref[...] = dot_nn(coeff, stacked[...], HIGHEST)
    stacked[0:16] = image_ref[...]
    stacked[16:32] = residual_image_ref[...]
    stacked[32:48] = previous_image_ref[...]
    new_image_ref[...] = dot_nn(coeff, stacked[...], HIGHEST)


def finish(root_rows, packed, basis, residual, previous, image, residual_image, previous_image):
    return call(
        functools.partial(final_kernel, root_rows),
        (shaped(basis.shape, F32), shaped(basis.shape, F32)),
        [VMEM] * 7,
        (VMEM, VMEM),
        (pltpu.VMEM((BS, BS), F32), pltpu.VMEM((48, basis.shape[1]), F32)),
        flops=1000000,
        moved=3000000,
    )(packed, basis, residual, previous, image, residual_image, previous_image)


def to_all(value, axis):
    return lax.all_to_all(value, axis, split_axis=0, concat_axis=0, tiled=True)


def body(
    n_dom, n_row,
    basis, previous, previous_image, degree, coupling, slot_row, slot_column, send_lists, live_slots,
):
    part = n_row * RB
    place = lax.axis_index("row").astype(jnp.int32).reshape(1)
    send_list = send_lists.reshape(n_dom * SEND)
    degree = degree.reshape(RB, BS)
    own_list, halo_list, counts = make_lists(slot_row, slot_column, live_slots, part)

    gathered = gather_row(cast_tiles(basis, degree), n_row, HALF + 2)
    part_tiles, inverse, chosen = first_select(gathered, place, send_list, n_row)
    halo_tiles = to_all(chosen, "dom")
    own, own_scaled, own_kept = first_own(own_list, counts, part_tiles, inverse, coupling)
    image, tiles = make_image(halo_list, counts, halo_tiles, coupling, own, basis, degree)

    gathered = gather_row(tiles, n_row, HALF)
    part_tiles, chosen, table = second_select(gathered, place, send_list, picks(send_list), n_row)
    far_tiles = to_all(chosen, "dom")
    own, scaled, kept = second_own(
        own_list, halo_list, counts, part_tiles, table, own_kept, own_scaled, halo_tiles, coupling, n_row
    )
    residual, residual_image, packed = make_grams(
        halo_list, counts, far_tiles, coupling, own, scaled, kept, basis, image, degree, previous, previous_image, n_dom
    )
    packed = to_all(add_and_repeat(to_all(packed, "dom"), n_row), "row")
    root_rows = math.sqrt(basis.shape[1] * n_dom * n_row)
    return finish(root_rows, packed, basis, residual, previous, image, residual_image, previous_image)


def solution(mesh):
    split = P(None, ("dom", "row"))
    flat = P(("dom", "row"))
    return jax.shard_map(
        functools.partial(body, mesh.shape["dom"], mesh.shape["row"]),
        mesh=mesh,
        in_specs=(
            split, split, split, flat, P(("dom", "row"), None, None), flat, flat, P("dom", None, None), flat,
        ),
        out_specs=(split, split),
        check_vma=False,
    )
```

```python
import functools
import math

import jax
import jax.numpy as jnp
from jax import lax
from jax.experimental import pallas as pl
from jax.experimental.pallas import tpu as pltpu
from jax.sharding import PartitionSpec as P

K = 16
BS = 128
RB = 32
SLOTS = 256
SEND = 8
HALF = RB // 2
EXTRA = SEND + 1
GROUP = 32
LEN = SLOTS + GROUP
F32 = jnp.float32
BF16 = jnp.bfloat16
HIGHEST = lax.Precision.HIGHEST
MARGIN = 6 * 1024 * 1024
SMEM = pl.BlockSpec(memory_space=pltpu.SMEM)
HBM = pl.BlockSpec(memory_space=pltpu.HBM)
VMEM = pl.BlockSpec(memory_space=pltpu.VMEM)


def size(array):
    return math.prod(array.shape) * jnp.dtype(array.dtype).itemsize


def call(kernel, out_shape, in_specs, out_specs, scratch=(), flops=0, moved=0):
    def run(*args):
        arrays = list(args) + jax.tree.leaves(out_shape) + [held for held in scratch if jnp.issubdtype(held.dtype, jnp.floating)]
        return pl.pallas_call(
            kernel,
            out_shape=out_shape,
            in_specs=in_specs,
            out_specs=out_specs,
            scratch_shapes=scratch,
            compiler_params=pltpu.CompilerParams(vmem_limit_bytes=MARGIN + sum(map(size, arrays))),
            cost_estimate=pl.CostEstimate(flops=flops, bytes_accessed=moved, transcendentals=0),
        )(*args)

    return run


def shaped(shape, dtype):
    return jax.ShapeDtypeStruct(shape, dtype)


def dot_nt(left, right, precision=None):
    return lax.dot_general(
        left, right, (((1,), (1,)), ((), ())), precision=precision, preferred_element_type=F32
    )


def dot_nn(left, right, precision=None):
    return lax.dot_general(
        left, right, (((1,), (0,)), ((), ())), precision=precision, preferred_element_type=F32
    )


def columns(block):
    return slice(block * BS, (block + 1) * BS)


def iota2(shape, axis):
    return lax.broadcasted_iota(jnp.int32, shape, axis)


def list_kernel(part, row_ref, column_ref, live_ref, own_ref, halo_ref, count_ref):
    live = live_ref[0]

    def step(slot, counts):
        n_own, n_halo = counts
        column = column_ref[slot]
        row = row_ref[slot]
        received = jnp.maximum(column - part, 0)
        own_ref[0, n_own] = slot
        own_ref[1, n_own] = jnp.minimum(column, part - 1)
        own_ref[2, n_own] = row
        own_ref[3, n_own] = jnp.minimum(column, part - 1) >> 5
        halo_ref[0, n_halo] = slot
        halo_ref[1, n_halo] = received + (received >> 3)
        halo_ref[2, n_halo] = row
        halo_ref[3, n_halo] = received
        used = slot < live
        n_own = n_own + jnp.where(used & (column < part), 1, 0)
        n_halo = n_halo + jnp.where(used & (column >= part), 1, 0)
        return n_own, n_halo

    n_own, n_halo = lax.fori_loop(0, SLOTS, step, (jnp.int32(0), jnp.int32(0)))
    for ref, count in ((own_ref, n_own), (halo_ref, n_halo)):
        for extra in range(GROUP):
            ref[0, count + extra] = 0
            ref[1, count + extra] = 0
            ref[2, count + extra] = RB
            ref[3, count + extra] = 0
    count_ref[0] = n_own
    count_ref[1] = n_halo


def make_lists(slot_row, slot_column, live_slots, part):
    return call(
        functools.partial(list_kernel, part),
        (shaped((4, LEN), jnp.int32), shaped((4, LEN), jnp.int32), shaped((2,), jnp.int32)),
        [SMEM, SMEM, SMEM],
        (SMEM, SMEM, SMEM),
        moved=20000,
    )(slot_row, slot_column, live_slots)


def split3(value):
    high = value.astype(BF16).astype(F32)
    rest = value - high
    middle = rest.astype(BF16).astype(F32)
    return high, middle, (rest - middle).astype(BF16).astype(F32)


def cast_kernel(field_hbm, degree_hbm, tiles_ref, field_ref, degree_ref, sems):
    copies = [
        pltpu.make_async_copy(field_hbm, field_ref, sems.at[0]),
        pltpu.make_async_copy(degree_hbm, degree_ref, sems.at[1]),
    ]
    for copy in copies:
        copy.start()
    for copy in copies:
        copy.wait()
    for block in range(RB):
        tiles_ref[block + 2 * (block // HALF)] = field_ref[:, columns(block)].astype(BF16)
    for half in range(2):
        inverse = 1.0 / degree_ref[half * HALF : (half + 1) * HALF]
        high = inverse.astype(BF16)
        at = half * (HALF + 2) + HALF
        tiles_ref[at] = high
        tiles_ref[at + 1] = (inverse - high.astype(F32)).astype(BF16)


def cast_tiles(field, degree):
    return call(
        cast_kernel,
        shaped((RB + 4, K, BS), BF16),
        [HBM, HBM],
        VMEM,
        (pltpu.VMEM(field.shape, F32), pltpu.VMEM(degree.shape, F32), pltpu.SemaphoreType.DMA((2,))),
        moved=400000,
    )(field, degree)


def gather_row(tiles, n_row, half):
    up = [(i, (i + 1) % n_row) for i in range(n_row)]
    down = [(i, (i - 1) % n_row) for i in range(n_row)]
    pieces = [(0, tiles)]
    from_below = from_above = tiles
    for step in range(1, n_row // 2):
        from_below = lax.ppermute(from_below, "row", up)
        from_above = lax.ppermute(from_above, "row", down)
        pieces += [(-step, from_below), (step, from_above)]
    far_low = lax.ppermute(from_below[:half], "row", up)
    far_high = lax.ppermute(from_above[half:], "row", down)
    return pieces, far_low, far_high


def halves(offsets, pieces, half, n_row, place):
    parts = []
    for offset, piece in zip(offsets, pieces):
        owner = lax.rem(place + offset + n_row, n_row)
        parts += [(owner, 0, piece, 0), (owner, 1, piece, half)]
    owner = lax.rem(place + n_row // 2, n_row)
    return parts + [(owner, 0, pieces[-2], 0), (owner, 1, pieces[-1], 0)]


def fill_and_send(fill, chosen_ref, chosen_hbm, sems):
    peers = chosen_ref.shape[0] // EXTRA
    quarter = max(1, peers // 4)
    copies = []
    for at in range(peers // quarter):

        def step(peer, carry):
            fill(peer)
            return carry

        lax.fori_loop(at * quarter, (at + 1) * quarter, step, 0)
        span = pl.ds(at * quarter * EXTRA, quarter * EXTRA)
        copies.append(pltpu.make_async_copy(chosen_ref.at[span], chosen_hbm.at[span], sems.at[at]))
        copies[-1].start()
    for copy in copies:
        copy.wait()


def first_select_kernel(offsets, n_row, place_ref, send_ref, *refs):
    pieces, (part_ref, inverse_ref, chosen_hbm, rows_ref, chosen_ref, sems) = refs[:-6], refs[-6:]
    for owner, half, piece, start in halves(offsets, pieces, HALF + 2, n_row, place_ref[0]):
        at = owner * RB + half * HALF
        part_ref[pl.ds(at, HALF)] = piece[start : start + HALF]
        inverse_ref[pl.ds(pl.multiple_of(at, HALF), HALF), :] = (
            piece[start + HALF].astype(F32) + piece[start + HALF + 1].astype(F32)
        )

    def fill(peer):
        for j in range(SEND):
            block = send_ref[peer * SEND + j]
            chosen_ref[peer * EXTRA + j] = part_ref[block]
            rows_ref[j : j + 1, :] = inverse_ref[pl.ds(block, 1), :]
        rows = rows_ref[...]
        high = rows.astype(BF16).astype(F32)
        chosen_ref[peer * EXTRA + SEND] = jnp.concatenate([high, rows - high], axis=0).astype(BF16)

    fill_and_send(fill, chosen_ref, chosen_hbm, sems)


def first_select(gathered, place, send_list, n_row):
    pieces, far_low, far_high = gathered
    part = n_row * RB
    peers = send_list.shape[0] // SEND
    return call(
        functools.partial(first_select_kernel, [offset for offset, _ in pieces], n_row),
        (shaped((part, K, BS), BF16), shaped((part, BS), F32), shaped((peers * EXTRA, K, BS), BF16)),
        [SMEM, SMEM] + [VMEM] * (len(pieces) + 2),
        (VMEM, VMEM, HBM),
        (pltpu.VMEM((SEND, BS), F32), pltpu.VMEM((peers * EXTRA, K, BS), BF16), pltpu.SemaphoreType.DMA((4,))),
        moved=3000000,
    )(place, send_list, *[piece for _, piece in pieces], far_low, far_high)


def second_select_kernel(offsets, n_row, place_ref, send_ref, pick_ref, *refs):
    pieces, (part_ref, chosen_hbm, table_ref, chosen_ref, sems) = refs[:-5], refs[-5:]
    lane = iota2((K, BS), 1)
    table = jnp.zeros((K, BS), F32)
    side_sum = jnp.zeros((K, BS), F32)
    for owner, half, piece, start in halves(offsets, pieces, HALF, n_row, place_ref[0]):
        part_ref[pl.ds(owner * RB + half * HALF, HALF)] = piece[start : start + HALF]
        if half == 1:
            side = piece[start + HALF].astype(F32)
            table = jnp.where(lane == owner, side[:, 0:1], table)
            side_sum = side_sum + side
    top = jnp.sum(jnp.where((lane >= 1) & (lane <= 3), side_sum, 0.0), axis=1, keepdims=True)
    bottom = jnp.sum(jnp.where((lane >= 4) & (lane <= 6), side_sum, 0.0), axis=1, keepdims=True)
    for at, value in enumerate(split3(top) + split3(bottom)):
        table = jnp.where(lane == 8 + at, value, table)
    table = table.astype(BF16)
    table_ref[...] = table
    sides = dot_nn(table, pick_ref[...])
    for peer in range(chosen_ref.shape[0] // EXTRA):
        chosen_ref[peer * EXTRA + SEND] = sides[:, columns(peer)].astype(BF16)

    def fill(peer):
        for j in range(SEND):
            chosen_ref[peer * EXTRA + j] = part_ref[send_ref[peer * SEND + j]]

    fill_and_send(fill, chosen_ref, chosen_hbm, sems)


def second_select(gathered, place, send_list, pick, n_row):
    pieces, far_low, far_high = gathered
    peers = send_list.shape[0] // SEND
    return call(
        functools.partial(second_select_kernel, [offset for offset, _ in pieces], n_row),
        (shaped((n_row * RB, K, BS), BF16), shaped((peers * EXTRA, K, BS), BF16), shaped((K, BS), BF16)),
        [SMEM, SMEM] + [VMEM] * (len(pieces) + 3),
        (VMEM, HBM, VMEM),
        (pltpu.VMEM((peers * EXTRA, K, BS), BF16), pltpu.SemaphoreType.DMA((4,))),
        moved=3000000,
    )(place, send_list, pick, *[piece for _, piece in pieces], far_low, far_high)


def picks(send_list):
    peers = send_list.shape[0] // SEND
    owner = (send_list >> 5).reshape(peers, SEND)
    lane = jnp.broadcast_to(jnp.arange(BS, dtype=jnp.int32)[None, :], (peers, BS))
    target = jnp.where(lane < 14, lane, -1)
    target = jnp.concatenate([owner, target[:, SEND:]], axis=1).reshape(-1)
    return (jnp.arange(BS, dtype=jnp.int32)[:, None] == target[None, :]).astype(BF16)


def work(count, list_ref, coupling_ref, multiply, add):
    def step(group, carry):
        base = group * GROUP
        products = [
            multiply(list_ref[1, base + j], list_ref[3, base + j], coupling_ref[list_ref[0, base + j]])
            for j in range(GROUP)
        ]
        for j in range(GROUP):
            add(base + j, list_ref[2, base + j], list_ref[3, base + j], products[j])
        return carry

    lax.fori_loop(0, lax.div(count + GROUP - 1, GROUP), step, 0)


ROWS = shaped((RB + 1, K, BS), F32)
PRODUCTS = shaped((SLOTS, K, BS), F32)


def scale_block(block, inverse):
    return (block.astype(F32) * inverse).astype(BF16)


def first_own_kernel(
    list_ref, count_ref, part_ref, inverse_ref, coupling_ref, acc_ref, scaled_ref, kept_ref
):
    acc_ref[...] = jnp.zeros_like(acc_ref)
    scaled_ref[...] = jnp.zeros_like(scaled_ref)

    def multiply(tile, side, weights):
        block = part_ref[tile]
        scaled = scale_block(block, inverse_ref[pl.ds(tile, 1), :])
        return dot_nt(jnp.concatenate([block, scaled], axis=0), weights)

    def add(at, row, side, product):
        acc_ref[row] = acc_ref[row] + product[0:K]
        scaled_ref[row] = scaled_ref[row] + product[K:]
        kept_ref[at] = product[K:]

    work(count_ref[0], list_ref, coupling_ref, multiply, add)


def first_own(own_list, counts, part_tiles, inverse, coupling):
    return call(
        first_own_kernel,
        (ROWS, ROWS, PRODUCTS),
        [SMEM, SMEM, VMEM, VMEM, VMEM],
        (VMEM, VMEM, VMEM),
        flops=2 * SLOTS * K * BS * BS,
        moved=10000000,
    )(own_list, counts, part_tiles, inverse, coupling)


def image_kernel(
    list_ref, count_ref, halo_ref, coupling_ref, own_ref, basis_ref, degree_ref, image_ref, tiles_ref, acc_ref,
):
    acc_ref[...] = own_ref[...]

    def multiply(tile, side, weights):
        return dot_nt(halo_ref[tile], weights)

    def add(at, row, side, product):
        acc_ref[row] = acc_ref[row] + product

    work(count_ref[1], list_ref, coupling_ref, multiply, add)
    top = jnp.zeros((K, BS), F32)
    bottom = jnp.zeros((K, BS), F32)
    for block in range(RB):
        at = columns(block)
        basis = basis_ref[:, at]
        image = degree_ref[block : block + 1, :] * basis - acc_ref[block]
        image_ref[:, at] = image
        top = top + basis * image
        bottom = bottom + basis * basis
    top = jnp.sum(top, axis=1, keepdims=True)
    bottom = jnp.sum(bottom, axis=1, keepdims=True)
    usable = bottom > 1e-30
    quotient = jnp.where(usable, top / jnp.where(usable, bottom, 1.0), 0.0).astype(BF16).astype(F32)
    for block in range(RB):
        at = columns(block)
        residual = (image_ref[:, at] - quotient * basis_ref[:, at]) / degree_ref[block : block + 1, :]
        tiles_ref[block] = residual.astype(BF16)
    lane = iota2((K, BS), 1)
    side = jnp.where(lane == 0, quotient, 0.0)
    for at, value in enumerate(split3(top) + split3(bottom)):
        side = jnp.where(lane == 1 + at, value, side)
    tiles_ref[RB] = side.astype(BF16)


def make_image(halo_list, counts, halo_tiles, coupling, own, basis, degree):
    return call(
        image_kernel,
        (shaped(basis.shape, F32), shaped((RB + 1, K, BS), BF16)),
        [SMEM, SMEM] + [VMEM] * 5,
        (VMEM, VMEM),
        (pltpu.VMEM((RB + 1, K, BS), F32),),
        flops=2 * SLOTS * K * BS * BS,
        moved=8000000,
    )(halo_list, counts, halo_tiles, coupling, own, basis, degree)


def second_own_kernel(
    own_list, halo_list, count_ref, part_ref, table_ref, own_kept_ref, own_scaled_ref, halo_ref, coupling_ref,
    acc_ref, scaled_ref, kept_ref, quotient_ref, inverse_ref,
):
    acc_ref[...] = jnp.zeros_like(acc_ref)
    scaled_ref[...] = own_scaled_ref[...]
    table = table_ref[...].astype(F32)
    lane = iota2((K, BS), 1)
    for owner in range(quotient_ref.shape[0]):
        quotient_ref[owner] = jnp.broadcast_to(table[:, owner : owner + 1], (K, BS))
    for peer in range(halo_ref.shape[0] // EXTRA):
        side = halo_ref[peer * EXTRA + SEND].astype(F32)
        inverse_ref[peer * SEND : (peer + 1) * SEND, :] = side[0:SEND] + side[SEND:]

    def multiply(tile, side, weights):
        return dot_nt(part_ref[tile], weights)

    def add(at, row, side, product):
        acc_ref[row] = acc_ref[row] + (product + quotient_ref[side] * own_kept_ref[at])

    work(count_ref[0], own_list, coupling_ref, multiply, add)

    def multiply_halo(tile, side, weights):
        return dot_nt(scale_block(halo_ref[tile], inverse_ref[pl.ds(side, 1), :]), weights)

    def add_halo(at, row, side, product):
        scaled_ref[row] = scaled_ref[row] + product
        kept_ref[at] = product

    work(count_ref[1], halo_list, coupling_ref, multiply_halo, add_halo)


def second_own(
    own_list, halo_list, counts, part_tiles, table, own_kept, own_scaled, halo_tiles, coupling, n_row
):
    return call(
        second_own_kernel,
        (ROWS, ROWS, PRODUCTS),
        [SMEM, SMEM, SMEM] + [VMEM] * 6,
        (VMEM, VMEM, VMEM),
        (pltpu.VMEM((n_row, K, BS), F32), pltpu.VMEM((halo_tiles.shape[0] // EXTRA * SEND, BS), F32)),
        flops=4 * SLOTS * K * BS * BS,
        moved=10000000,
    )(own_list, halo_list, counts, part_tiles, table, own_kept, own_scaled, halo_tiles, coupling)


def spread_kernel(taken_ref, given_ref):
    total = taken_ref[0]
    for peer in range(1, taken_ref.shape[0]):
        total = total + taken_ref[peer]
    for peer in range(given_ref.shape[0]):
        given_ref[peer] = total


def add_and_repeat(taken, peers):
    return call(
        spread_kernel, shaped((peers,) + taken.shape[1:], F32), [VMEM], VMEM, moved=400000
    )(taken)


def square(value, wide_ref):
    rows, cols = value.shape
    wide_ref[...] = jnp.zeros_like(wide_ref)
    wide_ref[0:rows, 0:cols] = value
    return wide_ref[...]


def pack_grams(gram_b, gram_a, wide_ref):
    wide_a = square(gram_a, wide_ref)
    both = 0.5 * (wide_a + wide_a.T)
    wide_b = square(gram_b, wide_ref)
    row = iota2((BS, BS), 0)
    lane = iota2((BS, BS), 1)
    packed = jnp.where(row <= lane, wide_b, both)
    diagonal = jnp.sum(jnp.where(row == lane, both, 0.0), axis=1, keepdims=True)
    low, high = packed[0:24], pltpu.roll(packed[24:48], 48, 1)
    at = iota2((24, BS), 1)
    out = jnp.where(at < 48, low, high)
    out = jnp.where(at == 96, diagonal[0:24], out)
    return jnp.where(at == 97, diagonal[24:48], out)


def unpack_grams(packed, wide_ref):
    wide_ref[...] = jnp.zeros_like(wide_ref)
    at = iota2((24, BS), 1)
    wide_ref[0:24] = jnp.where(at < 48, packed, 0.0)
    wide_ref[24:48] = jnp.where(at < 48, pltpu.roll(packed, 80, 1), 0.0)
    wide = wide_ref[...]
    flipped = wide.T
    row = iota2((48, BS), 0)
    lane = iota2((48, BS), 1)
    wide, flipped = wide[0:48], flipped[0:48]
    diagonal = jnp.concatenate([packed[:, 96:97], packed[:, 97:98]], axis=0)
    gram_b = jnp.where(row <= lane, wide, flipped)
    gram_a = jnp.where(row == lane, diagonal, jnp.where(row > lane, wide, flipped))
    return gram_b, gram_a


def gram_kernel(
    list_ref, count_ref, halo_ref, coupling_ref, own_ref, scaled_ref, kept_ref, basis_ref, image_ref, degree_ref,
    previous_ref, previous_image_ref, residual_ref, residual_image_ref, packed_ref, acc_ref, side_ref,
    quotient_ref, stacked, stacked_image, wide_ref,
):
    acc_ref[...] = own_ref[...]
    peers = halo_ref.shape[0] // EXTRA
    total = jnp.zeros((K, BS), F32)
    for peer in range(peers):
        side = halo_ref[peer * EXTRA + SEND]
        side_ref[peer * K : (peer + 1) * K, :] = side
        total = total + side.astype(F32)
    side = side_ref[...]
    for j in range(SEND):
        spread = (iota2((BS, BS), 0) == j).astype(F32).astype(BF16)
        quotient_ref[j] = dot_nn(side, spread).reshape(peers, K, BS)
    lane = iota2((K, BS), 1)
    top = jnp.sum(jnp.where((lane >= 8) & (lane <= 10), total, 0.0), axis=1, keepdims=True)
    bottom = jnp.sum(jnp.where((lane >= 11) & (lane <= 13), total, 0.0), axis=1, keepdims=True)
    theta = top / bottom

    def multiply(tile, side, weights):
        return dot_nt(halo_ref[tile], weights)

    def add(at, row, side, product):
        acc_ref[row] = acc_ref[row] + (product + quotient_ref[side & 7, side >> 3] * kept_ref[at])

    work(count_ref[1], list_ref, coupling_ref, multiply, add)
    stacked[0:16] = basis_ref[...]
    stacked[32:48] = previous_ref[...]
    stacked_image[0:16] = image_ref[...]
    stacked_image[32:48] = previous_image_ref[...]
    for block in range(RB):
        at = columns(block)
        degree = degree_ref[block : block + 1, :]
        residual = (image_ref[:, at] - theta * basis_ref[:, at]) / degree
        residual_ref[:, at] = residual
        stacked[16:32, at] = residual
        value = degree * residual - (acc_ref[block] - theta * scaled_ref[block])
        residual_image_ref[:, at] = value
        stacked_image[16:32, at] = value
    gram_b = dot_nt(stacked[...], stacked[...], HIGHEST)
    gram_a = dot_nt(stacked[...], stacked_image[...], HIGHEST)
    packed = pack_grams(gram_b, gram_a, wide_ref)
    for peer in range(packed_ref.shape[0]):
        packed_ref[peer] = packed


def make_grams(
    halo_list, counts, halo_tiles, coupling, own, scaled, kept, basis, image, degree, previous, previous_image, n_dom
):
    width = basis.shape[1]
    return call(
        gram_kernel,
        (shaped(basis.shape, F32), shaped(basis.shape, F32), shaped((n_dom, 24, BS), F32)),
        [SMEM, SMEM] + [VMEM] * 10,
        (VMEM, VMEM, VMEM),
        (
            pltpu.VMEM((RB + 1, K, BS), F32),
            pltpu.VMEM((n_dom * K, BS), BF16),
            pltpu.VMEM((SEND, n_dom, K, BS), F32),
            pltpu.VMEM((48, width), F32),
            pltpu.VMEM((48, width), F32),
            pltpu.VMEM((BS, BS), F32),
        ),
        flops=2 * SLOTS * K * BS * BS,
        moved=10000000,
    )(halo_list, counts, halo_tiles, coupling, own, scaled, kept, basis, image, degree, previous, previous_image)


def inverse_factor(gram, n):
    row = iota2((n, BS), 0)
    lane = iota2((n, BS), 1)
    work = jnp.where(lane < n, gram, jnp.where(lane == row + n, 1.0, 0.0))
    for first in range(0, n, 8):
        left = [jnp.broadcast_to(work[:, first + j : first + j + 1], (n, BS)) for j in range(8)]
        rows = [work[first + j : first + j + 1, :] for j in range(8)]
        for j in range(8):
            scale = lax.rsqrt(left[j][first + j : first + j + 1, :])
            rows[j] = rows[j] * scale
            left[j] = jnp.where(row > first + j, left[j] * scale, 0.0)
            for k in range(j + 1, 8):
                entry = left[j][first + k : first + k + 1, :]
                rows[k] = rows[k] - entry * rows[j]
                left[k] = left[k] - left[j] * entry
        for j in range(8):
            work = jnp.where(row == first + j, rows[j], work - left[j] * rows[j])
    return pltpu.roll(work, BS - n, 1)


def final_kernel(
    root_rows, taken_ref, basis_ref, residual_ref, previous_ref, image_ref, residual_image_ref, previous_image_ref,
    new_basis_ref, new_image_ref, wide_ref, stacked,
):
    packed = taken_ref[0]
    for peer in range(1, taken_ref.shape[0]):
        packed = packed + taken_ref[peer]
    gram_b, gram_a = unpack_grams(packed, wide_ref)
    inverse = inverse_factor(gram_b, 48)[:, 0:48]
    symmetric = gram_a[:, 0:48]
    reduced = dot_nt(dot_nn(inverse, symmetric, HIGHEST), inverse, HIGHEST)
    wide = square(reduced, wide_ref)
    reduced = 0.5 * (wide + wide.T)[0:48, 0:48]
    spread = jnp.max(jnp.sum(jnp.abs(reduced), axis=1, keepdims=True), axis=0, keepdims=True)
    row = iota2((48, 48), 0)
    lane = iota2((48, 48), 1)
    filter_mat = (jnp.where(row == lane, spread, 0.0) - reduced) / (2.0 * spread)
    turned = filter_mat[0:16, :]
    for repeat in range(3):
        turned = dot_nn(turned, filter_mat, HIGHEST)
    inner = dot_nt(turned, turned, HIGHEST)
    wide_ref[...] = jnp.zeros_like(wide_ref)
    wide_ref[0:16, 0:16] = inner
    sub_inverse = inverse_factor(wide_ref[0:16, :], 16)[:, 0:16]
    coeff = dot_nn(dot_nn(sub_inverse, turned, HIGHEST), inverse, HIGHEST) * root_rows
    stacked[0:16] = basis_ref[...]
    stacked[16:32] = residual_ref[...]
    stacked[32:48] = previous_ref[...]
    new_basis_ref[...] = dot_nn(coeff, stacked[...], HIGHEST)
    stacked[0:16] = image_ref[...]
    stacked[16:32] = residual_image_ref[...]
    stacked[32:48] = previous_image_ref[...]
    new_image_ref[...] = dot_nn(coeff, stacked[...], HIGHEST)


def finish(root_rows, packed, basis, residual, previous, image, residual_image, previous_image):
    return call(
        functools.partial(final_kernel, root_rows),
        (shaped(basis.shape, F32), shaped(basis.shape, F32)),
        [VMEM] * 7,
        (VMEM, VMEM),
        (pltpu.VMEM((BS, BS), F32), pltpu.VMEM((48, basis.shape[1]), F32)),
        flops=1000000,
        moved=3000000,
    )(packed, basis, residual, previous, image, residual_image, previous_image)


def to_all(value, axis):
    return lax.all_to_all(value, axis, split_axis=0, concat_axis=0, tiled=True)


def body(
    n_dom, n_row,
    basis, previous, previous_image, degree, coupling, slot_row, slot_column, send_lists, live_slots,
):
    part = n_row * RB
    place = lax.axis_index("row").astype(jnp.int32).reshape(1)
    send_list = send_lists.reshape(n_dom * SEND)
    degree = degree.reshape(RB, BS)
    own_list, halo_list, counts = make_lists(slot_row, slot_column, live_slots, part)

    gathered = gather_row(cast_tiles(basis, degree), n_row, HALF + 2)
    part_tiles, inverse, chosen = first_select(gathered, place, send_list, n_row)
    halo_tiles = to_all(chosen, "dom")
    own, own_scaled, own_kept = first_own(own_list, counts, part_tiles, inverse, coupling)
    image, tiles = make_image(halo_list, counts, halo_tiles, coupling, own, basis, degree)

    gathered = gather_row(tiles, n_row, HALF)
    part_tiles, chosen, table = second_select(gathered, place, send_list, picks(send_list), n_row)
    far_tiles = to_all(chosen, "dom")
    own, scaled, kept = second_own(
        own_list, halo_list, counts, part_tiles, table, own_kept, own_scaled, halo_tiles, coupling, n_row
    )
    residual, residual_image, packed = make_grams(
        halo_list, counts, far_tiles, coupling, own, scaled, kept, basis, image, degree, previous, previous_image, n_dom
    )
    packed = to_all(add_and_repeat(to_all(packed, "dom"), n_row), "row")
    root_rows = math.sqrt(basis.shape[1] * n_dom * n_row)
    return finish(root_rows, packed, basis, residual, previous, image, residual_image, previous_image)


def solution(mesh):
    split = P(None, ("dom", "row"))
    flat = P(("dom", "row"))
    return jax.shard_map(
        functools.partial(body, mesh.shape["dom"], mesh.shape["row"]),
        mesh=mesh,
        in_specs=(
            split, split, split, flat, P(("dom", "row"), None, None), flat, flat, P("dom", None, None), flat,
        ),
        out_specs=(split, split),
        check_vma=False,
    )
```

```python
import functools
import math

import jax
import jax.numpy as jnp
from jax import lax
from jax.experimental import pallas as pl
from jax.experimental.pallas import tpu as pltpu
from jax.sharding import PartitionSpec as P

K = 16
BS = 128
RB = 32
SLOTS = 256
SEND = 8
HALF = RB // 2
EXTRA = SEND + 1
CHUNK = 32
GROUP = 32
LEN = SLOTS + GROUP
F32 = jnp.float32
BF16 = jnp.bfloat16
HIGHEST = lax.Precision.HIGHEST
MARGIN = 6 * 1024 * 1024
SMEM = pl.BlockSpec(memory_space=pltpu.SMEM)
HBM = pl.BlockSpec(memory_space=pl.ANY)
VMEM = pl.BlockSpec(memory_space=pltpu.VMEM)


def size(array):
    return math.prod(array.shape) * jnp.dtype(array.dtype).itemsize


def call(kernel, out_shape, in_specs, out_specs, scratch=(), flops=0, moved=0):
    def run(*args):
        arrays = list(args) + jax.tree.leaves(out_shape) + [held for held in scratch if jnp.issubdtype(held.dtype, jnp.floating)]
        return pl.pallas_call(
            kernel,
            out_shape=out_shape,
            in_specs=in_specs,
            out_specs=out_specs,
            scratch_shapes=scratch,
            compiler_params=pltpu.CompilerParams(vmem_limit_bytes=MARGIN + sum(map(size, arrays))),
            cost_estimate=pl.CostEstimate(flops=flops, bytes_accessed=moved, transcendentals=0),
        )(*args)

    return run


def shaped(shape, dtype):
    return jax.ShapeDtypeStruct(shape, dtype)


def dot_nt(left, right, precision=None):
    return lax.dot_general(
        left, right, (((1,), (1,)), ((), ())), precision=precision, preferred_element_type=F32
    )


def dot_nn(left, right, precision=None):
    return lax.dot_general(
        left, right, (((1,), (0,)), ((), ())), precision=precision, preferred_element_type=F32
    )


def columns(block):
    return slice(block * BS, (block + 1) * BS)


def iota2(shape, axis):
    return lax.broadcasted_iota(jnp.int32, shape, axis)


def list_kernel(part, row_ref, column_ref, live_ref, own_ref, halo_ref, count_ref):
    live = live_ref[0]

    def step(quad, counts):
        n_own, n_halo = counts
        for j in range(4):
            slot = quad * 4 + j
            column = column_ref[slot]
            entry = slot + (row_ref[slot] << 16)
            own_ref[n_own] = entry + (column << 8)
            halo_ref[n_halo] = entry + ((column - part) << 8)
            used = slot < live
            is_own = used & (column < part)
            is_halo = used & (column >= part)
            n_own = n_own + is_own.astype(jnp.int32)
            n_halo = n_halo + is_halo.astype(jnp.int32)
        return n_own, n_halo

    n_own, n_halo = lax.fori_loop(0, lax.div(live + 3, 4), step, (jnp.int32(0), jnp.int32(0)))
    for ref, count in ((own_ref, n_own), (halo_ref, n_halo)):
        for extra in range(GROUP):
            ref[count + extra] = RB << 16
    count_ref[0] = n_own
    count_ref[1] = n_halo
    count_ref[2] = live


def make_lists(slot_row, slot_column, live_slots, part):
    return call(
        functools.partial(list_kernel, part),
        (shaped((LEN,), jnp.int32), shaped((LEN,), jnp.int32), shaped((3,), jnp.int32)),
        [SMEM, SMEM, SMEM],
        (SMEM, SMEM, SMEM),
        moved=20000,
    )(slot_row, slot_column, live_slots)


def split3(value):
    high = value.astype(BF16).astype(F32)
    rest = value - high
    middle = rest.astype(BF16).astype(F32)
    return high, middle, (rest - middle).astype(BF16).astype(F32)


def cast_kernel(field_hbm, degree_hbm, tiles_ref, field_ref, degree_ref, sems):
    copies = [
        pltpu.make_async_copy(field_hbm, field_ref, sems.at[0]),
        pltpu.make_async_copy(degree_hbm, degree_ref, sems.at[1]),
    ]
    for copy in copies:
        copy.start()
    for copy in copies:
        copy.wait()
    for block in range(RB):
        tiles_ref[block + 2 * (block // HALF)] = field_ref[:, columns(block)].astype(BF16)
    for half in range(2):
        inverse = 1.0 / degree_ref[half * HALF : (half + 1) * HALF]
        high = inverse.astype(BF16)
        at = half * (HALF + 2) + HALF
        tiles_ref[at] = high
        tiles_ref[at + 1] = (inverse - high.astype(F32)).astype(BF16)


def cast_tiles(field, degree):
    return call(
        cast_kernel,
        shaped((RB + 4, K, BS), BF16),
        [HBM, HBM],
        VMEM,
        (pltpu.VMEM(field.shape, F32), pltpu.VMEM(degree.shape, F32), pltpu.SemaphoreType.DMA((2,))),
        moved=400000,
    )(field, degree)


def gather_row(tiles, n_row, half):
    up = [(i, (i + 1) % n_row) for i in range(n_row)]
    down = [(i, (i - 1) % n_row) for i in range(n_row)]
    pieces = [(0, tiles)]
    from_below = from_above = tiles
    for step in range(1, n_row // 2):
        from_below = lax.ppermute(from_below, "row", up)
        from_above = lax.ppermute(from_above, "row", down)
        pieces += [(-step, from_below), (step, from_above)]
    far_low = lax.ppermute(from_below[:half], "row", up)
    far_high = lax.ppermute(from_above[half:], "row", down)
    return pieces, far_low, far_high


def halves(offsets, pieces, half, n_row, place):
    parts = []
    for offset, piece in zip(offsets, pieces):
        owner = lax.rem(place + offset + n_row, n_row)
        parts += [(owner, 0, piece, 0), (owner, 1, piece, half)]
    owner = lax.rem(place + n_row // 2, n_row)
    return parts + [(owner, 0, pieces[-2], 0), (owner, 1, pieces[-1], 0)]


def fill_and_send(fill, chosen_ref, chosen_hbm, sems):
    peers = chosen_ref.shape[0] // EXTRA
    quarter = max(1, peers // 4)
    copies = []
    for at in range(peers // quarter):

        def step(peer, carry):
            fill(peer)
            return carry

        lax.fori_loop(at * quarter, (at + 1) * quarter, step, 0)
        span = pl.ds(at * quarter * EXTRA, quarter * EXTRA)
        copies.append(pltpu.make_async_copy(chosen_ref.at[span], chosen_hbm.at[span], sems.at[at]))
        copies[-1].start()
    for copy in copies:
        copy.wait()


def first_select_kernel(offsets, n_row, place_ref, send_ref, *refs):
    pieces, (part_ref, inverse_ref, chosen_hbm, rows_ref, chosen_ref, sems) = refs[:-6], refs[-6:]
    for owner, half, piece, start in halves(offsets, pieces, HALF + 2, n_row, place_ref[0]):
        at = owner * RB + half * HALF
        part_ref[pl.ds(at, HALF)] = piece[start : start + HALF]
        inverse_ref[pl.ds(pl.multiple_of(at, HALF), HALF), :] = (
            piece[start + HALF].astype(F32) + piece[start + HALF + 1].astype(F32)
        )

    def fill(peer):
        for j in range(SEND):
            block = send_ref[peer * SEND + j]
            chosen_ref[peer * EXTRA + j] = part_ref[block]
            rows_ref[j : j + 1, :] = inverse_ref[pl.ds(block, 1), :]
        rows = rows_ref[...]
        high = rows.astype(BF16).astype(F32)
        chosen_ref[peer * EXTRA + SEND] = jnp.concatenate([high, rows - high], axis=0).astype(BF16)

    fill_and_send(fill, chosen_ref, chosen_hbm, sems)


def first_select(gathered, place, send_list, n_row):
    pieces, far_low, far_high = gathered
    part = n_row * RB
    peers = send_list.shape[0] // SEND
    return call(
        functools.partial(first_select_kernel, [offset for offset, _ in pieces], n_row),
        (shaped((part, K, BS), BF16), shaped((part, BS), F32), pltpu.HBM((peers * EXTRA, K, BS), BF16)),
        [SMEM, SMEM] + [VMEM] * (len(pieces) + 2),
        (VMEM, VMEM, HBM),
        (pltpu.VMEM((SEND, BS), F32), pltpu.VMEM((peers * EXTRA, K, BS), BF16), pltpu.SemaphoreType.DMA((4,))),
        moved=3000000,
    )(place, send_list, *[piece for _, piece in pieces], far_low, far_high)


def second_select_kernel(offsets, n_row, place_ref, send_ref, pick_ref, *refs):
    pieces, (part_ref, chosen_hbm, table_ref, chosen_ref, sems) = refs[:-5], refs[-5:]
    lane = iota2((K, BS), 1)
    table = jnp.zeros((K, BS), F32)
    side_sum = jnp.zeros((K, BS), F32)
    for owner, half, piece, start in halves(offsets, pieces, HALF, n_row, place_ref[0]):
        part_ref[pl.ds(owner * RB + half * HALF, HALF)] = piece[start : start + HALF]
        if half == 1:
            side = piece[start + HALF].astype(F32)
            table = jnp.where(lane == owner, side[:, 0:1], table)
            side_sum = side_sum + side
    top = jnp.sum(jnp.where((lane >= 1) & (lane <= 3), side_sum, 0.0), axis=1, keepdims=True)
    bottom = jnp.sum(jnp.where((lane >= 4) & (lane <= 6), side_sum, 0.0), axis=1, keepdims=True)
    for at, value in enumerate(split3(top) + split3(bottom)):
        table = jnp.where(lane == 8 + at, value, table)
    table = table.astype(BF16)
    table_ref[...] = table
    sides = dot_nn(table, pick_ref[...])
    for peer in range(chosen_ref.shape[0] // EXTRA):
        chosen_ref[peer * EXTRA + SEND] = sides[:, columns(peer)].astype(BF16)

    def fill(peer):
        for j in range(SEND):
            chosen_ref[peer * EXTRA + j] = part_ref[send_ref[peer * SEND + j]]

    fill_and_send(fill, chosen_ref, chosen_hbm, sems)


def second_select(gathered, place, send_list, pick, n_row):
    pieces, far_low, far_high = gathered
    peers = send_list.shape[0] // SEND
    return call(
        functools.partial(second_select_kernel, [offset for offset, _ in pieces], n_row),
        (shaped((n_row * RB, K, BS), BF16), pltpu.HBM((peers * EXTRA, K, BS), BF16), shaped((K, BS), BF16)),
        [SMEM, SMEM] + [VMEM] * (len(pieces) + 3),
        (VMEM, HBM, VMEM),
        (pltpu.VMEM((peers * EXTRA, K, BS), BF16), pltpu.SemaphoreType.DMA((4,))),
        moved=3000000,
    )(place, send_list, pick, *[piece for _, piece in pieces], far_low, far_high)


def picks(send_list):
    peers = send_list.shape[0] // SEND
    owner = (send_list >> 5).reshape(peers, SEND)
    lane = jnp.broadcast_to(jnp.arange(BS, dtype=jnp.int32)[None, :], (peers, BS))
    target = jnp.where(lane < 14, lane, -1)
    target = jnp.concatenate([owner, target[:, SEND:]], axis=1).reshape(-1)
    return (jnp.arange(BS, dtype=jnp.int32)[:, None] == target[None, :]).astype(BF16)


def fetch(live, coupling_ref, held, sems):
    def start(chunk, carry):
        span = pl.ds(chunk * CHUNK, CHUNK)
        pltpu.make_async_copy(coupling_ref.at[span], held.at[span], sems.at[chunk]).start()
        return carry

    lax.fori_loop(0, lax.div(live + CHUNK - 1, CHUNK), start, 0)


def work(count, live, list_ref, coupling_ref, held, sems, multiply, add):
    def wait(chunk, carry):
        span = pl.ds(chunk * CHUNK, CHUNK)
        pltpu.make_async_copy(coupling_ref.at[span], held.at[span], sems.at[chunk]).wait()
        return carry

    def step(group, waited):
        base = group * GROUP
        last = list_ref[jnp.minimum(base + GROUP, count) - 1] & 255
        needed = lax.div(last, CHUNK) + 1
        lax.fori_loop(waited, needed, wait, 0)
        entries = [list_ref[base + j] for j in range(GROUP)]
        products = [multiply((entry >> 8) & 255, held[entry & 255]) for entry in entries]
        for entry, product in zip(entries, products):
            add(entry >> 16, (entry >> 8) & 255, product)
        return jnp.maximum(waited, needed)

    waited = lax.fori_loop(0, lax.div(count + GROUP - 1, GROUP), step, jnp.int32(0))
    lax.fori_loop(waited, lax.div(live + CHUNK - 1, CHUNK), wait, 0)


HELD = (pltpu.VMEM((SLOTS, BS, BS), BF16), pltpu.SemaphoreType.DMA((SLOTS // CHUNK,)))
ROWS = shaped((RB + 1, K, BS), F32)


def scale_block(block, inverse):
    return (block.astype(F32) * inverse).astype(BF16)


def first_own_kernel(list_ref, count_ref, part_ref, coupling_ref, acc_ref, held, sems):
    fetch(count_ref[2], coupling_ref, held, sems)
    acc_ref[...] = jnp.zeros_like(acc_ref)

    def multiply(block, weights):
        return dot_nt(part_ref[block], weights)

    def add(row, block, product):
        acc_ref[row] = acc_ref[row] + product

    work(count_ref[0], count_ref[2], list_ref, coupling_ref, held, sems, multiply, add)


def first_own(own_list, counts, part_tiles, coupling):
    return call(
        first_own_kernel,
        ROWS,
        [SMEM, SMEM, VMEM, HBM],
        VMEM,
        HELD,
        flops=2 * SLOTS * K * BS * BS,
        moved=10000000,
    )(own_list, counts, part_tiles, coupling)


def image_kernel(
    list_ref, count_ref, halo_ref, coupling_ref, own_ref, basis_ref, degree_ref, image_ref, tiles_ref, acc_ref, held,
    sems,
):
    fetch(count_ref[2], coupling_ref, held, sems)
    acc_ref[...] = own_ref[...]

    def multiply(block, weights):
        return dot_nt(halo_ref[block + (block >> 3)], weights)

    def add(row, block, product):
        acc_ref[row] = acc_ref[row] + product

    work(count_ref[1], count_ref[2], list_ref, coupling_ref, held, sems, multiply, add)
    top = jnp.zeros((K, BS), F32)
    bottom = jnp.zeros((K, BS), F32)
    for block in range(RB):
        at = columns(block)
        basis = basis_ref[:, at]
        image = degree_ref[block : block + 1, :] * basis - acc_ref[block]
        image_ref[:, at] = image
        top = top + basis * image
        bottom = bottom + basis * basis
    top = jnp.sum(top, axis=1, keepdims=True)
    bottom = jnp.sum(bottom, axis=1, keepdims=True)
    usable = bottom > 1e-30
    quotient = jnp.where(usable, top / jnp.where(usable, bottom, 1.0), 0.0).astype(BF16).astype(F32)
    for block in range(RB):
        at = columns(block)
        residual = (image_ref[:, at] - quotient * basis_ref[:, at]) / degree_ref[block : block + 1, :]
        tiles_ref[block] = residual.astype(BF16)
    lane = iota2((K, BS), 1)
    side = jnp.where(lane == 0, quotient, 0.0)
    for at, value in enumerate(split3(top) + split3(bottom)):
        side = jnp.where(lane == 1 + at, value, side)
    tiles_ref[RB] = side.astype(BF16)


def make_image(halo_list, counts, halo_tiles, coupling, own, basis, degree):
    return call(
        image_kernel,
        (shaped(basis.shape, F32), shaped((RB + 1, K, BS), BF16)),
        [SMEM, SMEM, VMEM, HBM, VMEM, VMEM, VMEM],
        (VMEM, VMEM),
        (pltpu.VMEM((RB + 1, K, BS), F32),) + HELD,
        flops=2 * SLOTS * K * BS * BS,
        moved=8000000,
    )(halo_list, counts, halo_tiles, coupling, own, basis, degree)


def second_own_kernel(
    list_ref, count_ref, part_ref, table_ref, basis_part_ref, inverse_ref, coupling_ref, acc_ref, scaled_ref, held,
    sems, quotient_ref,
):
    fetch(count_ref[2], coupling_ref, held, sems)
    acc_ref[...] = jnp.zeros_like(acc_ref)
    scaled_ref[...] = jnp.zeros_like(scaled_ref)
    table = table_ref[...].astype(F32)
    for owner in range(quotient_ref.shape[0]):
        quotient_ref[owner] = jnp.broadcast_to(table[:, owner : owner + 1], (K, BS))

    def multiply(block, weights):
        scaled = scale_block(basis_part_ref[block], inverse_ref[pl.ds(block, 1), :])
        return dot_nt(jnp.concatenate([part_ref[block], scaled], axis=0), weights)

    def add(row, block, product):
        acc_ref[row] = acc_ref[row] + (product[0:K] + quotient_ref[block >> 5] * product[K:])
        scaled_ref[row] = scaled_ref[row] + product[K:]

    work(count_ref[0], count_ref[2], list_ref, coupling_ref, held, sems, multiply, add)


def second_own(own_list, counts, part_tiles, table, basis_part, inverse, coupling, n_row):
    return call(
        second_own_kernel,
        (ROWS, ROWS),
        [SMEM, SMEM, VMEM, VMEM, VMEM, VMEM, HBM],
        (VMEM, VMEM),
        HELD + (pltpu.VMEM((n_row, K, BS), F32),),
        flops=4 * SLOTS * K * BS * BS,
        moved=10000000,
    )(own_list, counts, part_tiles, table, basis_part, inverse, coupling)


def spread_kernel(taken_ref, given_ref):
    total = taken_ref[0]
    for peer in range(1, taken_ref.shape[0]):
        total = total + taken_ref[peer]
    for peer in range(given_ref.shape[0]):
        given_ref[peer] = total


def add_and_repeat(taken, peers):
    return call(
        spread_kernel, shaped((peers,) + taken.shape[1:], F32), [VMEM], VMEM, moved=400000
    )(taken)


def square(value, wide_ref):
    rows, cols = value.shape
    wide_ref[...] = jnp.zeros_like(wide_ref)
    wide_ref[0:rows, 0:cols] = value
    return wide_ref[...]


def pack_grams(gram_b, gram_a, wide_ref):
    wide_a = square(gram_a, wide_ref)
    both = 0.5 * (wide_a + wide_a.T)
    wide_b = square(gram_b, wide_ref)
    row = iota2((BS, BS), 0)
    lane = iota2((BS, BS), 1)
    packed = jnp.where(row <= lane, wide_b, both)
    diagonal = jnp.sum(jnp.where(row == lane, both, 0.0), axis=1, keepdims=True)
    low, high = packed[0:24], pltpu.roll(packed[24:48], 48, 1)
    at = iota2((24, BS), 1)
    out = jnp.where(at < 48, low, high)
    out = jnp.where(at == 96, diagonal[0:24], out)
    return jnp.where(at == 97, diagonal[24:48], out)


def unpack_grams(packed, wide_ref):
    wide_ref[...] = jnp.zeros_like(wide_ref)
    at = iota2((24, BS), 1)
    wide_ref[0:24] = jnp.where(at < 48, packed, 0.0)
    wide_ref[24:48] = jnp.where(at < 48, pltpu.roll(packed, 80, 1), 0.0)
    wide = wide_ref[...]
    flipped = wide.T
    row = iota2((48, BS), 0)
    lane = iota2((48, BS), 1)
    wide, flipped = wide[0:48], flipped[0:48]
    diagonal = jnp.concatenate([packed[:, 96:97], packed[:, 97:98]], axis=0)
    gram_b = jnp.where(row <= lane, wide, flipped)
    gram_a = jnp.where(row == lane, diagonal, jnp.where(row > lane, wide, flipped))
    return gram_b, gram_a


def gram_kernel(
    list_ref, count_ref, halo_ref, basis_halo_ref, coupling_ref, own_ref, own_scaled_ref, basis_ref, image_ref, degree_ref,
    previous_ref, previous_image_ref, residual_ref, residual_image_ref, packed_ref, acc_ref, scaled_ref, held, sems,
    side_ref, quotient_ref, inverse_ref, stacked, stacked_image, wide_ref,
):
    fetch(count_ref[2], coupling_ref, held, sems)
    acc_ref[...] = own_ref[...]
    scaled_ref[...] = own_scaled_ref[...]
    peers = halo_ref.shape[0] // EXTRA
    total = jnp.zeros((K, BS), F32)
    for peer in range(peers):
        side = halo_ref[peer * EXTRA + SEND]
        side_ref[peer * K : (peer + 1) * K, :] = side
        total = total + side.astype(F32)
        inverse = basis_halo_ref[peer * EXTRA + SEND].astype(F32)
        inverse_ref[peer * SEND : (peer + 1) * SEND, :] = inverse[0:SEND] + inverse[SEND:]
    side = side_ref[...]
    for j in range(SEND):
        spread = (iota2((BS, BS), 0) == j).astype(F32).astype(BF16)
        quotient_ref[j] = dot_nn(side, spread).reshape(peers, K, BS)
    lane = iota2((K, BS), 1)
    top = jnp.sum(jnp.where((lane >= 8) & (lane <= 10), total, 0.0), axis=1, keepdims=True)
    bottom = jnp.sum(jnp.where((lane >= 11) & (lane <= 13), total, 0.0), axis=1, keepdims=True)
    theta = top / bottom

    def multiply(block, weights):
        tile = block + (block >> 3)
        scaled = scale_block(basis_halo_ref[tile], inverse_ref[pl.ds(block, 1), :])
        return dot_nt(jnp.concatenate([halo_ref[tile], scaled], axis=0), weights)

    def add(row, block, product):
        quotient = quotient_ref[block & 7, block >> 3]
        acc_ref[row] = acc_ref[row] + (product[0:K] + quotient * product[K:])
        scaled_ref[row] = scaled_ref[row] + product[K:]

    work(count_ref[1], count_ref[2], list_ref, coupling_ref, held, sems, multiply, add)
    stacked[0:16] = basis_ref[...]
    stacked[32:48] = previous_ref[...]
    stacked_image[0:16] = image_ref[...]
    stacked_image[32:48] = previous_image_ref[...]
    for block in range(RB):
        at = columns(block)
        degree = degree_ref[block : block + 1, :]
        residual = (image_ref[:, at] - theta * basis_ref[:, at]) / degree
        residual_ref[:, at] = residual
        stacked[16:32, at] = residual
        value = degree * residual - (acc_ref[block] - theta * scaled_ref[block])
        residual_image_ref[:, at] = value
        stacked_image[16:32, at] = value
    gram_b = dot_nt(stacked[...], stacked[...], HIGHEST)
    gram_a = dot_nt(stacked[...], stacked_image[...], HIGHEST)
    packed = pack_grams(gram_b, gram_a, wide_ref)
    for peer in range(packed_ref.shape[0]):
        packed_ref[peer] = packed


def make_grams(
    halo_list, counts, halo_tiles, basis_halo, coupling, own, scaled, basis, image, degree, previous, previous_image, n_dom
):
    width = basis.shape[1]
    return call(
        gram_kernel,
        (shaped(basis.shape, F32), shaped(basis.shape, F32), shaped((n_dom, 24, BS), F32)),
        [SMEM, SMEM, VMEM, VMEM, HBM] + [VMEM] * 7,
        (VMEM, VMEM, VMEM),
        (pltpu.VMEM((RB + 1, K, BS), F32), pltpu.VMEM((RB + 1, K, BS), F32))
        + HELD
        + (
            pltpu.VMEM((n_dom * K, BS), BF16),
            pltpu.VMEM((SEND, n_dom, K, BS), F32),
            pltpu.VMEM((n_dom * SEND, BS), F32),
            pltpu.VMEM((48, width), F32),
            pltpu.VMEM((48, width), F32),
            pltpu.VMEM((BS, BS), F32),
        ),
        flops=2 * SLOTS * K * BS * BS,
        moved=10000000,
    )(halo_list, counts, halo_tiles, basis_halo, coupling, own, scaled, basis, image, degree, previous, previous_image)


def inverse_factor(gram, n):
    row = iota2((n, BS), 0)
    lane = iota2((n, BS), 1)
    work = jnp.where(lane < n, gram, jnp.where(lane == row + n, 1.0, 0.0))
    for first in range(0, n, 8):
        left = [jnp.broadcast_to(work[:, first + j : first + j + 1], (n, BS)) for j in range(8)]
        rows = [work[first + j : first + j + 1, :] for j in range(8)]
        for j in range(8):
            scale = lax.rsqrt(left[j][first + j : first + j + 1, :])
            rows[j] = rows[j] * scale
            left[j] = jnp.where(row > first + j, left[j] * scale, 0.0)
            for k in range(j + 1, 8):
                entry = left[j][first + k : first + k + 1, :]
                rows[k] = rows[k] - entry * rows[j]
                left[k] = left[k] - left[j] * entry
        for j in range(8):
            work = jnp.where(row == first + j, rows[j], work - left[j] * rows[j])
    return pltpu.roll(work, BS - n, 1)


def final_kernel(
    root_rows, taken_ref, basis_ref, residual_ref, previous_ref, image_ref, residual_image_ref, previous_image_ref,
    new_basis_ref, new_image_ref, wide_ref, stacked,
):
    packed = taken_ref[0]
    for peer in range(1, taken_ref.shape[0]):
        packed = packed + taken_ref[peer]
    gram_b, gram_a = unpack_grams(packed, wide_ref)
    inverse = inverse_factor(gram_b, 48)[:, 0:48]
    symmetric = gram_a[:, 0:48]
    reduced = dot_nt(dot_nn(inverse, symmetric, HIGHEST), inverse, HIGHEST)
    wide = square(reduced, wide_ref)
    reduced = 0.5 * (wide + wide.T)[0:48, 0:48]
    spread = jnp.max(jnp.sum(jnp.abs(reduced), axis=1, keepdims=True), axis=0, keepdims=True)
    row = iota2((48, 48), 0)
    lane = iota2((48, 48), 1)
    filter_mat = (jnp.where(row == lane, spread, 0.0) - reduced) / (2.0 * spread)
    turned = filter_mat[0:16, :]
    for repeat in range(3):
        turned = dot_nn(turned, filter_mat, HIGHEST)
    inner = dot_nt(turned, turned, HIGHEST)
    wide_ref[...] = jnp.zeros_like(wide_ref)
    wide_ref[0:16, 0:16] = inner
    sub_inverse = inverse_factor(wide_ref[0:16, :], 16)[:, 0:16]
    coeff = dot_nn(dot_nn(sub_inverse, turned, HIGHEST), inverse, HIGHEST) * root_rows
    stacked[0:16] = basis_ref[...]
    stacked[16:32] = residual_ref[...]
    stacked[32:48] = previous_ref[...]
    new_basis_ref[...] = dot_nn(coeff, stacked[...], HIGHEST)
    stacked[0:16] = image_ref[...]
    stacked[16:32] = residual_image_ref[...]
    stacked[32:48] = previous_image_ref[...]
    new_image_ref[...] = dot_nn(coeff, stacked[...], HIGHEST)


def finish(root_rows, packed, basis, residual, previous, image, residual_image, previous_image):
    return call(
        functools.partial(final_kernel, root_rows),
        (shaped(basis.shape, F32), shaped(basis.shape, F32)),
        [VMEM] * 7,
        (VMEM, VMEM),
        (pltpu.VMEM((BS, BS), F32), pltpu.VMEM((48, basis.shape[1]), F32)),
        flops=1000000,
        moved=3000000,
    )(packed, basis, residual, previous, image, residual_image, previous_image)


def to_all(value, axis):
    return lax.all_to_all(value, axis, split_axis=0, concat_axis=0, tiled=True)


def body(
    n_dom, n_row,
    basis, previous, previous_image, degree, coupling, slot_row, slot_column, send_lists, live_slots,
):
    part = n_row * RB
    place = lax.axis_index("row").astype(jnp.int32).reshape(1)
    send_list = send_lists.reshape(n_dom * SEND)
    degree = degree.reshape(RB, BS)
    coupling = pltpu.with_memory_space_constraint(coupling, pltpu.HBM)
    own_list, halo_list, counts = make_lists(slot_row, slot_column, live_slots, part)

    in_hbm = [pltpu.with_memory_space_constraint(value, pltpu.HBM) for value in (basis, degree)]
    gathered = gather_row(cast_tiles(*in_hbm), n_row, HALF + 2)
    basis_part, inverse, chosen = first_select(gathered, place, send_list, n_row)
    basis_halo = to_all(chosen, "dom")
    own = first_own(own_list, counts, basis_part, coupling)
    image, tiles = make_image(halo_list, counts, basis_halo, coupling, own, basis, degree)

    gathered = gather_row(tiles, n_row, HALF)
    part_tiles, chosen, table = second_select(gathered, place, send_list, picks(send_list), n_row)
    halo_tiles = to_all(chosen, "dom")
    own, scaled = second_own(own_list, counts, part_tiles, table, basis_part, inverse, coupling, n_row)
    residual, residual_image, packed = make_grams(
        halo_list, counts, halo_tiles, basis_halo, coupling, own, scaled, basis, image, degree, previous, previous_image,
        n_dom,
    )
    packed = to_all(add_and_repeat(to_all(packed, "dom"), n_row), "row")
    root_rows = math.sqrt(basis.shape[1] * n_dom * n_row)
    return finish(root_rows, packed, basis, residual, previous, image, residual_image, previous_image)


def solution(mesh):
    split = P(None, ("dom", "row"))
    flat = P(("dom", "row"))
    return jax.shard_map(
        functools.partial(body, mesh.shape["dom"], mesh.shape["row"]),
        mesh=mesh,
        in_specs=(
            split, split, split, flat, P(("dom", "row"), None, None), flat, flat, P("dom", None, None), flat,
        ),
        out_specs=(split, split),
        check_vma=False,
    )
```

```python
import functools
import math

import jax
import jax.numpy as jnp
from jax import lax
from jax.experimental import pallas as pl
from jax.experimental.pallas import tpu as pltpu
from jax.sharding import PartitionSpec as P

K = 16
BS = 128
RB = 32
SLOTS = 256
SEND = 8
HALF = RB // 2
EXTRA = SEND + 1
CHUNK = 32
GROUP = 32
LEN = SLOTS + GROUP
F32 = jnp.float32
BF16 = jnp.bfloat16
HIGHEST = lax.Precision.HIGHEST
MARGIN = 6 * 1024 * 1024
SMEM = pl.BlockSpec(memory_space=pltpu.SMEM)
HBM = pl.BlockSpec(memory_space=pl.ANY)
VMEM = pl.BlockSpec(memory_space=pltpu.VMEM)


def size(array):
    return math.prod(array.shape) * jnp.dtype(array.dtype).itemsize


def call(kernel, out_shape, in_specs, out_specs, scratch=(), flops=0, moved=0):
    def run(*args):
        arrays = list(args) + jax.tree.leaves(out_shape) + [held for held in scratch if jnp.issubdtype(held.dtype, jnp.floating)]
        return pl.pallas_call(
            kernel,
            out_shape=out_shape,
            in_specs=in_specs,
            out_specs=out_specs,
            scratch_shapes=scratch,
            compiler_params=pltpu.CompilerParams(vmem_limit_bytes=MARGIN + sum(map(size, arrays))),
            cost_estimate=pl.CostEstimate(flops=flops, bytes_accessed=moved, transcendentals=0),
        )(*args)

    return run


def shaped(shape, dtype):
    return jax.ShapeDtypeStruct(shape, dtype)


def in_hbm(value):
    return pltpu.with_memory_space_constraint(value, pltpu.HBM)


def start_copies(pairs, sems, first=0):
    copies = [pltpu.make_async_copy(source, target, sems.at[first + i]) for i, (source, target) in enumerate(pairs)]
    for copy in copies:
        copy.start()
    return copies


def wait_all(copies):
    for copy in copies:
        copy.wait()


def dot_nt(left, right, precision=None):
    return lax.dot_general(
        left, right, (((1,), (1,)), ((), ())), precision=precision, preferred_element_type=F32
    )


def dot_nn(left, right, precision=None):
    return lax.dot_general(
        left, right, (((1,), (0,)), ((), ())), precision=precision, preferred_element_type=F32
    )


def columns(block):
    return slice(block * BS, (block + 1) * BS)


def iota2(shape, axis):
    return lax.broadcasted_iota(jnp.int32, shape, axis)


def list_kernel(part, row_ref, column_ref, live_ref, own_ref, halo_ref, count_ref):
    live = live_ref[0]

    def step(quad, counts):
        n_own, n_halo = counts
        for j in range(4):
            slot = quad * 4 + j
            column = column_ref[slot]
            entry = slot + (row_ref[slot] << 16)
            own_ref[n_own] = entry + (column << 8)
            halo_ref[n_halo] = entry + ((column - part) << 8)
            used = slot < live
            is_own = used & (column < part)
            is_halo = used & (column >= part)
            n_own = n_own + is_own.astype(jnp.int32)
            n_halo = n_halo + is_halo.astype(jnp.int32)
        return n_own, n_halo

    n_own, n_halo = lax.fori_loop(0, lax.div(live + 3, 4), step, (jnp.int32(0), jnp.int32(0)))
    for ref, count in ((own_ref, n_own), (halo_ref, n_halo)):
        for extra in range(GROUP):
            ref[count + extra] = RB << 16
    count_ref[0] = n_own
    count_ref[1] = n_halo
    count_ref[2] = live


def make_lists(slot_row, slot_column, live_slots, part):
    return call(
        functools.partial(list_kernel, part),
        (shaped((LEN,), jnp.int32), shaped((LEN,), jnp.int32), shaped((3,), jnp.int32)),
        [SMEM, SMEM, SMEM],
        (SMEM, SMEM, SMEM),
        moved=20000,
    )(slot_row, slot_column, live_slots)


def split3(value):
    high = value.astype(BF16).astype(F32)
    rest = value - high
    middle = rest.astype(BF16).astype(F32)
    return high, middle, (rest - middle).astype(BF16).astype(F32)


def cast_kernel(field_hbm, degree_hbm, tiles_ref, field_ref, degree_ref, sems):
    wait_all(start_copies([(field_hbm, field_ref), (degree_hbm, degree_ref)], sems))
    for block in range(RB):
        tiles_ref[block + 2 * (block // HALF)] = field_ref[:, columns(block)].astype(BF16)
    for half in range(2):
        inverse = 1.0 / degree_ref[half * HALF : (half + 1) * HALF]
        high = inverse.astype(BF16)
        at = half * (HALF + 2) + HALF
        tiles_ref[at] = high
        tiles_ref[at + 1] = (inverse - high.astype(F32)).astype(BF16)


def cast_tiles(field, degree):
    return call(
        cast_kernel,
        shaped((RB + 4, K, BS), BF16),
        [HBM, HBM],
        VMEM,
        (pltpu.VMEM(field.shape, F32), pltpu.VMEM(degree.shape, F32), pltpu.SemaphoreType.DMA((2,))),
        moved=400000,
    )(field, degree)


def gather_row(tiles, n_row, half):
    up = [(i, (i + 1) % n_row) for i in range(n_row)]
    down = [(i, (i - 1) % n_row) for i in range(n_row)]
    pieces = [(0, tiles)]
    from_below = from_above = tiles
    for step in range(1, n_row // 2):
        from_below = lax.ppermute(from_below, "row", up)
        from_above = lax.ppermute(from_above, "row", down)
        pieces += [(-step, from_below), (step, from_above)]
    far_low = lax.ppermute(from_below[:half], "row", up)
    far_high = lax.ppermute(from_above[half:], "row", down)
    return pieces, far_low, far_high


def halves(offsets, pieces, half, n_row, place):
    parts = []
    for offset, piece in zip(offsets, pieces):
        owner = lax.rem(place + offset + n_row, n_row)
        parts += [(owner, 0, piece, 0), (owner, 1, piece, half)]
    owner = lax.rem(place + n_row // 2, n_row)
    return parts + [(owner, 0, pieces[-2], 0), (owner, 1, pieces[-1], 0)]


def fill_and_send(fill, chosen_ref, chosen_hbm, sems):
    peers = chosen_ref.shape[0] // EXTRA
    quarter = max(1, peers // 4)
    copies = []
    for at in range(peers // quarter):

        def step(peer, carry):
            fill(peer)
            return carry

        lax.fori_loop(at * quarter, (at + 1) * quarter, step, 0)
        span = pl.ds(at * quarter * EXTRA, quarter * EXTRA)
        copies.append(pltpu.make_async_copy(chosen_ref.at[span], chosen_hbm.at[span], sems.at[at]))
        copies[-1].start()
    for copy in copies:
        copy.wait()


def first_select_kernel(offsets, n_row, place_ref, send_ref, *refs):
    pieces, (part_hbm, inverse_hbm, chosen_hbm) = refs[:-8], refs[-8:-5]
    part_ref, inverse_ref, rows_ref, chosen_ref, sems = refs[-5:]
    for owner, half, piece, start in halves(offsets, pieces, HALF + 2, n_row, place_ref[0]):
        at = owner * RB + half * HALF
        part_ref[pl.ds(at, HALF)] = piece[start : start + HALF]
        inverse_ref[pl.ds(pl.multiple_of(at, HALF), HALF), :] = (
            piece[start + HALF].astype(F32) + piece[start + HALF + 1].astype(F32)
        )

    copies = start_copies([(part_ref, part_hbm), (inverse_ref, inverse_hbm)], sems, 4)

    def fill(peer):
        for j in range(SEND):
            block = send_ref[peer * SEND + j]
            chosen_ref[peer * EXTRA + j] = part_ref[block]
            rows_ref[j : j + 1, :] = inverse_ref[pl.ds(block, 1), :]
        rows = rows_ref[...]
        high = rows.astype(BF16).astype(F32)
        chosen_ref[peer * EXTRA + SEND] = jnp.concatenate([high, rows - high], axis=0).astype(BF16)

    fill_and_send(fill, chosen_ref, chosen_hbm, sems)
    wait_all(copies)


def first_select(gathered, place, send_list, n_row):
    pieces, far_low, far_high = gathered
    part = n_row * RB
    peers = send_list.shape[0] // SEND
    return call(
        functools.partial(first_select_kernel, [offset for offset, _ in pieces], n_row),
        (pltpu.HBM((part, K, BS), BF16), pltpu.HBM((part, BS), F32), pltpu.HBM((peers * EXTRA, K, BS), BF16)),
        [SMEM, SMEM] + [VMEM] * (len(pieces) + 2),
        (HBM, HBM, HBM),
        (
            pltpu.VMEM((part, K, BS), BF16),
            pltpu.VMEM((part, BS), F32),
            pltpu.VMEM((SEND, BS), F32),
            pltpu.VMEM((peers * EXTRA, K, BS), BF16),
            pltpu.SemaphoreType.DMA((6,)),
        ),
        moved=3000000,
    )(place, send_list, *[piece for _, piece in pieces], far_low, far_high)


def second_select_kernel(offsets, n_row, place_ref, send_ref, pick_ref, *refs):
    pieces, (part_hbm, chosen_hbm, table_hbm, part_ref, chosen_ref, table_ref, sems) = refs[:-7], refs[-7:]
    lane = iota2((K, BS), 1)
    table = jnp.zeros((K, BS), F32)
    side_sum = jnp.zeros((K, BS), F32)
    for owner, half, piece, start in halves(offsets, pieces, HALF, n_row, place_ref[0]):
        part_ref[pl.ds(owner * RB + half * HALF, HALF)] = piece[start : start + HALF]
        if half == 1:
            side = piece[start + HALF].astype(F32)
            table = jnp.where(lane == owner, side[:, 0:1], table)
            side_sum = side_sum + side
    top = jnp.sum(jnp.where((lane >= 1) & (lane <= 3), side_sum, 0.0), axis=1, keepdims=True)
    bottom = jnp.sum(jnp.where((lane >= 4) & (lane <= 6), side_sum, 0.0), axis=1, keepdims=True)
    for at, value in enumerate(split3(top) + split3(bottom)):
        table = jnp.where(lane == 8 + at, value, table)
    table = table.astype(BF16)
    table_ref[...] = table
    copies = start_copies([(part_ref, part_hbm), (table_ref, table_hbm)], sems, 4)
    sides = dot_nn(table, pick_ref[...])
    for peer in range(chosen_ref.shape[0] // EXTRA):
        chosen_ref[peer * EXTRA + SEND] = sides[:, columns(peer)].astype(BF16)

    def fill(peer):
        for j in range(SEND):
            chosen_ref[peer * EXTRA + j] = part_ref[send_ref[peer * SEND + j]]

    fill_and_send(fill, chosen_ref, chosen_hbm, sems)
    wait_all(copies)


def second_select(gathered, place, send_list, pick, n_row):
    pieces, far_low, far_high = gathered
    peers = send_list.shape[0] // SEND
    return call(
        functools.partial(second_select_kernel, [offset for offset, _ in pieces], n_row),
        (pltpu.HBM((n_row * RB, K, BS), BF16), pltpu.HBM((peers * EXTRA, K, BS), BF16), pltpu.HBM((K, BS), BF16)),
        [SMEM, SMEM] + [VMEM] * (len(pieces) + 3),
        (HBM, HBM, HBM),
        (
            pltpu.VMEM((n_row * RB, K, BS), BF16),
            pltpu.VMEM((peers * EXTRA, K, BS), BF16),
            pltpu.VMEM((K, BS), BF16),
            pltpu.SemaphoreType.DMA((6,)),
        ),
        moved=3000000,
    )(place, send_list, pick, *[piece for _, piece in pieces], far_low, far_high)


def picks(send_list):
    peers = send_list.shape[0] // SEND
    owner = (send_list >> 5).reshape(peers, SEND)
    lane = jnp.broadcast_to(jnp.arange(BS, dtype=jnp.int32)[None, :], (peers, BS))
    target = jnp.where(lane < 14, lane, -1)
    target = jnp.concatenate([owner, target[:, SEND:]], axis=1).reshape(-1)
    return (jnp.arange(BS, dtype=jnp.int32)[:, None] == target[None, :]).astype(BF16)


def fetch(live, coupling_ref, held, sems):
    def start(chunk, carry):
        span = pl.ds(chunk * CHUNK, CHUNK)
        pltpu.make_async_copy(coupling_ref.at[span], held.at[span], sems.at[chunk]).start()
        return carry

    lax.fori_loop(0, lax.div(live + CHUNK - 1, CHUNK), start, 0)


def work(count, live, list_ref, coupling_ref, held, sems, multiply, add):
    def wait(chunk, carry):
        span = pl.ds(chunk * CHUNK, CHUNK)
        pltpu.make_async_copy(coupling_ref.at[span], held.at[span], sems.at[chunk]).wait()
        return carry

    def step(group, waited):
        base = group * GROUP
        last = list_ref[jnp.minimum(base + GROUP, count) - 1] & 255
        needed = lax.div(last, CHUNK) + 1
        lax.fori_loop(waited, needed, wait, 0)
        entries = [list_ref[base + j] for j in range(GROUP)]
        products = [multiply((entry >> 8) & 255, held[entry & 255]) for entry in entries]
        for entry, product in zip(entries, products):
            add(entry >> 16, (entry >> 8) & 255, product)
        return jnp.maximum(waited, needed)

    waited = lax.fori_loop(0, lax.div(count + GROUP - 1, GROUP), step, jnp.int32(0))
    lax.fori_loop(waited, lax.div(live + CHUNK - 1, CHUNK), wait, 0)


HELD = (pltpu.VMEM((SLOTS, BS, BS), BF16), pltpu.SemaphoreType.DMA((SLOTS // CHUNK,)))
ROWS = shaped((RB + 1, K, BS), F32)


def scale_block(block, inverse):
    return (block.astype(F32) * inverse).astype(BF16)


def first_own_kernel(list_ref, count_ref, part_ref, coupling_ref, acc_ref, held, sems):
    fetch(count_ref[2], coupling_ref, held, sems)
    acc_ref[...] = jnp.zeros_like(acc_ref)

    def multiply(block, weights):
        return dot_nt(part_ref[block], weights)

    def add(row, block, product):
        acc_ref[row] = acc_ref[row] + product

    work(count_ref[0], count_ref[2], list_ref, coupling_ref, held, sems, multiply, add)


def first_own(own_list, counts, part_tiles, coupling):
    return call(
        first_own_kernel,
        ROWS,
        [SMEM, SMEM, VMEM, HBM],
        VMEM,
        HELD,
        flops=2 * SLOTS * K * BS * BS,
        moved=10000000,
    )(own_list, counts, in_hbm(part_tiles), in_hbm(coupling))


def image_kernel(
    list_ref, count_ref, halo_ref, coupling_ref, own_ref, basis_ref, degree_ref, image_hbm, tiles_ref, halo_hbm, image_ref,
    out_sems, acc_ref, held, sems,
):
    copies = start_copies([(halo_ref, halo_hbm)], out_sems)
    fetch(count_ref[2], coupling_ref, held, sems)
    acc_ref[...] = own_ref[...]

    def multiply(block, weights):
        return dot_nt(halo_ref[block + (block >> 3)], weights)

    def add(row, block, product):
        acc_ref[row] = acc_ref[row] + product

    work(count_ref[1], count_ref[2], list_ref, coupling_ref, held, sems, multiply, add)
    top = jnp.zeros((K, BS), F32)
    bottom = jnp.zeros((K, BS), F32)
    for block in range(RB):
        at = columns(block)
        basis = basis_ref[:, at]
        image = degree_ref[block : block + 1, :] * basis - acc_ref[block]
        image_ref[:, at] = image
        top = top + basis * image
        bottom = bottom + basis * basis
    copies += start_copies([(image_ref, image_hbm)], out_sems, 1)
    top = jnp.sum(top, axis=1, keepdims=True)
    bottom = jnp.sum(bottom, axis=1, keepdims=True)
    usable = bottom > 1e-30
    quotient = jnp.where(usable, top / jnp.where(usable, bottom, 1.0), 0.0).astype(BF16).astype(F32)
    for block in range(RB):
        at = columns(block)
        residual = (image_ref[:, at] - quotient * basis_ref[:, at]) / degree_ref[block : block + 1, :]
        tiles_ref[block] = residual.astype(BF16)
    lane = iota2((K, BS), 1)
    side = jnp.where(lane == 0, quotient, 0.0)
    for at, value in enumerate(split3(top) + split3(bottom)):
        side = jnp.where(lane == 1 + at, value, side)
    tiles_ref[RB] = side.astype(BF16)
    wait_all(copies)


def make_image(halo_list, counts, halo_tiles, coupling, own, basis, degree):
    return call(
        image_kernel,
        (pltpu.HBM(basis.shape, F32), shaped((RB + 1, K, BS), BF16), pltpu.HBM(halo_tiles.shape, BF16)),
        [SMEM, SMEM, VMEM, HBM, VMEM, VMEM, VMEM],
        (HBM, VMEM, HBM),
        (pltpu.VMEM(basis.shape, F32), pltpu.SemaphoreType.DMA((2,)), pltpu.VMEM((RB + 1, K, BS), F32)) + HELD,
        flops=2 * SLOTS * K * BS * BS,
        moved=8000000,
    )(halo_list, counts, halo_tiles, in_hbm(coupling), own, basis, degree)


def second_own_kernel(
    list_ref, count_ref, part_ref, table_ref, basis_part_ref, inverse_ref, coupling_ref, acc_ref, scaled_ref, held,
    sems, quotient_ref,
):
    fetch(count_ref[2], coupling_ref, held, sems)
    acc_ref[...] = jnp.zeros_like(acc_ref)
    scaled_ref[...] = jnp.zeros_like(scaled_ref)
    table = table_ref[...].astype(F32)
    for owner in range(quotient_ref.shape[0]):
        quotient_ref[owner] = jnp.broadcast_to(table[:, owner : owner + 1], (K, BS))

    def multiply(block, weights):
        scaled = scale_block(basis_part_ref[block], inverse_ref[pl.ds(block, 1), :])
        return dot_nt(jnp.concatenate([part_ref[block], scaled], axis=0), weights)

    def add(row, block, product):
        acc_ref[row] = acc_ref[row] + (product[0:K] + quotient_ref[block >> 5] * product[K:])
        scaled_ref[row] = scaled_ref[row] + product[K:]

    work(count_ref[0], count_ref[2], list_ref, coupling_ref, held, sems, multiply, add)


def second_own(own_list, counts, part_tiles, table, basis_part, inverse, coupling, n_row):
    return call(
        second_own_kernel,
        (pltpu.HBM(ROWS.shape, F32), pltpu.HBM(ROWS.shape, F32)),
        [SMEM, SMEM, VMEM, VMEM, VMEM, VMEM, HBM],
        (VMEM, VMEM),
        HELD + (pltpu.VMEM((n_row, K, BS), F32),),
        flops=4 * SLOTS * K * BS * BS,
        moved=10000000,
    )(own_list, counts, *map(in_hbm, (part_tiles, table, basis_part, inverse, coupling)))


def spread_kernel(taken_ref, given_ref):
    total = taken_ref[0]
    for peer in range(1, taken_ref.shape[0]):
        total = total + taken_ref[peer]
    for peer in range(given_ref.shape[0]):
        given_ref[peer] = total


def add_and_repeat(taken, peers):
    return call(
        spread_kernel, shaped((peers,) + taken.shape[1:], F32), [VMEM], VMEM, moved=400000
    )(taken)


def square(value, wide_ref):
    rows, cols = value.shape
    wide_ref[...] = jnp.zeros_like(wide_ref)
    wide_ref[0:rows, 0:cols] = value
    return wide_ref[...]


def pack_grams(gram_b, gram_a, wide_ref):
    wide_a = square(gram_a, wide_ref)
    both = 0.5 * (wide_a + wide_a.T)
    wide_b = square(gram_b, wide_ref)
    row = iota2((BS, BS), 0)
    lane = iota2((BS, BS), 1)
    packed = jnp.where(row <= lane, wide_b, both)
    diagonal = jnp.sum(jnp.where(row == lane, both, 0.0), axis=1, keepdims=True)
    low, high = packed[0:24], pltpu.roll(packed[24:48], 48, 1)
    at = iota2((24, BS), 1)
    out = jnp.where(at < 48, low, high)
    out = jnp.where(at == 96, diagonal[0:24], out)
    return jnp.where(at == 97, diagonal[24:48], out)


def unpack_grams(packed, wide_ref):
    wide_ref[...] = jnp.zeros_like(wide_ref)
    at = iota2((24, BS), 1)
    wide_ref[0:24] = jnp.where(at < 48, packed, 0.0)
    wide_ref[24:48] = jnp.where(at < 48, pltpu.roll(packed, 80, 1), 0.0)
    wide = wide_ref[...]
    flipped = wide.T
    row = iota2((48, BS), 0)
    lane = iota2((48, BS), 1)
    wide, flipped = wide[0:48], flipped[0:48]
    diagonal = jnp.concatenate([packed[:, 96:97], packed[:, 97:98]], axis=0)
    gram_b = jnp.where(row <= lane, wide, flipped)
    gram_a = jnp.where(row == lane, diagonal, jnp.where(row > lane, wide, flipped))
    return gram_b, gram_a


def gram_kernel(
    list_ref, count_ref, halo_ref, basis_halo_hbm, coupling_ref, own_hbm, own_scaled_hbm, basis_hbm, image_hbm, degree_hbm,
    previous_hbm, previous_image_hbm, stacked, stacked_image, packed_ref, basis_halo_ref, acc_ref, scaled_ref, degree_ref,
    in_sems, held, sems, side_ref, quotient_ref, inverse_ref, wide_ref,
):
    early = [(basis_halo_hbm, basis_halo_ref), (own_hbm, acc_ref), (own_scaled_hbm, scaled_ref)]
    late = [
        (basis_hbm, stacked.at[0:16]),
        (previous_hbm, stacked.at[32:48]),
        (image_hbm, stacked_image.at[0:16]),
        (previous_image_hbm, stacked_image.at[32:48]),
        (degree_hbm, degree_ref),
    ]
    early = start_copies(early, in_sems)
    fetch(count_ref[2], coupling_ref, held, sems)
    late = start_copies(late, in_sems, 3)
    peers = halo_ref.shape[0] // EXTRA
    total = jnp.zeros((K, BS), F32)
    for peer in range(peers):
        side = halo_ref[peer * EXTRA + SEND]
        side_ref[peer * K : (peer + 1) * K, :] = side
        total = total + side.astype(F32)
    side = side_ref[...]
    for j in range(SEND):
        spread = (iota2((BS, BS), 0) == j).astype(F32).astype(BF16)
        quotient_ref[j] = dot_nn(side, spread).reshape(peers, K, BS)
    lane = iota2((K, BS), 1)
    top = jnp.sum(jnp.where((lane >= 8) & (lane <= 10), total, 0.0), axis=1, keepdims=True)
    bottom = jnp.sum(jnp.where((lane >= 11) & (lane <= 13), total, 0.0), axis=1, keepdims=True)
    theta = top / bottom
    wait_all(early)
    for peer in range(peers):
        inverse = basis_halo_ref[peer * EXTRA + SEND].astype(F32)
        inverse_ref[peer * SEND : (peer + 1) * SEND, :] = inverse[0:SEND] + inverse[SEND:]

    def multiply(block, weights):
        tile = block + (block >> 3)
        scaled = scale_block(basis_halo_ref[tile], inverse_ref[pl.ds(block, 1), :])
        return dot_nt(jnp.concatenate([halo_ref[tile], scaled], axis=0), weights)

    def add(row, block, product):
        quotient = quotient_ref[block & 7, block >> 3]
        acc_ref[row] = acc_ref[row] + (product[0:K] + quotient * product[K:])
        scaled_ref[row] = scaled_ref[row] + product[K:]

    work(count_ref[1], count_ref[2], list_ref, coupling_ref, held, sems, multiply, add)
    wait_all(late)
    for block in range(RB):
        at = columns(block)
        degree = degree_ref[block : block + 1, :]
        residual = (stacked_image[0:16, at] - theta * stacked[0:16, at]) / degree
        stacked[16:32, at] = residual
        stacked_image[16:32, at] = degree * residual - (acc_ref[block] - theta * scaled_ref[block])
    gram_b = dot_nt(stacked[...], stacked[...], HIGHEST)
    gram_a = dot_nt(stacked[...], stacked_image[...], HIGHEST)
    packed = pack_grams(gram_b, gram_a, wide_ref)
    for peer in range(packed_ref.shape[0]):
        packed_ref[peer] = packed


def make_grams(
    halo_list, counts, halo_tiles, basis_halo, coupling, own, scaled, basis, image, degree, previous, previous_image, n_dom
):
    stack = shaped((3 * K, basis.shape[1]), F32)
    return call(
        gram_kernel,
        (stack, stack, shaped((n_dom, 24, BS), F32)),
        [SMEM, SMEM, VMEM] + [HBM] * 9,
        (VMEM, VMEM, VMEM),
        (
            pltpu.VMEM(basis_halo.shape, BF16),
            pltpu.VMEM((RB + 1, K, BS), F32),
            pltpu.VMEM((RB + 1, K, BS), F32),
            pltpu.VMEM(degree.shape, F32),
            pltpu.SemaphoreType.DMA((8,)),
        )
        + HELD
        + (
            pltpu.VMEM((n_dom * K, BS), BF16),
            pltpu.VMEM((SEND, n_dom, K, BS), F32),
            pltpu.VMEM((n_dom * SEND, BS), F32),
            pltpu.VMEM((BS, BS), F32),
        ),
        flops=2 * SLOTS * K * BS * BS,
        moved=10000000,
    )(
        halo_list, counts, halo_tiles,
        *map(in_hbm, (basis_halo, coupling, own, scaled, basis, image, degree, previous, previous_image)),
    )


def inverse_factor(gram, n):
    row = iota2((n, BS), 0)
    lane = iota2((n, BS), 1)
    work = jnp.where(lane < n, gram, jnp.where(lane == row + n, 1.0, 0.0))
    for first in range(0, n, 8):
        left = [jnp.broadcast_to(work[:, first + j : first + j + 1], (n, BS)) for j in range(8)]
        rows = [work[first + j : first + j + 1, :] for j in range(8)]
        for j in range(8):
            scale = lax.rsqrt(left[j][first + j : first + j + 1, :])
            rows[j] = rows[j] * scale
            left[j] = jnp.where(row > first + j, left[j] * scale, 0.0)
            for k in range(j + 1, 8):
                entry = left[j][first + k : first + k + 1, :]
                rows[k] = rows[k] - entry * rows[j]
                left[k] = left[k] - left[j] * entry
        for j in range(8):
            work = jnp.where(row == first + j, rows[j], work - left[j] * rows[j])
    return pltpu.roll(work, BS - n, 1)


def final_kernel(
    root_rows, taken_ref, stacked_ref, stacked_image_ref, new_basis_ref, new_image_ref, wide_ref
):
    packed = taken_ref[0]
    for peer in range(1, taken_ref.shape[0]):
        packed = packed + taken_ref[peer]
    gram_b, gram_a = unpack_grams(packed, wide_ref)
    inverse = inverse_factor(gram_b, 48)[:, 0:48]
    symmetric = gram_a[:, 0:48]
    reduced = dot_nt(dot_nn(inverse, symmetric, HIGHEST), inverse, HIGHEST)
    wide = square(reduced, wide_ref)
    reduced = 0.5 * (wide + wide.T)[0:48, 0:48]
    spread = jnp.max(jnp.sum(jnp.abs(reduced), axis=1, keepdims=True), axis=0, keepdims=True)
    row = iota2((48, 48), 0)
    lane = iota2((48, 48), 1)
    filter_mat = (jnp.where(row == lane, spread, 0.0) - reduced) / (2.0 * spread)
    turned = filter_mat[0:16, :]
    for repeat in range(3):
        turned = dot_nn(turned, filter_mat, HIGHEST)
    inner = dot_nt(turned, turned, HIGHEST)
    wide_ref[...] = jnp.zeros_like(wide_ref)
    wide_ref[0:16, 0:16] = inner
    sub_inverse = inverse_factor(wide_ref[0:16, :], 16)[:, 0:16]
    coeff = dot_nn(dot_nn(sub_inverse, turned, HIGHEST), inverse, HIGHEST) * root_rows
    new_basis_ref[...] = dot_nn(coeff, stacked_ref[...], HIGHEST)
    new_image_ref[...] = dot_nn(coeff, stacked_image_ref[...], HIGHEST)


def finish(root_rows, packed, stacked, stacked_image):
    shape = (K, stacked.shape[1])
    return call(
        functools.partial(final_kernel, root_rows),
        (shaped(shape, F32), shaped(shape, F32)),
        [VMEM] * 3,
        (VMEM, VMEM),
        (pltpu.VMEM((BS, BS), F32),),
        flops=1000000,
        moved=3000000,
    )(packed, stacked, stacked_image)


def to_all(value, axis):
    return lax.all_to_all(value, axis, split_axis=0, concat_axis=0, tiled=True)


def body(
    n_dom, n_row,
    basis, previous, previous_image, degree, coupling, slot_row, slot_column, send_lists, live_slots,
):
    part = n_row * RB
    place = lax.axis_index("row").astype(jnp.int32).reshape(1)
    send_list = send_lists.reshape(n_dom * SEND)
    degree = degree.reshape(RB, BS)
    own_list, halo_list, counts = make_lists(slot_row, slot_column, live_slots, part)

    gathered = gather_row(cast_tiles(in_hbm(basis), in_hbm(degree)), n_row, HALF + 2)
    basis_part, inverse, chosen = first_select(gathered, place, send_list, n_row)
    halo_tiles = to_all(chosen, "dom")
    own = first_own(own_list, counts, basis_part, coupling)
    image, tiles, basis_halo = make_image(halo_list, counts, halo_tiles, coupling, own, basis, degree)

    gathered = gather_row(tiles, n_row, HALF)
    part_tiles, chosen, table = second_select(gathered, place, send_list, picks(send_list), n_row)
    halo_tiles = to_all(chosen, "dom")
    own, scaled = second_own(own_list, counts, part_tiles, table, basis_part, inverse, coupling, n_row)
    stacked, stacked_image, packed = make_grams(
        halo_list, counts, halo_tiles, basis_halo, coupling, own, scaled, basis, image, degree, previous, previous_image,
        n_dom,
    )
    packed = to_all(add_and_repeat(to_all(packed, "dom"), n_row), "row")
    root_rows = math.sqrt(basis.shape[1] * n_dom * n_row)
    return finish(root_rows, packed, stacked, stacked_image)


def solution(mesh):
    split = P(None, ("dom", "row"))
    flat = P(("dom", "row"))
    return jax.shard_map(
        functools.partial(body, mesh.shape["dom"], mesh.shape["row"]),
        mesh=mesh,
        in_specs=(
            split, split, split, flat, P(("dom", "row"), None, None), flat, flat, P("dom", None, None), flat,
        ),
        out_specs=(split, split),
        check_vma=False,
    )
```

```python
import functools
import math

import jax
import jax.numpy as jnp
from jax import lax
from jax.experimental import pallas as pl
from jax.experimental.pallas import tpu as pltpu
from jax.sharding import PartitionSpec as P

K = 16
BS = 128
RB = 32
SLOTS = 256
SEND = 8
HALF = RB // 2
EXTRA = SEND + 1
CHUNK = 32
GROUP = 32
LEN = SLOTS + GROUP
F32 = jnp.float32
BF16 = jnp.bfloat16
HIGHEST = lax.Precision.HIGHEST
MARGIN = 6 * 1024 * 1024
SMEM = pl.BlockSpec(memory_space=pltpu.SMEM)
HBM = pl.BlockSpec(memory_space=pl.ANY)
VMEM = pl.BlockSpec(memory_space=pltpu.VMEM)


def size(array):
    return math.prod(array.shape) * jnp.dtype(array.dtype).itemsize


def call(kernel, out_shape, in_specs, out_specs, scratch=(), flops=0, moved=0):
    def run(*args):
        arrays = list(args) + jax.tree.leaves(out_shape) + [held for held in scratch if jnp.issubdtype(held.dtype, jnp.floating)]
        return pl.pallas_call(
            kernel,
            out_shape=out_shape,
            in_specs=in_specs,
            out_specs=out_specs,
            scratch_shapes=scratch,
            compiler_params=pltpu.CompilerParams(vmem_limit_bytes=MARGIN + sum(map(size, arrays))),
            cost_estimate=pl.CostEstimate(flops=flops, bytes_accessed=moved, transcendentals=0),
        )(*args)

    return run


def shaped(shape, dtype):
    return jax.ShapeDtypeStruct(shape, dtype)


def in_hbm(value):
    return pltpu.with_memory_space_constraint(value, pltpu.HBM)


def start_copies(pairs, sems, first=0):
    copies = [pltpu.make_async_copy(source, target, sems.at[first + i]) for i, (source, target) in enumerate(pairs)]
    for copy in copies:
        copy.start()
    return copies


def wait_all(copies):
    for copy in copies:
        copy.wait()


def dot_nt(left, right, precision=None):
    return lax.dot_general(
        left, right, (((1,), (1,)), ((), ())), precision=precision, preferred_element_type=F32
    )


def dot_nn(left, right, precision=None):
    return lax.dot_general(
        left, right, (((1,), (0,)), ((), ())), precision=precision, preferred_element_type=F32
    )


def columns(block):
    return slice(block * BS, (block + 1) * BS)


def iota2(shape, axis):
    return lax.broadcasted_iota(jnp.int32, shape, axis)


def list_kernel(part, row_ref, column_ref, live_ref, own_ref, halo_ref, count_ref):
    live = live_ref[0]

    def step(quad, counts):
        n_own, n_halo = counts
        for j in range(4):
            slot = quad * 4 + j
            column = column_ref[slot]
            entry = slot + (row_ref[slot] << 16)
            own_ref[n_own] = entry + (column << 8)
            halo_ref[n_halo] = entry + ((column - part) << 8)
            used = slot < live
            is_own = used & (column < part)
            is_halo = used & (column >= part)
            n_own = n_own + is_own.astype(jnp.int32)
            n_halo = n_halo + is_halo.astype(jnp.int32)
        return n_own, n_halo

    n_own, n_halo = lax.fori_loop(0, lax.div(live + 3, 4), step, (jnp.int32(0), jnp.int32(0)))
    for ref, count in ((own_ref, n_own), (halo_ref, n_halo)):
        for extra in range(GROUP):
            ref[count + extra] = RB << 16
    count_ref[0] = n_own
    count_ref[1] = n_halo
    count_ref[2] = live


def make_lists(slot_row, slot_column, live_slots, part):
    return call(
        functools.partial(list_kernel, part),
        (shaped((LEN,), jnp.int32), shaped((LEN,), jnp.int32), shaped((3,), jnp.int32)),
        [SMEM, SMEM, SMEM],
        (SMEM, SMEM, SMEM),
        moved=20000,
    )(slot_row, slot_column, live_slots)


def split3(value):
    high = value.astype(BF16).astype(F32)
    rest = value - high
    middle = rest.astype(BF16).astype(F32)
    return high, middle, (rest - middle).astype(BF16).astype(F32)


def cast_kernel(field_hbm, degree_hbm, tiles_ref, field_ref, degree_ref, sems):
    wait_all(start_copies([(field_hbm, field_ref), (degree_hbm, degree_ref)], sems))
    for block in range(RB):
        tiles_ref[block + 2 * (block // HALF)] = field_ref[:, columns(block)].astype(BF16)
    for half in range(2):
        inverse = 1.0 / degree_ref[half * HALF : (half + 1) * HALF]
        high = inverse.astype(BF16)
        at = half * (HALF + 2) + HALF
        tiles_ref[at] = high
        tiles_ref[at + 1] = (inverse - high.astype(F32)).astype(BF16)


def cast_tiles(field, degree):
    return call(
        cast_kernel,
        shaped((RB + 4, K, BS), BF16),
        [HBM, HBM],
        VMEM,
        (pltpu.VMEM(field.shape, F32), pltpu.VMEM(degree.shape, F32), pltpu.SemaphoreType.DMA((2,))),
        moved=400000,
    )(field, degree)


def gather_row(tiles, n_row, half):
    up = [(i, (i + 1) % n_row) for i in range(n_row)]
    down = [(i, (i - 1) % n_row) for i in range(n_row)]
    pieces = [(0, tiles)]
    from_below = from_above = tiles
    for step in range(1, n_row // 2):
        from_below = lax.ppermute(from_below, "row", up)
        from_above = lax.ppermute(from_above, "row", down)
        pieces += [(-step, from_below), (step, from_above)]
    far_low = lax.ppermute(from_below[:half], "row", up)
    far_high = lax.ppermute(from_above[half:], "row", down)
    return pieces, far_low, far_high


def halves(offsets, pieces, half, n_row, place):
    parts = []
    for offset, piece in zip(offsets, pieces):
        owner = lax.rem(place + offset + n_row, n_row)
        parts += [(owner, 0, piece, 0), (owner, 1, piece, half)]
    owner = lax.rem(place + n_row // 2, n_row)
    return parts + [(owner, 0, pieces[-2], 0), (owner, 1, pieces[-1], 0)]


def fill_and_send(fill, chosen_ref, chosen_hbm, sems):
    peers = chosen_ref.shape[0] // EXTRA
    quarter = max(1, peers // 4)
    copies = []
    for at in range(peers // quarter):

        def step(peer, carry):
            fill(peer)
            return carry

        lax.fori_loop(at * quarter, (at + 1) * quarter, step, 0)
        span = pl.ds(at * quarter * EXTRA, quarter * EXTRA)
        copies.append(pltpu.make_async_copy(chosen_ref.at[span], chosen_hbm.at[span], sems.at[at]))
        copies[-1].start()
    for copy in copies:
        copy.wait()


def first_select_kernel(offsets, n_row, place_ref, send_ref, *refs):
    pieces, (part_hbm, inverse_hbm, chosen_hbm) = refs[:-8], refs[-8:-5]
    part_ref, inverse_ref, rows_ref, chosen_ref, sems = refs[-5:]
    for owner, half, piece, start in halves(offsets, pieces, HALF + 2, n_row, place_ref[0]):
        at = owner * RB + half * HALF
        part_ref[pl.ds(at, HALF)] = piece[start : start + HALF]
        inverse_ref[pl.ds(pl.multiple_of(at, HALF), HALF), :] = (
            piece[start + HALF].astype(F32) + piece[start + HALF + 1].astype(F32)
        )

    copies = start_copies([(part_ref, part_hbm), (inverse_ref, inverse_hbm)], sems, 4)

    def fill(peer):
        for j in range(SEND):
            block = send_ref[peer * SEND + j]
            chosen_ref[peer * EXTRA + j] = part_ref[block]
            rows_ref[j : j + 1, :] = inverse_ref[pl.ds(block, 1), :]
        rows = rows_ref[...]
        high = rows.astype(BF16).astype(F32)
        chosen_ref[peer * EXTRA + SEND] = jnp.concatenate([high, rows - high], axis=0).astype(BF16)

    fill_and_send(fill, chosen_ref, chosen_hbm, sems)
    wait_all(copies)


def first_select(gathered, place, send_list, n_row):
    pieces, far_low, far_high = gathered
    part = n_row * RB
    peers = send_list.shape[0] // SEND
    return call(
        functools.partial(first_select_kernel, [offset for offset, _ in pieces], n_row),
        (pltpu.HBM((part, K, BS), BF16), pltpu.HBM((part, BS), F32), pltpu.HBM((peers * EXTRA, K, BS), BF16)),
        [SMEM, SMEM] + [VMEM] * (len(pieces) + 2),
        (HBM, HBM, HBM),
        (
            pltpu.VMEM((part, K, BS), BF16),
            pltpu.VMEM((part, BS), F32),
            pltpu.VMEM((SEND, BS), F32),
            pltpu.VMEM((peers * EXTRA, K, BS), BF16),
            pltpu.SemaphoreType.DMA((6,)),
        ),
        moved=3000000,
    )(place, send_list, *[piece for _, piece in pieces], far_low, far_high)


def second_select_kernel(offsets, n_row, place_ref, send_ref, pick_ref, *refs):
    pieces, (part_hbm, chosen_hbm, table_hbm, part_ref, chosen_ref, table_ref, sems) = refs[:-7], refs[-7:]
    lane = iota2((K, BS), 1)
    table = jnp.zeros((K, BS), F32)
    side_sum = jnp.zeros((K, BS), F32)
    for owner, half, piece, start in halves(offsets, pieces, HALF, n_row, place_ref[0]):
        part_ref[pl.ds(owner * RB + half * HALF, HALF)] = piece[start : start + HALF]
        if half == 1:
            side = piece[start + HALF].astype(F32)
            table = jnp.where(lane == owner, side[:, 0:1], table)
            side_sum = side_sum + side
    top = jnp.sum(jnp.where((lane >= 1) & (lane <= 3), side_sum, 0.0), axis=1, keepdims=True)
    bottom = jnp.sum(jnp.where((lane >= 4) & (lane <= 6), side_sum, 0.0), axis=1, keepdims=True)
    for at, value in enumerate(split3(top) + split3(bottom)):
        table = jnp.where(lane == 8 + at, value, table)
    table = table.astype(BF16)
    table_ref[...] = table
    copies = start_copies([(part_ref, part_hbm), (table_ref, table_hbm)], sems, 4)
    sides = dot_nn(table, pick_ref[...])
    for peer in range(chosen_ref.shape[0] // EXTRA):
        chosen_ref[peer * EXTRA + SEND] = sides[:, columns(peer)].astype(BF16)

    def fill(peer):
        for j in range(SEND):
            chosen_ref[peer * EXTRA + j] = part_ref[send_ref[peer * SEND + j]]

    fill_and_send(fill, chosen_ref, chosen_hbm, sems)
    wait_all(copies)


def second_select(gathered, place, send_list, pick, n_row):
    pieces, far_low, far_high = gathered
    peers = send_list.shape[0] // SEND
    return call(
        functools.partial(second_select_kernel, [offset for offset, _ in pieces], n_row),
        (pltpu.HBM((n_row * RB, K, BS), BF16), pltpu.HBM((peers * EXTRA, K, BS), BF16), pltpu.HBM((K, BS), BF16)),
        [SMEM, SMEM] + [VMEM] * (len(pieces) + 3),
        (HBM, HBM, HBM),
        (
            pltpu.VMEM((n_row * RB, K, BS), BF16),
            pltpu.VMEM((peers * EXTRA, K, BS), BF16),
            pltpu.VMEM((K, BS), BF16),
            pltpu.SemaphoreType.DMA((6,)),
        ),
        moved=3000000,
    )(place, send_list, pick, *[piece for _, piece in pieces], far_low, far_high)


def picks(send_list):
    peers = send_list.shape[0] // SEND
    owner = (send_list >> 5).reshape(peers, SEND)
    lane = jnp.broadcast_to(jnp.arange(BS, dtype=jnp.int32)[None, :], (peers, BS))
    target = jnp.where(lane < 14, lane, -1)
    target = jnp.concatenate([owner, target[:, SEND:]], axis=1).reshape(-1)
    return (jnp.arange(BS, dtype=jnp.int32)[:, None] == target[None, :]).astype(BF16)


def work(count, list_ref, weights_ref, load, add):
    def step(group, carry):
        base = group * GROUP
        entries = [list_ref[base + j] for j in range(GROUP)]
        products = []
        for one, two in zip(entries[0::2], entries[1::2]):
            left = [load((entry >> 8) & 255) for entry in (one, two)]
            right = [weights_ref[entry & 255] for entry in (one, two)]
            product = dot_nn(jnp.concatenate(left, axis=0), jnp.concatenate(right, axis=1))
            rows = left[0].shape[0]
            products += [product[:rows, :BS], product[rows:, BS:]]
        for entry, product in zip(entries, products):
            add(entry >> 16, (entry >> 8) & 255, product)
        return carry

    lax.fori_loop(0, lax.div(count + GROUP - 1, GROUP), step, 0)


ROWS = shaped((RB + 1, K, BS), F32)


def scale_block(block, inverse):
    return (block.astype(F32) * inverse).astype(BF16)


def first_own_kernel(list_ref, count_ref, part_ref, coupling_ref, acc_ref, weights_ref, held, sems):
    chunks = lax.div(count_ref[2] + CHUNK - 1, CHUNK)

    def copy_of(chunk):
        span = pl.ds(chunk * CHUNK, CHUNK)
        return pltpu.make_async_copy(coupling_ref.at[span], held.at[span], sems.at[chunk])

    def start(chunk, carry):
        copy_of(chunk).start()
        return carry

    def turn(chunk, carry):
        copy_of(chunk).wait()
        for j in range(CHUNK):
            weights_ref[chunk * CHUNK + j] = held[chunk * CHUNK + j].T
        return carry

    lax.fori_loop(0, chunks, start, 0)
    lax.fori_loop(0, chunks, turn, 0)
    acc_ref[...] = jnp.zeros_like(acc_ref)

    def load(block):
        return part_ref[block]

    def add(row, block, product):
        acc_ref[row] = acc_ref[row] + product

    work(count_ref[0], list_ref, weights_ref, load, add)


def first_own(own_list, counts, part_tiles, coupling):
    return call(
        first_own_kernel,
        (ROWS, pltpu.VMEM((SLOTS, BS, BS), BF16)),
        [SMEM, SMEM, VMEM, HBM],
        (VMEM, VMEM),
        (pltpu.VMEM((SLOTS, BS, BS), BF16), pltpu.SemaphoreType.DMA((SLOTS // CHUNK,))),
        flops=2 * SLOTS * K * BS * BS,
        moved=10000000,
    )(own_list, counts, in_hbm(part_tiles), in_hbm(coupling))


def image_kernel(
    list_ref, count_ref, halo_ref, weights_ref, own_ref, basis_ref, degree_ref, image_hbm, tiles_ref, halo_hbm, image_ref,
    out_sems, acc_ref,
):
    copies = start_copies([(halo_ref, halo_hbm)], out_sems)
    acc_ref[...] = own_ref[...]

    def load(block):
        return halo_ref[block + (block >> 3)]

    def add(row, block, product):
        acc_ref[row] = acc_ref[row] + product

    work(count_ref[1], list_ref, weights_ref, load, add)
    top = jnp.zeros((K, BS), F32)
    bottom = jnp.zeros((K, BS), F32)
    for block in range(RB):
        at = columns(block)
        basis = basis_ref[:, at]
        image = degree_ref[block : block + 1, :] * basis - acc_ref[block]
        image_ref[:, at] = image
        top = top + basis * image
        bottom = bottom + basis * basis
    copies += start_copies([(image_ref, image_hbm)], out_sems, 1)
    top = jnp.sum(top, axis=1, keepdims=True)
    bottom = jnp.sum(bottom, axis=1, keepdims=True)
    usable = bottom > 1e-30
    quotient = jnp.where(usable, top / jnp.where(usable, bottom, 1.0), 0.0).astype(BF16).astype(F32)
    for block in range(RB):
        at = columns(block)
        residual = (image_ref[:, at] - quotient * basis_ref[:, at]) / degree_ref[block : block + 1, :]
        tiles_ref[block] = residual.astype(BF16)
    lane = iota2((K, BS), 1)
    side = jnp.where(lane == 0, quotient, 0.0)
    for at, value in enumerate(split3(top) + split3(bottom)):
        side = jnp.where(lane == 1 + at, value, side)
    tiles_ref[RB] = side.astype(BF16)
    wait_all(copies)


def make_image(halo_list, counts, halo_tiles, weights, own, basis, degree):
    return call(
        image_kernel,
        (pltpu.HBM(basis.shape, F32), shaped((RB + 1, K, BS), BF16), pltpu.HBM(halo_tiles.shape, BF16)),
        [SMEM, SMEM, VMEM, VMEM, VMEM, VMEM, VMEM],
        (HBM, VMEM, HBM),
        (pltpu.VMEM(basis.shape, F32), pltpu.SemaphoreType.DMA((2,)), pltpu.VMEM((RB + 1, K, BS), F32)),
        flops=2 * SLOTS * K * BS * BS,
        moved=8000000,
    )(halo_list, counts, halo_tiles, weights, own, basis, degree)


def second_own_kernel(
    list_ref, count_ref, part_ref, table_ref, basis_part_ref, inverse_ref, weights_ref, acc_ref, scaled_ref, quotient_ref
):
    acc_ref[...] = jnp.zeros_like(acc_ref)
    scaled_ref[...] = jnp.zeros_like(scaled_ref)
    table = table_ref[...].astype(F32)
    for owner in range(quotient_ref.shape[0]):
        quotient_ref[owner] = jnp.broadcast_to(table[:, owner : owner + 1], (K, BS))

    def load(block):
        scaled = scale_block(basis_part_ref[block], inverse_ref[pl.ds(block, 1), :])
        return jnp.concatenate([part_ref[block], scaled], axis=0)

    def add(row, block, product):
        acc_ref[row] = acc_ref[row] + (product[0:K] + quotient_ref[block >> 5] * product[K:])
        scaled_ref[row] = scaled_ref[row] + product[K:]

    work(count_ref[0], list_ref, weights_ref, load, add)


def second_own(own_list, counts, part_tiles, table, basis_part, inverse, weights, n_row):
    return call(
        second_own_kernel,
        (pltpu.HBM(ROWS.shape, F32), pltpu.HBM(ROWS.shape, F32)),
        [SMEM, SMEM, VMEM, VMEM, VMEM, VMEM, VMEM],
        (VMEM, VMEM),
        (pltpu.VMEM((n_row, K, BS), F32),),
        flops=4 * SLOTS * K * BS * BS,
        moved=10000000,
    )(own_list, counts, *map(in_hbm, (part_tiles, table, basis_part, inverse)), weights)


def spread_kernel(taken_ref, given_ref):
    total = taken_ref[0]
    for peer in range(1, taken_ref.shape[0]):
        total = total + taken_ref[peer]
    for peer in range(given_ref.shape[0]):
        given_ref[peer] = total


def add_and_repeat(taken, peers):
    return call(
        spread_kernel, shaped((peers,) + taken.shape[1:], F32), [VMEM], VMEM, moved=400000
    )(taken)


def square(value, wide_ref):
    rows, cols = value.shape
    wide_ref[...] = jnp.zeros_like(wide_ref)
    wide_ref[0:rows, 0:cols] = value
    return wide_ref[...]


def pack_grams(gram_b, gram_a, wide_ref):
    wide_a = square(gram_a, wide_ref)
    both = 0.5 * (wide_a + wide_a.T)
    wide_b = square(gram_b, wide_ref)
    row = iota2((BS, BS), 0)
    lane = iota2((BS, BS), 1)
    packed = jnp.where(row <= lane, wide_b, both)
    diagonal = jnp.sum(jnp.where(row == lane, both, 0.0), axis=1, keepdims=True)
    low, high = packed[0:24], pltpu.roll(packed[24:48], 48, 1)
    at = iota2((24, BS), 1)
    out = jnp.where(at < 48, low, high)
    out = jnp.where(at == 96, diagonal[0:24], out)
    return jnp.where(at == 97, diagonal[24:48], out)


def unpack_grams(packed, wide_ref):
    wide_ref[...] = jnp.zeros_like(wide_ref)
    at = iota2((24, BS), 1)
    wide_ref[0:24] = jnp.where(at < 48, packed, 0.0)
    wide_ref[24:48] = jnp.where(at < 48, pltpu.roll(packed, 80, 1), 0.0)
    wide = wide_ref[...]
    flipped = wide.T
    row = iota2((48, BS), 0)
    lane = iota2((48, BS), 1)
    wide, flipped = wide[0:48], flipped[0:48]
    diagonal = jnp.concatenate([packed[:, 96:97], packed[:, 97:98]], axis=0)
    gram_b = jnp.where(row <= lane, wide, flipped)
    gram_a = jnp.where(row == lane, diagonal, jnp.where(row > lane, wide, flipped))
    return gram_b, gram_a


def gram_kernel(
    list_ref, count_ref, halo_ref, weights_ref, basis_halo_hbm, own_hbm, own_scaled_hbm, basis_hbm, image_hbm, degree_hbm,
    previous_hbm, previous_image_hbm, stacked, stacked_image, packed_ref, basis_halo_ref, acc_ref, scaled_ref, degree_ref,
    in_sems, side_ref, quotient_ref, inverse_ref, wide_ref,
):
    early = [(basis_halo_hbm, basis_halo_ref), (own_hbm, acc_ref), (own_scaled_hbm, scaled_ref)]
    late = [
        (basis_hbm, stacked.at[0:16]),
        (previous_hbm, stacked.at[32:48]),
        (image_hbm, stacked_image.at[0:16]),
        (previous_image_hbm, stacked_image.at[32:48]),
        (degree_hbm, degree_ref),
    ]
    early = start_copies(early, in_sems)
    late = start_copies(late, in_sems, 3)
    peers = halo_ref.shape[0] // EXTRA
    total = jnp.zeros((K, BS), F32)
    for peer in range(peers):
        side = halo_ref[peer * EXTRA + SEND]
        side_ref[peer * K : (peer + 1) * K, :] = side
        total = total + side.astype(F32)
    side = side_ref[...]
    for j in range(SEND):
        spread = (iota2((BS, BS), 0) == j).astype(F32).astype(BF16)
        quotient_ref[j] = dot_nn(side, spread).reshape(peers, K, BS)
    lane = iota2((K, BS), 1)
    top = jnp.sum(jnp.where((lane >= 8) & (lane <= 10), total, 0.0), axis=1, keepdims=True)
    bottom = jnp.sum(jnp.where((lane >= 11) & (lane <= 13), total, 0.0), axis=1, keepdims=True)
    theta = top / bottom
    wait_all(early)
    for peer in range(peers):
        inverse = basis_halo_ref[peer * EXTRA + SEND].astype(F32)
        inverse_ref[peer * SEND : (peer + 1) * SEND, :] = inverse[0:SEND] + inverse[SEND:]

    def load(block):
        tile = block + (block >> 3)
        scaled = scale_block(basis_halo_ref[tile], inverse_ref[pl.ds(block, 1), :])
        return jnp.concatenate([halo_ref[tile], scaled], axis=0)

    def add(row, block, product):
        quotient = quotient_ref[block & 7, block >> 3]
        acc_ref[row] = acc_ref[row] + (product[0:K] + quotient * product[K:])
        scaled_ref[row] = scaled_ref[row] + product[K:]

    work(count_ref[1], list_ref, weights_ref, load, add)
    wait_all(late)
    for block in range(RB):
        at = columns(block)
        degree = degree_ref[block : block + 1, :]
        residual = (stacked_image[0:16, at] - theta * stacked[0:16, at]) / degree
        stacked[16:32, at] = residual
        stacked_image[16:32, at] = degree * residual - (acc_ref[block] - theta * scaled_ref[block])
    gram_b = dot_nt(stacked[...], stacked[...], HIGHEST)
    gram_a = dot_nt(stacked[...], stacked_image[...], HIGHEST)
    packed = pack_grams(gram_b, gram_a, wide_ref)
    for peer in range(packed_ref.shape[0]):
        packed_ref[peer] = packed


def make_grams(
    halo_list, counts, halo_tiles, weights, basis_halo, own, scaled, basis, image, degree, previous, previous_image, n_dom
):
    stack = shaped((3 * K, basis.shape[1]), F32)
    return call(
        gram_kernel,
        (stack, stack, shaped((n_dom, 24, BS), F32)),
        [SMEM, SMEM, VMEM, VMEM] + [HBM] * 8,
        (VMEM, VMEM, VMEM),
        (
            pltpu.VMEM(basis_halo.shape, BF16),
            pltpu.VMEM((RB + 1, K, BS), F32),
            pltpu.VMEM((RB + 1, K, BS), F32),
            pltpu.VMEM(degree.shape, F32),
            pltpu.SemaphoreType.DMA((8,)),
            pltpu.VMEM((n_dom * K, BS), BF16),
            pltpu.VMEM((SEND, n_dom, K, BS), F32),
            pltpu.VMEM((n_dom * SEND, BS), F32),
            pltpu.VMEM((BS, BS), F32),
        ),
        flops=2 * SLOTS * K * BS * BS,
        moved=10000000,
    )(
        halo_list, counts, halo_tiles, weights,
        *map(in_hbm, (basis_halo, own, scaled, basis, image, degree, previous, previous_image)),
    )


def inverse_factor(gram, n):
    row = iota2((n, BS), 0)
    lane = iota2((n, BS), 1)
    work = jnp.where(lane < n, gram, jnp.where(lane == row + n, 1.0, 0.0))
    for first in range(0, n, 8):
        left = [jnp.broadcast_to(work[:, first + j : first + j + 1], (n, BS)) for j in range(8)]
        rows = [work[first + j : first + j + 1, :] for j in range(8)]
        for j in range(8):
            scale = lax.rsqrt(left[j][first + j : first + j + 1, :])
            rows[j] = rows[j] * scale
            left[j] = jnp.where(row > first + j, left[j] * scale, 0.0)
            for k in range(j + 1, 8):
                entry = left[j][first + k : first + k + 1, :]
                rows[k] = rows[k] - entry * rows[j]
                left[k] = left[k] - left[j] * entry
        for j in range(8):
            work = jnp.where(row == first + j, rows[j], work - left[j] * rows[j])
    return pltpu.roll(work, BS - n, 1)


def final_kernel(
    root_rows, taken_ref, stacked_ref, stacked_image_ref, new_basis_ref, new_image_ref, wide_ref
):
    packed = taken_ref[0]
    for peer in range(1, taken_ref.shape[0]):
        packed = packed + taken_ref[peer]
    gram_b, gram_a = unpack_grams(packed, wide_ref)
    inverse = inverse_factor(gram_b, 48)[:, 0:48]
    symmetric = gram_a[:, 0:48]
    reduced = dot_nt(dot_nn(inverse, symmetric, HIGHEST), inverse, HIGHEST)
    wide = square(reduced, wide_ref)
    reduced = 0.5 * (wide + wide.T)[0:48, 0:48]
    spread = jnp.max(jnp.sum(jnp.abs(reduced), axis=1, keepdims=True), axis=0, keepdims=True)
    row = iota2((48, 48), 0)
    lane = iota2((48, 48), 1)
    filter_mat = (jnp.where(row == lane, spread, 0.0) - reduced) / (2.0 * spread)
    turned = filter_mat[0:16, :]
    for repeat in range(3):
        turned = dot_nn(turned, filter_mat, HIGHEST)
    inner = dot_nt(turned, turned, HIGHEST)
    wide_ref[...] = jnp.zeros_like(wide_ref)
    wide_ref[0:16, 0:16] = inner
    sub_inverse = inverse_factor(wide_ref[0:16, :], 16)[:, 0:16]
    coeff = dot_nn(dot_nn(sub_inverse, turned, HIGHEST), inverse, HIGHEST) * root_rows
    new_basis_ref[...] = dot_nn(coeff, stacked_ref[...], HIGHEST)
    new_image_ref[...] = dot_nn(coeff, stacked_image_ref[...], HIGHEST)


def finish(root_rows, packed, stacked, stacked_image):
    shape = (K, stacked.shape[1])
    return call(
        functools.partial(final_kernel, root_rows),
        (shaped(shape, F32), shaped(shape, F32)),
        [VMEM] * 3,
        (VMEM, VMEM),
        (pltpu.VMEM((BS, BS), F32),),
        flops=1000000,
        moved=3000000,
    )(packed, stacked, stacked_image)


def to_all(value, axis):
    return lax.all_to_all(value, axis, split_axis=0, concat_axis=0, tiled=True)


def body(
    n_dom, n_row,
    basis, previous, previous_image, degree, coupling, slot_row, slot_column, send_lists, live_slots,
):
    part = n_row * RB
    place = lax.axis_index("row").astype(jnp.int32).reshape(1)
    send_list = send_lists.reshape(n_dom * SEND)
    degree = degree.reshape(RB, BS)
    own_list, halo_list, counts = make_lists(slot_row, slot_column, live_slots, part)

    gathered = gather_row(cast_tiles(in_hbm(basis), in_hbm(degree)), n_row, HALF + 2)
    basis_part, inverse, chosen = first_select(gathered, place, send_list, n_row)
    halo_tiles = to_all(chosen, "dom")
    own, weights = first_own(own_list, counts, basis_part, coupling)
    image, tiles, basis_halo = make_image(halo_list, counts, halo_tiles, weights, own, basis, degree)

    gathered = gather_row(tiles, n_row, HALF)
    part_tiles, chosen, table = second_select(gathered, place, send_list, picks(send_list), n_row)
    halo_tiles = to_all(chosen, "dom")
    own, scaled = second_own(own_list, counts, part_tiles, table, basis_part, inverse, weights, n_row)
    stacked, stacked_image, packed = make_grams(
        halo_list, counts, halo_tiles, weights, basis_halo, own, scaled, basis, image, degree, previous, previous_image,
        n_dom,
    )
    packed = to_all(add_and_repeat(to_all(packed, "dom"), n_row), "row")
    root_rows = math.sqrt(basis.shape[1] * n_dom * n_row)
    return finish(root_rows, packed, stacked, stacked_image)


def solution(mesh):
    split = P(None, ("dom", "row"))
    flat = P(("dom", "row"))
    return jax.shard_map(
        functools.partial(body, mesh.shape["dom"], mesh.shape["row"]),
        mesh=mesh,
        in_specs=(
            split, split, split, flat, P(("dom", "row"), None, None), flat, flat, P("dom", None, None), flat,
        ),
        out_specs=(split, split),
        check_vma=False,
    )
```

```python
import functools
import math

import jax
import jax.numpy as jnp
from jax import lax
from jax.experimental import pallas as pl
from jax.experimental.pallas import tpu as pltpu
from jax.sharding import PartitionSpec as P

K = 16
BS = 128
RB = 32
SLOTS = 256
SEND = 8
HALF = RB // 2
EXTRA = SEND + 1
GROUP = 32
LEN = SLOTS + GROUP
F32 = jnp.float32
BF16 = jnp.bfloat16
HIGHEST = lax.Precision.HIGHEST
MARGIN = 6 * 1024 * 1024
SMEM = pl.BlockSpec(memory_space=pltpu.SMEM)
HBM = pl.BlockSpec(memory_space=pl.ANY)
VMEM = pl.BlockSpec(memory_space=pltpu.VMEM)


def size(array):
    return math.prod(array.shape) * jnp.dtype(array.dtype).itemsize


def call(kernel, out_shape, in_specs, out_specs, scratch=(), flops=0, moved=0):
    def run(*args):
        arrays = list(args) + jax.tree.leaves(out_shape) + [held for held in scratch if jnp.issubdtype(held.dtype, jnp.floating)]
        return pl.pallas_call(
            kernel,
            out_shape=out_shape,
            in_specs=in_specs,
            out_specs=out_specs,
            scratch_shapes=scratch,
            compiler_params=pltpu.CompilerParams(vmem_limit_bytes=MARGIN + sum(map(size, arrays))),
            cost_estimate=pl.CostEstimate(flops=flops, bytes_accessed=moved, transcendentals=0),
        )(*args)

    return run


def shaped(shape, dtype):
    return jax.ShapeDtypeStruct(shape, dtype)


def in_hbm(value):
    return pltpu.with_memory_space_constraint(value, pltpu.HBM)


def start_copies(pairs, sems, first=0):
    copies = [pltpu.make_async_copy(source, target, sems.at[first + i]) for i, (source, target) in enumerate(pairs)]
    for copy in copies:
        copy.start()
    return copies


def wait_all(copies):
    for copy in copies:
        copy.wait()


def dot_nt(left, right, precision=None):
    return lax.dot_general(
        left, right, (((1,), (1,)), ((), ())), precision=precision, preferred_element_type=F32
    )


def dot_nn(left, right, precision=None):
    return lax.dot_general(
        left, right, (((1,), (0,)), ((), ())), precision=precision, preferred_element_type=F32
    )


def columns(block):
    return slice(block * BS, (block + 1) * BS)


def iota2(shape, axis):
    return lax.broadcasted_iota(jnp.int32, shape, axis)


def list_kernel(part, row_ref, column_ref, live_ref, own_ref, halo_ref, count_ref):
    live = live_ref[0]

    def step(quad, counts):
        n_own, n_halo = counts
        for j in range(4):
            slot = quad * 4 + j
            column = column_ref[slot]
            entry = slot + (row_ref[slot] << 16)
            own_ref[n_own] = entry + (column << 8)
            halo_ref[n_halo] = entry + ((column - part) << 8)
            used = slot < live
            is_own = used & (column < part)
            is_halo = used & (column >= part)
            n_own = n_own + is_own.astype(jnp.int32)
            n_halo = n_halo + is_halo.astype(jnp.int32)
        return n_own, n_halo

    n_own, n_halo = lax.fori_loop(0, lax.div(live + 3, 4), step, (jnp.int32(0), jnp.int32(0)))
    for ref, count in ((own_ref, n_own), (halo_ref, n_halo)):
        for extra in range(GROUP):
            ref[count + extra] = RB << 16
    count_ref[0] = n_own
    count_ref[1] = n_halo
    count_ref[2] = live


def make_lists(slot_row, slot_column, live_slots, part):
    return call(
        functools.partial(list_kernel, part),
        (shaped((LEN,), jnp.int32), shaped((LEN,), jnp.int32), shaped((3,), jnp.int32)),
        [SMEM, SMEM, SMEM],
        (SMEM, SMEM, SMEM),
        moved=20000,
    )(slot_row, slot_column, live_slots)


def split3(value):
    high = value.astype(BF16).astype(F32)
    rest = value - high
    middle = rest.astype(BF16).astype(F32)
    return high, middle, (rest - middle).astype(BF16).astype(F32)


def cast_kernel(field_hbm, degree_hbm, tiles_ref, field_ref, degree_ref, sems):
    wait_all(start_copies([(field_hbm, field_ref), (degree_hbm, degree_ref)], sems))
    for block in range(RB):
        tiles_ref[block + 2 * (block // HALF)] = field_ref[:, columns(block)].astype(BF16)
    for half in range(2):
        inverse = 1.0 / degree_ref[half * HALF : (half + 1) * HALF]
        high = inverse.astype(BF16)
        at = half * (HALF + 2) + HALF
        tiles_ref[at] = high
        tiles_ref[at + 1] = (inverse - high.astype(F32)).astype(BF16)


def cast_tiles(field, degree):
    return call(
        cast_kernel,
        shaped((RB + 4, K, BS), BF16),
        [HBM, HBM],
        VMEM,
        (pltpu.VMEM(field.shape, F32), pltpu.VMEM(degree.shape, F32), pltpu.SemaphoreType.DMA((2,))),
        moved=400000,
    )(field, degree)


def gather_row(tiles, n_row, half):
    up = [(i, (i + 1) % n_row) for i in range(n_row)]
    down = [(i, (i - 1) % n_row) for i in range(n_row)]
    pieces = [(0, tiles)]
    from_below = from_above = tiles
    for step in range(1, n_row // 2):
        from_below = lax.ppermute(from_below, "row", up)
        from_above = lax.ppermute(from_above, "row", down)
        pieces += [(-step, from_below), (step, from_above)]
    far_low = lax.ppermute(from_below[:half], "row", up)
    far_high = lax.ppermute(from_above[half:], "row", down)
    return pieces, far_low, far_high


def halves(offsets, pieces, half, n_row, place):
    parts = []
    for offset, piece in zip(offsets, pieces):
        owner = lax.rem(place + offset + n_row, n_row)
        parts += [(owner, 0, piece, 0), (owner, 1, piece, half)]
    owner = lax.rem(place + n_row // 2, n_row)
    return parts + [(owner, 0, pieces[-2], 0), (owner, 1, pieces[-1], 0)]


def fill_and_send(fill, chosen_ref, chosen_hbm, sems):
    peers = chosen_ref.shape[0] // EXTRA
    quarter = max(1, peers // 4)
    copies = []
    for at in range(peers // quarter):

        def step(peer, carry):
            fill(peer)
            return carry

        lax.fori_loop(at * quarter, (at + 1) * quarter, step, 0)
        span = pl.ds(at * quarter * EXTRA, quarter * EXTRA)
        copies.append(pltpu.make_async_copy(chosen_ref.at[span], chosen_hbm.at[span], sems.at[at]))
        copies[-1].start()
    for copy in copies:
        copy.wait()


def first_select_kernel(offsets, n_row, place_ref, send_ref, *refs):
    pieces, (part_hbm, inverse_hbm, chosen_hbm) = refs[:-8], refs[-8:-5]
    part_ref, inverse_ref, rows_ref, chosen_ref, sems = refs[-5:]
    for owner, half, piece, start in halves(offsets, pieces, HALF + 2, n_row, place_ref[0]):
        at = owner * RB + half * HALF
        part_ref[pl.ds(at, HALF)] = piece[start : start + HALF]
        inverse_ref[pl.ds(pl.multiple_of(at, HALF), HALF), :] = (
            piece[start + HALF].astype(F32) + piece[start + HALF + 1].astype(F32)
        )

    copies = start_copies([(part_ref, part_hbm), (inverse_ref, inverse_hbm)], sems, 4)

    def fill(peer):
        for j in range(SEND):
            block = send_ref[peer * SEND + j]
            chosen_ref[peer * EXTRA + j] = part_ref[block]
            rows_ref[j : j + 1, :] = inverse_ref[pl.ds(block, 1), :]
        rows = rows_ref[...]
        high = rows.astype(BF16).astype(F32)
        chosen_ref[peer * EXTRA + SEND] = jnp.concatenate([high, rows - high], axis=0).astype(BF16)

    fill_and_send(fill, chosen_ref, chosen_hbm, sems)
    wait_all(copies)


def first_select(gathered, place, send_list, n_row):
    pieces, far_low, far_high = gathered
    part = n_row * RB
    peers = send_list.shape[0] // SEND
    return call(
        functools.partial(first_select_kernel, [offset for offset, _ in pieces], n_row),
        (pltpu.HBM((part, K, BS), BF16), pltpu.HBM((part, BS), F32), pltpu.HBM((peers * EXTRA, K, BS), BF16)),
        [SMEM, SMEM] + [VMEM] * (len(pieces) + 2),
        (HBM, HBM, HBM),
        (
            pltpu.VMEM((part, K, BS), BF16),
            pltpu.VMEM((part, BS), F32),
            pltpu.VMEM((SEND, BS), F32),
            pltpu.VMEM((peers * EXTRA, K, BS), BF16),
            pltpu.SemaphoreType.DMA((6,)),
        ),
        moved=3000000,
    )(place, send_list, *[piece for _, piece in pieces], far_low, far_high)


def second_select_kernel(offsets, n_row, place_ref, send_ref, pick_ref, *refs):
    pieces, (part_hbm, chosen_hbm, table_hbm, part_ref, chosen_ref, table_ref, sems) = refs[:-7], refs[-7:]
    lane = iota2((K, BS), 1)
    table = jnp.zeros((K, BS), F32)
    side_sum = jnp.zeros((K, BS), F32)
    for owner, half, piece, start in halves(offsets, pieces, HALF, n_row, place_ref[0]):
        part_ref[pl.ds(owner * RB + half * HALF, HALF)] = piece[start : start + HALF]
        if half == 1:
            side = piece[start + HALF].astype(F32)
            table = jnp.where(lane == owner, side[:, 0:1], table)
            side_sum = side_sum + side
    top = jnp.sum(jnp.where((lane >= 1) & (lane <= 3), side_sum, 0.0), axis=1, keepdims=True)
    bottom = jnp.sum(jnp.where((lane >= 4) & (lane <= 6), side_sum, 0.0), axis=1, keepdims=True)
    for at, value in enumerate(split3(top) + split3(bottom)):
        table = jnp.where(lane == 8 + at, value, table)
    table = table.astype(BF16)
    table_ref[...] = table
    copies = start_copies([(part_ref, part_hbm), (table_ref, table_hbm)], sems, 4)
    sides = dot_nn(table, pick_ref[...])
    for peer in range(chosen_ref.shape[0] // EXTRA):
        chosen_ref[peer * EXTRA + SEND] = sides[:, columns(peer)].astype(BF16)

    def fill(peer):
        for j in range(SEND):
            chosen_ref[peer * EXTRA + j] = part_ref[send_ref[peer * SEND + j]]

    fill_and_send(fill, chosen_ref, chosen_hbm, sems)
    wait_all(copies)


def second_select(gathered, place, send_list, pick, n_row):
    pieces, far_low, far_high = gathered
    peers = send_list.shape[0] // SEND
    return call(
        functools.partial(second_select_kernel, [offset for offset, _ in pieces], n_row),
        (pltpu.HBM((n_row * RB, K, BS), BF16), pltpu.HBM((peers * EXTRA, K, BS), BF16), pltpu.HBM((K, BS), BF16)),
        [SMEM, SMEM] + [VMEM] * (len(pieces) + 3),
        (HBM, HBM, HBM),
        (
            pltpu.VMEM((n_row * RB, K, BS), BF16),
            pltpu.VMEM((peers * EXTRA, K, BS), BF16),
            pltpu.VMEM((K, BS), BF16),
            pltpu.SemaphoreType.DMA((6,)),
        ),
        moved=3000000,
    )(place, send_list, pick, *[piece for _, piece in pieces], far_low, far_high)


def picks(send_list):
    peers = send_list.shape[0] // SEND
    owner = (send_list >> 5).reshape(peers, SEND)
    lane = jnp.broadcast_to(jnp.arange(BS, dtype=jnp.int32)[None, :], (peers, BS))
    target = jnp.where(lane < 14, lane, -1)
    target = jnp.concatenate([owner, target[:, SEND:]], axis=1).reshape(-1)
    return (jnp.arange(BS, dtype=jnp.int32)[:, None] == target[None, :]).astype(BF16)


def groups_of(count):
    return lax.div(count + GROUP - 1, GROUP)


def copy_group(source, target, sems, group):
    span = pl.ds(group * GROUP, GROUP)
    return pltpu.make_async_copy(source.at[span], target.at[span], sems.at[group])


def start_groups(count, source, target, sems):
    def start(group, carry):
        copy_group(source, target, sems, group).start()
        return carry

    lax.fori_loop(0, groups_of(count), start, 0)


def wait_groups(count, source, target, sems):
    def wait(group, carry):
        copy_group(source, target, sems, group).wait()
        return carry

    lax.fori_loop(0, groups_of(count), wait, 0)


def products_of(entries, weights, load):
    products = []
    for at in range(0, GROUP, 2):
        left = [load((entry >> 8) & 255) for entry in entries[at : at + 2]]
        product = dot_nn(jnp.concatenate(left, axis=0), jnp.concatenate(weights[at : at + 2], axis=1))
        rows = left[0].shape[0]
        products += [product[:rows, :BS], product[rows:, BS:]]
    return products


def work(count, list_ref, weights_hbm, held, sems, load, add):
    def step(group, carry):
        base = group * GROUP
        copy_group(weights_hbm, held, sems, group).wait()
        entries = [list_ref[base + j] for j in range(GROUP)]
        products = products_of(entries, [held[base + j] for j in range(GROUP)], load)
        for entry, product in zip(entries, products):
            add(entry >> 16, (entry >> 8) & 255, product)
        return carry

    lax.fori_loop(0, groups_of(count), step, 0)


WEIGHTS = pltpu.HBM((SLOTS, BS, BS), BF16)
HELD = pltpu.VMEM((SLOTS, BS, BS), BF16)
GROUP_SEMS = pltpu.SemaphoreType.DMA((SLOTS // GROUP,))
ROWS = shaped((RB + 1, K, BS), F32)


def scale_block(block, inverse):
    return (block.astype(F32) * inverse).astype(BF16)


def first_own_kernel(
    own_list, halo_list, count_ref, part_ref, coupling_ref, acc_ref, own_hbm, halo_hbm, held, own_held, halo_held, sems,
    own_sems, halo_sems,
):
    live = count_ref[2]
    start_groups(live, coupling_ref, held, sems)
    acc_ref[...] = jnp.zeros_like(acc_ref)
    wait_groups(live, coupling_ref, held, sems)

    def own_step(group, carry):
        base = group * GROUP
        entries = [own_list[base + j] for j in range(GROUP)]
        weights = [held[entry & 255].T for entry in entries]
        for j in range(GROUP):
            own_held[base + j] = weights[j]
        copy_group(own_held, own_hbm, own_sems, group).start()
        products = products_of(entries, weights, lambda block: part_ref[block])
        for entry, product in zip(entries, products):
            row = entry >> 16
            acc_ref[row] = acc_ref[row] + product
        return carry

    def halo_step(group, carry):
        base = group * GROUP
        for j in range(GROUP):
            halo_held[base + j] = held[halo_list[base + j] & 255].T
        copy_group(halo_held, halo_hbm, halo_sems, group).start()
        return carry

    lax.fori_loop(0, groups_of(count_ref[0]), own_step, 0)
    lax.fori_loop(0, groups_of(count_ref[1]), halo_step, 0)
    wait_groups(count_ref[0], own_held, own_hbm, own_sems)
    wait_groups(count_ref[1], halo_held, halo_hbm, halo_sems)


def first_own(own_list, halo_list, counts, part_tiles, coupling):
    return call(
        first_own_kernel,
        (pltpu.HBM(ROWS.shape, F32), WEIGHTS, WEIGHTS),
        [SMEM, SMEM, SMEM, VMEM, HBM],
        (VMEM, HBM, HBM),
        (HELD, HELD, HELD, GROUP_SEMS, GROUP_SEMS, GROUP_SEMS),
        flops=2 * SLOTS * K * BS * BS,
        moved=10000000,
    )(own_list, halo_list, counts, in_hbm(part_tiles), in_hbm(coupling))


def image_kernel(
    list_ref, count_ref, halo_ref, weights_hbm, own_hbm, basis_ref, degree_ref, image_hbm, tiles_ref, halo_hbm, image_ref,
    out_sems, acc_ref, held, sems,
):
    own = start_copies([(own_hbm, acc_ref)], out_sems, 2)
    start_groups(count_ref[1], weights_hbm, held, sems)
    copies = start_copies([(halo_ref, halo_hbm)], out_sems)
    wait_all(own)

    def load(block):
        return halo_ref[block + (block >> 3)]

    def add(row, block, product):
        acc_ref[row] = acc_ref[row] + product

    work(count_ref[1], list_ref, weights_hbm, held, sems, load, add)
    top = jnp.zeros((K, BS), F32)
    bottom = jnp.zeros((K, BS), F32)
    for block in range(RB):
        at = columns(block)
        basis = basis_ref[:, at]
        image = degree_ref[block : block + 1, :] * basis - acc_ref[block]
        image_ref[:, at] = image
        top = top + basis * image
        bottom = bottom + basis * basis
    copies += start_copies([(image_ref, image_hbm)], out_sems, 1)
    top = jnp.sum(top, axis=1, keepdims=True)
    bottom = jnp.sum(bottom, axis=1, keepdims=True)
    usable = bottom > 1e-30
    quotient = jnp.where(usable, top / jnp.where(usable, bottom, 1.0), 0.0).astype(BF16).astype(F32)
    for block in range(RB):
        at = columns(block)
        residual = (image_ref[:, at] - quotient * basis_ref[:, at]) / degree_ref[block : block + 1, :]
        tiles_ref[block] = residual.astype(BF16)
    lane = iota2((K, BS), 1)
    side = jnp.where(lane == 0, quotient, 0.0)
    for at, value in enumerate(split3(top) + split3(bottom)):
        side = jnp.where(lane == 1 + at, value, side)
    tiles_ref[RB] = side.astype(BF16)
    wait_all(copies)


def make_image(halo_list, counts, halo_tiles, weights, own, basis, degree):
    return call(
        image_kernel,
        (pltpu.HBM(basis.shape, F32), shaped((RB + 1, K, BS), BF16), pltpu.HBM(halo_tiles.shape, BF16)),
        [SMEM, SMEM, VMEM, HBM, HBM, VMEM, VMEM],
        (HBM, VMEM, HBM),
        (
            pltpu.VMEM(basis.shape, F32),
            pltpu.SemaphoreType.DMA((3,)),
            pltpu.VMEM((RB + 1, K, BS), F32),
            HELD,
            GROUP_SEMS,
        ),
        flops=2 * SLOTS * K * BS * BS,
        moved=8000000,
    )(halo_list, counts, halo_tiles, in_hbm(weights), in_hbm(own), basis, degree)


def second_own_kernel(
    list_ref, count_ref, part_ref, table_ref, basis_part_ref, inverse_ref, weights_hbm, acc_ref, scaled_ref, quotient_ref,
    held, sems,
):
    start_groups(count_ref[0], weights_hbm, held, sems)
    acc_ref[...] = jnp.zeros_like(acc_ref)
    scaled_ref[...] = jnp.zeros_like(scaled_ref)
    table = table_ref[...].astype(F32)
    for owner in range(quotient_ref.shape[0]):
        quotient_ref[owner] = jnp.broadcast_to(table[:, owner : owner + 1], (K, BS))

    def load(block):
        scaled = scale_block(basis_part_ref[block], inverse_ref[pl.ds(block, 1), :])
        return jnp.concatenate([part_ref[block], scaled], axis=0)

    def add(row, block, product):
        acc_ref[row] = acc_ref[row] + (product[0:K] + quotient_ref[block >> 5] * product[K:])
        scaled_ref[row] = scaled_ref[row] + product[K:]

    work(count_ref[0], list_ref, weights_hbm, held, sems, load, add)


def second_own(own_list, counts, part_tiles, table, basis_part, inverse, weights, n_row):
    return call(
        second_own_kernel,
        (pltpu.HBM(ROWS.shape, F32), pltpu.HBM(ROWS.shape, F32)),
        [SMEM, SMEM, VMEM, VMEM, VMEM, VMEM, HBM],
        (VMEM, VMEM),
        (pltpu.VMEM((n_row, K, BS), F32), HELD, GROUP_SEMS),
        flops=4 * SLOTS * K * BS * BS,
        moved=10000000,
    )(own_list, counts, *map(in_hbm, (part_tiles, table, basis_part, inverse, weights)))


def spread_kernel(taken_ref, given_ref):
    total = taken_ref[0]
    for peer in range(1, taken_ref.shape[0]):
        total = total + taken_ref[peer]
    for peer in range(given_ref.shape[0]):
        given_ref[peer] = total


def add_and_repeat(taken, peers):
    return call(
        spread_kernel, shaped((peers,) + taken.shape[1:], F32), [VMEM], VMEM, moved=400000
    )(taken)


def square(value, wide_ref):
    rows, cols = value.shape
    wide_ref[...] = jnp.zeros_like(wide_ref)
    wide_ref[0:rows, 0:cols] = value
    return wide_ref[...]


def pack_grams(gram_b, gram_a, wide_ref):
    wide_a = square(gram_a, wide_ref)
    both = 0.5 * (wide_a + wide_a.T)
    wide_b = square(gram_b, wide_ref)
    row = iota2((BS, BS), 0)
    lane = iota2((BS, BS), 1)
    packed = jnp.where(row <= lane, wide_b, both)
    diagonal = jnp.sum(jnp.where(row == lane, both, 0.0), axis=1, keepdims=True)
    low, high = packed[0:24], pltpu.roll(packed[24:48], 48, 1)
    at = iota2((24, BS), 1)
    out = jnp.where(at < 48, low, high)
    out = jnp.where(at == 96, diagonal[0:24], out)
    return jnp.where(at == 97, diagonal[24:48], out)


def unpack_grams(packed, wide_ref):
    wide_ref[...] = jnp.zeros_like(wide_ref)
    at = iota2((24, BS), 1)
    wide_ref[0:24] = jnp.where(at < 48, packed, 0.0)
    wide_ref[24:48] = jnp.where(at < 48, pltpu.roll(packed, 80, 1), 0.0)
    wide = wide_ref[...]
    flipped = wide.T
    row = iota2((48, BS), 0)
    lane = iota2((48, BS), 1)
    wide, flipped = wide[0:48], flipped[0:48]
    diagonal = jnp.concatenate([packed[:, 96:97], packed[:, 97:98]], axis=0)
    gram_b = jnp.where(row <= lane, wide, flipped)
    gram_a = jnp.where(row == lane, diagonal, jnp.where(row > lane, wide, flipped))
    return gram_b, gram_a


def gram_kernel(
    list_ref, count_ref, halo_ref, weights_hbm, basis_halo_hbm, own_hbm, own_scaled_hbm, basis_hbm, image_hbm, degree_hbm,
    previous_hbm, previous_image_hbm, stacked, stacked_image, packed_ref, basis_halo_ref, acc_ref, scaled_ref, degree_ref,
    in_sems, held, sems, side_ref, quotient_ref, inverse_ref, wide_ref,
):
    early = [(basis_halo_hbm, basis_halo_ref), (own_hbm, acc_ref), (own_scaled_hbm, scaled_ref)]
    late = [
        (basis_hbm, stacked.at[0:16]),
        (previous_hbm, stacked.at[32:48]),
        (image_hbm, stacked_image.at[0:16]),
        (previous_image_hbm, stacked_image.at[32:48]),
        (degree_hbm, degree_ref),
    ]
    early = start_copies(early, in_sems)
    start_groups(count_ref[1], weights_hbm, held, sems)
    late = start_copies(late, in_sems, 3)
    peers = halo_ref.shape[0] // EXTRA
    total = jnp.zeros((K, BS), F32)
    for peer in range(peers):
        side = halo_ref[peer * EXTRA + SEND]
        side_ref[peer * K : (peer + 1) * K, :] = side
        total = total + side.astype(F32)
    side = side_ref[...]
    for j in range(SEND):
        spread = (iota2((BS, BS), 0) == j).astype(F32).astype(BF16)
        quotient_ref[j] = dot_nn(side, spread).reshape(peers, K, BS)
    lane = iota2((K, BS), 1)
    top = jnp.sum(jnp.where((lane >= 8) & (lane <= 10), total, 0.0), axis=1, keepdims=True)
    bottom = jnp.sum(jnp.where((lane >= 11) & (lane <= 13), total, 0.0), axis=1, keepdims=True)
    theta = top / bottom
    wait_all(early)
    for peer in range(peers):
        inverse = basis_halo_ref[peer * EXTRA + SEND].astype(F32)
        inverse_ref[peer * SEND : (peer + 1) * SEND, :] = inverse[0:SEND] + inverse[SEND:]

    def load(block):
        tile = block + (block >> 3)
        scaled = scale_block(basis_halo_ref[tile], inverse_ref[pl.ds(block, 1), :])
        return jnp.concatenate([halo_ref[tile], scaled], axis=0)

    def add(row, block, product):
        quotient = quotient_ref[block & 7, block >> 3]
        acc_ref[row] = acc_ref[row] + (product[0:K] + quotient * product[K:])
        scaled_ref[row] = scaled_ref[row] + product[K:]

    work(count_ref[1], list_ref, weights_hbm, held, sems, load, add)
    wait_all(late)
    for block in range(RB):
        at = columns(block)
        degree = degree_ref[block : block + 1, :]
        residual = (stacked_image[0:16, at] - theta * stacked[0:16, at]) / degree
        stacked[16:32, at] = residual
        stacked_image[16:32, at] = degree * residual - (acc_ref[block] - theta * scaled_ref[block])
    gram_b = dot_nt(stacked[...], stacked[...], HIGHEST)
    gram_a = dot_nt(stacked[...], stacked_image[...], HIGHEST)
    packed = pack_grams(gram_b, gram_a, wide_ref)
    for peer in range(packed_ref.shape[0]):
        packed_ref[peer] = packed


def make_grams(
    halo_list, counts, halo_tiles, weights, basis_halo, own, scaled, basis, image, degree, previous, previous_image, n_dom
):
    stack = shaped((3 * K, basis.shape[1]), F32)
    return call(
        gram_kernel,
        (stack, stack, shaped((n_dom, 24, BS), F32)),
        [SMEM, SMEM, VMEM] + [HBM] * 9,
        (VMEM, VMEM, VMEM),
        (
            pltpu.VMEM(basis_halo.shape, BF16),
            pltpu.VMEM((RB + 1, K, BS), F32),
            pltpu.VMEM((RB + 1, K, BS), F32),
            pltpu.VMEM(degree.shape, F32),
            pltpu.SemaphoreType.DMA((8,)),
            HELD,
            GROUP_SEMS,
            pltpu.VMEM((n_dom * K, BS), BF16),
            pltpu.VMEM((SEND, n_dom, K, BS), F32),
            pltpu.VMEM((n_dom * SEND, BS), F32),
            pltpu.VMEM((BS, BS), F32),
        ),
        flops=2 * SLOTS * K * BS * BS,
        moved=10000000,
    )(
        halo_list, counts, halo_tiles,
        *map(in_hbm, (weights, basis_halo, own, scaled, basis, image, degree, previous, previous_image)),
    )


def inverse_factor(gram, n):
    row = iota2((n, BS), 0)
    lane = iota2((n, BS), 1)
    work = jnp.where(lane < n, gram, jnp.where(lane == row + n, 1.0, 0.0))
    for first in range(0, n, 8):
        left = [jnp.broadcast_to(work[:, first + j : first + j + 1], (n, BS)) for j in range(8)]
        rows = [work[first + j : first + j + 1, :] for j in range(8)]
        for j in range(8):
            scale = lax.rsqrt(left[j][first + j : first + j + 1, :])
            rows[j] = rows[j] * scale
            left[j] = jnp.where(row > first + j, left[j] * scale, 0.0)
            for k in range(j + 1, 8):
                entry = left[j][first + k : first + k + 1, :]
                rows[k] = rows[k] - entry * rows[j]
                left[k] = left[k] - left[j] * entry
        for j in range(8):
            work = jnp.where(row == first + j, rows[j], work - left[j] * rows[j])
    return pltpu.roll(work, BS - n, 1)


def final_kernel(
    root_rows, taken_ref, stacked_ref, stacked_image_ref, new_basis_ref, new_image_ref, wide_ref
):
    packed = taken_ref[0]
    for peer in range(1, taken_ref.shape[0]):
        packed = packed + taken_ref[peer]
    gram_b, gram_a = unpack_grams(packed, wide_ref)
    inverse = inverse_factor(gram_b, 48)[:, 0:48]
    symmetric = gram_a[:, 0:48]
    reduced = dot_nt(dot_nn(inverse, symmetric, HIGHEST), inverse, HIGHEST)
    wide = square(reduced, wide_ref)
    reduced = 0.5 * (wide + wide.T)[0:48, 0:48]
    spread = jnp.max(jnp.sum(jnp.abs(reduced), axis=1, keepdims=True), axis=0, keepdims=True)
    row = iota2((48, 48), 0)
    lane = iota2((48, 48), 1)
    filter_mat = (jnp.where(row == lane, spread, 0.0) - reduced) / (2.0 * spread)
    turned = filter_mat[0:16, :]
    for repeat in range(3):
        turned = dot_nn(turned, filter_mat, HIGHEST)
    inner = dot_nt(turned, turned, HIGHEST)
    wide_ref[...] = jnp.zeros_like(wide_ref)
    wide_ref[0:16, 0:16] = inner
    sub_inverse = inverse_factor(wide_ref[0:16, :], 16)[:, 0:16]
    coeff = dot_nn(dot_nn(sub_inverse, turned, HIGHEST), inverse, HIGHEST) * root_rows
    new_basis_ref[...] = dot_nn(coeff, stacked_ref[...], HIGHEST)
    new_image_ref[...] = dot_nn(coeff, stacked_image_ref[...], HIGHEST)


def finish(root_rows, packed, stacked, stacked_image):
    shape = (K, stacked.shape[1])
    return call(
        functools.partial(final_kernel, root_rows),
        (shaped(shape, F32), shaped(shape, F32)),
        [VMEM] * 3,
        (VMEM, VMEM),
        (pltpu.VMEM((BS, BS), F32),),
        flops=1000000,
        moved=3000000,
    )(packed, stacked, stacked_image)


def to_all(value, axis):
    return lax.all_to_all(value, axis, split_axis=0, concat_axis=0, tiled=True)


def body(
    n_dom, n_row,
    basis, previous, previous_image, degree, coupling, slot_row, slot_column, send_lists, live_slots,
):
    part = n_row * RB
    place = lax.axis_index("row").astype(jnp.int32).reshape(1)
    send_list = send_lists.reshape(n_dom * SEND)
    degree = degree.reshape(RB, BS)
    own_list, halo_list, counts = make_lists(slot_row, slot_column, live_slots, part)

    gathered = gather_row(cast_tiles(in_hbm(basis), in_hbm(degree)), n_row, HALF + 2)
    basis_part, inverse, chosen = first_select(gathered, place, send_list, n_row)
    halo_tiles = to_all(chosen, "dom")
    own, own_weights, halo_weights = first_own(own_list, halo_list, counts, basis_part, coupling)
    image, tiles, basis_halo = make_image(halo_list, counts, halo_tiles, halo_weights, own, basis, degree)

    gathered = gather_row(tiles, n_row, HALF)
    part_tiles, chosen, table = second_select(gathered, place, send_list, picks(send_list), n_row)
    halo_tiles = to_all(chosen, "dom")
    own, scaled = second_own(own_list, counts, part_tiles, table, basis_part, inverse, own_weights, n_row)
    stacked, stacked_image, packed = make_grams(
        halo_list, counts, halo_tiles, halo_weights, basis_halo, own, scaled, basis, image, degree, previous, previous_image,
        n_dom,
    )
    packed = to_all(add_and_repeat(to_all(packed, "dom"), n_row), "row")
    root_rows = math.sqrt(basis.shape[1] * n_dom * n_row)
    return finish(root_rows, packed, stacked, stacked_image)


def solution(mesh):
    split = P(None, ("dom", "row"))
    flat = P(("dom", "row"))
    return jax.shard_map(
        functools.partial(body, mesh.shape["dom"], mesh.shape["row"]),
        mesh=mesh,
        in_specs=(
            split, split, split, flat, P(("dom", "row"), None, None), flat, flat, P("dom", None, None), flat,
        ),
        out_specs=(split, split),
        check_vma=False,
    )
```

```python
import functools
import math

import jax
import jax.numpy as jnp
from jax import lax
from jax.experimental import pallas as pl
from jax.experimental.pallas import tpu as pltpu
from jax.sharding import PartitionSpec as P

K = 16
BS = 128
RB = 32
SLOTS = 256
SEND = 8
HALF = RB // 2
EXTRA = SEND + 1
GROUP = 32
LEN = SLOTS + GROUP
F32 = jnp.float32
BF16 = jnp.bfloat16
HIGHEST = lax.Precision.HIGHEST
MARGIN = 6 * 1024 * 1024
SMEM = pl.BlockSpec(memory_space=pltpu.SMEM)
HBM = pl.BlockSpec(memory_space=pl.ANY)
VMEM = pl.BlockSpec(memory_space=pltpu.VMEM)


def size(array):
    return math.prod(array.shape) * jnp.dtype(array.dtype).itemsize


def call(kernel, out_shape, in_specs, out_specs, scratch=(), flops=0, moved=0):
    def run(*args):
        arrays = list(args) + jax.tree.leaves(out_shape) + [held for held in scratch if jnp.issubdtype(held.dtype, jnp.floating)]
        return pl.pallas_call(
            kernel,
            out_shape=out_shape,
            in_specs=in_specs,
            out_specs=out_specs,
            scratch_shapes=scratch,
            compiler_params=pltpu.CompilerParams(vmem_limit_bytes=MARGIN + sum(map(size, arrays))),
            cost_estimate=pl.CostEstimate(flops=flops, bytes_accessed=moved, transcendentals=0),
        )(*args)

    return run


def shaped(shape, dtype):
    return jax.ShapeDtypeStruct(shape, dtype)


def in_hbm(value):
    return pltpu.with_memory_space_constraint(value, pltpu.HBM)


def start_copies(pairs, sems, first=0):
    copies = [pltpu.make_async_copy(source, target, sems.at[first + i]) for i, (source, target) in enumerate(pairs)]
    for copy in copies:
        copy.start()
    return copies


def wait_all(copies):
    for copy in copies:
        copy.wait()


def dot_nt(left, right, precision=None):
    return lax.dot_general(
        left, right, (((1,), (1,)), ((), ())), precision=precision, preferred_element_type=F32
    )


def dot_nn(left, right, precision=None):
    return lax.dot_general(
        left, right, (((1,), (0,)), ((), ())), precision=precision, preferred_element_type=F32
    )


def columns(block):
    return slice(block * BS, (block + 1) * BS)


def iota2(shape, axis):
    return lax.broadcasted_iota(jnp.int32, shape, axis)


def list_kernel(part, row_ref, column_ref, live_ref, own_ref, halo_ref, count_ref):
    live = live_ref[0]

    def step(quad, counts):
        n_own, n_halo = counts
        for j in range(4):
            slot = quad * 4 + j
            column = column_ref[slot]
            entry = slot + (row_ref[slot] << 16)
            own_ref[n_own] = entry + (column << 8)
            halo_ref[n_halo] = entry + ((column - part) << 8)
            used = slot < live
            is_own = used & (column < part)
            is_halo = used & (column >= part)
            n_own = n_own + is_own.astype(jnp.int32)
            n_halo = n_halo + is_halo.astype(jnp.int32)
        return n_own, n_halo

    n_own, n_halo = lax.fori_loop(0, lax.div(live + 3, 4), step, (jnp.int32(0), jnp.int32(0)))
    for ref, count in ((own_ref, n_own), (halo_ref, n_halo)):
        for extra in range(GROUP):
            ref[count + extra] = RB << 16
    count_ref[0] = n_own
    count_ref[1] = n_halo
    count_ref[2] = live


def make_lists(slot_row, slot_column, live_slots, part):
    return call(
        functools.partial(list_kernel, part),
        (shaped((LEN,), jnp.int32), shaped((LEN,), jnp.int32), shaped((3,), jnp.int32)),
        [SMEM, SMEM, SMEM],
        (SMEM, SMEM, SMEM),
        moved=20000,
    )(slot_row, slot_column, live_slots)


def split3(value):
    high = value.astype(BF16).astype(F32)
    rest = value - high
    middle = rest.astype(BF16).astype(F32)
    return high, middle, (rest - middle).astype(BF16).astype(F32)


def cast_kernel(field_hbm, degree_hbm, tiles_ref, field_ref, degree_ref, sems):
    wait_all(start_copies([(field_hbm, field_ref), (degree_hbm, degree_ref)], sems))
    for block in range(RB):
        tiles_ref[block + 2 * (block // HALF)] = field_ref[:, columns(block)].astype(BF16)
    for half in range(2):
        inverse = 1.0 / degree_ref[half * HALF : (half + 1) * HALF]
        high = inverse.astype(BF16)
        at = half * (HALF + 2) + HALF
        tiles_ref[at] = high
        tiles_ref[at + 1] = (inverse - high.astype(F32)).astype(BF16)


def cast_tiles(field, degree):
    return call(
        cast_kernel,
        shaped((RB + 4, K, BS), BF16),
        [HBM, HBM],
        VMEM,
        (pltpu.VMEM(field.shape, F32), pltpu.VMEM(degree.shape, F32), pltpu.SemaphoreType.DMA((2,))),
        moved=400000,
    )(field, degree)


def gather_row(tiles, n_row):
    def shifted(value, shift):
        return lax.ppermute(value, "row", [(i, (i + shift) % n_row) for i in range(n_row)])

    pieces = [(0, tiles)]
    from_below = from_above = tiles
    for step in range(1, n_row // 2):
        from_below = shifted(from_below, 1)
        from_above = shifted(from_above, -1)
        pieces += [(-step, from_below), (step, from_above)]
    return pieces + [(n_row // 2, shifted(tiles, n_row // 2))]


def halves(offsets, pieces, half, n_row, place):
    parts = []
    for offset, piece in zip(offsets, pieces):
        owner = lax.rem(place + offset + n_row, n_row)
        parts += [(owner, 0, piece, 0), (owner, 1, piece, half)]
    return parts


def fill_and_send(fill, chosen_ref, chosen_hbm, sems):
    peers = chosen_ref.shape[0] // EXTRA
    quarter = max(1, peers // 4)
    copies = []
    for at in range(peers // quarter):
        for peer in range(at * quarter, (at + 1) * quarter):
            fill(peer)
        span = pl.ds(at * quarter * EXTRA, quarter * EXTRA)
        copies.append(pltpu.make_async_copy(chosen_ref.at[span], chosen_hbm.at[span], sems.at[at]))
        copies[-1].start()
    for copy in copies:
        copy.wait()


def first_select_kernel(offsets, n_row, place_ref, send_ref, *refs):
    pieces, (part_hbm, inverse_hbm, chosen_hbm) = refs[:-8], refs[-8:-5]
    part_ref, inverse_ref, rows_ref, chosen_ref, sems = refs[-5:]
    for owner, half, piece, start in halves(offsets, pieces, HALF + 2, n_row, place_ref[0]):
        at = owner * RB + half * HALF
        part_ref[pl.ds(at, HALF)] = piece[start : start + HALF]
        inverse_ref[pl.ds(pl.multiple_of(at, HALF), HALF), :] = (
            piece[start + HALF].astype(F32) + piece[start + HALF + 1].astype(F32)
        )

    copies = start_copies([(part_ref, part_hbm), (inverse_ref, inverse_hbm)], sems, 4)

    def fill(peer):
        for j in range(SEND):
            block = send_ref[peer * SEND + j]
            chosen_ref[peer * EXTRA + j] = part_ref[block]
            rows_ref[j : j + 1, :] = inverse_ref[pl.ds(block, 1), :]
        rows = rows_ref[...]
        high = rows.astype(BF16).astype(F32)
        chosen_ref[peer * EXTRA + SEND] = jnp.concatenate([high, rows - high], axis=0).astype(BF16)

    fill_and_send(fill, chosen_ref, chosen_hbm, sems)
    wait_all(copies)


def first_select(gathered, place, send_list, n_row):
    part = n_row * RB
    peers = send_list.shape[0] // SEND
    return call(
        functools.partial(first_select_kernel, [offset for offset, _ in gathered], n_row),
        (pltpu.HBM((part, K, BS), BF16), pltpu.HBM((part, BS), F32), pltpu.HBM((peers * EXTRA, K, BS), BF16)),
        [SMEM, SMEM] + [VMEM] * len(gathered),
        (HBM, HBM, HBM),
        (
            pltpu.VMEM((part, K, BS), BF16),
            pltpu.VMEM((part, BS), F32),
            pltpu.VMEM((SEND, BS), F32),
            pltpu.VMEM((peers * EXTRA, K, BS), BF16),
            pltpu.SemaphoreType.DMA((6,)),
        ),
        moved=3000000,
    )(place, send_list, *[piece for _, piece in gathered])


def second_select_kernel(offsets, n_row, place_ref, send_ref, pick_ref, *refs):
    pieces, (part_hbm, chosen_hbm, table_hbm, part_ref, chosen_ref, table_ref, sems) = refs[:-7], refs[-7:]
    lane = iota2((K, BS), 1)
    table = jnp.zeros((K, BS), F32)
    side_sum = jnp.zeros((K, BS), F32)
    for owner, half, piece, start in halves(offsets, pieces, HALF, n_row, place_ref[0]):
        part_ref[pl.ds(owner * RB + half * HALF, HALF)] = piece[start : start + HALF]
        if half == 1:
            side = piece[start + HALF].astype(F32)
            table = jnp.where(lane == owner, side[:, 0:1], table)
            side_sum = side_sum + side
    top = jnp.sum(jnp.where((lane >= 1) & (lane <= 3), side_sum, 0.0), axis=1, keepdims=True)
    bottom = jnp.sum(jnp.where((lane >= 4) & (lane <= 6), side_sum, 0.0), axis=1, keepdims=True)
    for at, value in enumerate(split3(top) + split3(bottom)):
        table = jnp.where(lane == 8 + at, value, table)
    table = table.astype(BF16)
    table_ref[...] = table
    copies = start_copies([(part_ref, part_hbm), (table_ref, table_hbm)], sems, 4)
    sides = dot_nn(table, pick_ref[...])
    for peer in range(chosen_ref.shape[0] // EXTRA):
        chosen_ref[peer * EXTRA + SEND] = sides[:, columns(peer)].astype(BF16)

    def fill(peer):
        for j in range(SEND):
            chosen_ref[peer * EXTRA + j] = part_ref[send_ref[peer * SEND + j]]

    fill_and_send(fill, chosen_ref, chosen_hbm, sems)
    wait_all(copies)


def second_select(gathered, place, send_list, pick, n_row):
    peers = send_list.shape[0] // SEND
    return call(
        functools.partial(second_select_kernel, [offset for offset, _ in gathered], n_row),
        (pltpu.HBM((n_row * RB, K, BS), BF16), pltpu.HBM((peers * EXTRA, K, BS), BF16), pltpu.HBM((K, BS), BF16)),
        [SMEM, SMEM] + [VMEM] * (len(gathered) + 1),
        (HBM, HBM, HBM),
        (
            pltpu.VMEM((n_row * RB, K, BS), BF16),
            pltpu.VMEM((peers * EXTRA, K, BS), BF16),
            pltpu.VMEM((K, BS), BF16),
            pltpu.SemaphoreType.DMA((6,)),
        ),
        moved=3000000,
    )(place, send_list, pick, *[piece for _, piece in gathered])


def picks(send_list):
    peers = send_list.shape[0] // SEND
    owner = (send_list >> 5).reshape(peers, SEND)
    lane = jnp.broadcast_to(jnp.arange(BS, dtype=jnp.int32)[None, :], (peers, BS))
    target = jnp.where(lane < 14, lane, -1)
    target = jnp.concatenate([owner, target[:, SEND:]], axis=1).reshape(-1)
    return (jnp.arange(BS, dtype=jnp.int32)[:, None] == target[None, :]).astype(BF16)


def groups_of(count):
    return lax.div(count + GROUP - 1, GROUP)


def copy_group(source, target, sems, group):
    span = pl.ds(group * GROUP, GROUP)
    return pltpu.make_async_copy(source.at[span], target.at[span], sems.at[group])


def start_groups(count, source, target, sems):
    def start(group, carry):
        copy_group(source, target, sems, group).start()
        return carry

    lax.fori_loop(0, groups_of(count), start, 0)


def wait_groups(count, source, target, sems):
    def wait(group, carry):
        copy_group(source, target, sems, group).wait()
        return carry

    lax.fori_loop(0, groups_of(count), wait, 0)


def products_of(entries, weights, load):
    products = []
    for at in range(0, GROUP, 2):
        left = [load((entry >> 8) & 255) for entry in entries[at : at + 2]]
        product = dot_nn(jnp.concatenate(left, axis=0), jnp.concatenate(weights[at : at + 2], axis=1))
        rows = left[0].shape[0]
        products += [product[:rows, :BS], product[rows:, BS:]]
    return products


def work(count, list_ref, weights_hbm, held, sems, load, add):
    def step(group, carry):
        base = group * GROUP
        copy_group(weights_hbm, held, sems, group).wait()
        entries = [list_ref[base + j] for j in range(GROUP)]
        products = products_of(entries, [held[base + j] for j in range(GROUP)], load)
        for entry, product in zip(entries, products):
            add(entry >> 16, (entry >> 8) & 255, product)
        return carry

    lax.fori_loop(0, groups_of(count), step, 0)


WEIGHTS = pltpu.HBM((SLOTS, BS, BS), BF16)
HELD = pltpu.VMEM((SLOTS, BS, BS), BF16)
GROUP_SEMS = pltpu.SemaphoreType.DMA((SLOTS // GROUP,))
ROWS = shaped((RB + 1, K, BS), F32)


def scale_block(block, inverse):
    return (block.astype(F32) * inverse).astype(BF16)


def first_own_kernel(
    own_list, halo_list, count_ref, part_ref, coupling_ref, acc_ref, own_hbm, halo_hbm, held, own_held, halo_held, sems,
    own_sems, halo_sems,
):
    live = count_ref[2]
    start_groups(live, coupling_ref, held, sems)
    acc_ref[...] = jnp.zeros_like(acc_ref)
    wait_groups(live, coupling_ref, held, sems)

    def own_step(group, carry):
        base = group * GROUP
        entries = [own_list[base + j] for j in range(GROUP)]
        weights = [held[entry & 255].T for entry in entries]
        for j in range(GROUP):
            own_held[base + j] = weights[j]
        copy_group(own_held, own_hbm, own_sems, group).start()
        products = products_of(entries, weights, lambda block: part_ref[block])
        for entry, product in zip(entries, products):
            row = entry >> 16
            acc_ref[row] = acc_ref[row] + product
        return carry

    def halo_step(group, carry):
        base = group * GROUP
        for j in range(GROUP):
            halo_held[base + j] = held[halo_list[base + j] & 255].T
        copy_group(halo_held, halo_hbm, halo_sems, group).start()
        return carry

    lax.fori_loop(0, groups_of(count_ref[0]), own_step, 0)
    lax.fori_loop(0, groups_of(count_ref[1]), halo_step, 0)
    wait_groups(count_ref[0], own_held, own_hbm, own_sems)
    wait_groups(count_ref[1], halo_held, halo_hbm, halo_sems)


def first_own(own_list, halo_list, counts, part_tiles, coupling):
    return call(
        first_own_kernel,
        (pltpu.HBM(ROWS.shape, F32), WEIGHTS, WEIGHTS),
        [SMEM, SMEM, SMEM, VMEM, HBM],
        (VMEM, HBM, HBM),
        (HELD, HELD, HELD, GROUP_SEMS, GROUP_SEMS, GROUP_SEMS),
        flops=2 * SLOTS * K * BS * BS,
        moved=10000000,
    )(own_list, halo_list, counts, in_hbm(part_tiles), in_hbm(coupling))


def image_kernel(
    list_ref, count_ref, halo_ref, weights_hbm, own_hbm, basis_ref, degree_ref, image_hbm, tiles_ref, halo_hbm, image_ref,
    out_sems, acc_ref, held, sems,
):
    own = start_copies([(own_hbm, acc_ref)], out_sems, 2)
    start_groups(count_ref[1], weights_hbm, held, sems)
    copies = start_copies([(halo_ref, halo_hbm)], out_sems)
    wait_all(own)

    def load(block):
        return halo_ref[block + (block >> 3)]

    def add(row, block, product):
        acc_ref[row] = acc_ref[row] + product

    work(count_ref[1], list_ref, weights_hbm, held, sems, load, add)
    top = jnp.zeros((K, BS), F32)
    bottom = jnp.zeros((K, BS), F32)
    for block in range(RB):
        at = columns(block)
        basis = basis_ref[:, at]
        image = degree_ref[block : block + 1, :] * basis - acc_ref[block]
        image_ref[:, at] = image
        top = top + basis * image
        bottom = bottom + basis * basis
    copies += start_copies([(image_ref, image_hbm)], out_sems, 1)
    top = jnp.sum(top, axis=1, keepdims=True)
    bottom = jnp.sum(bottom, axis=1, keepdims=True)
    usable = bottom > 1e-30
    quotient = jnp.where(usable, top / jnp.where(usable, bottom, 1.0), 0.0).astype(BF16).astype(F32)
    for block in range(RB):
        at = columns(block)
        residual = (image_ref[:, at] - quotient * basis_ref[:, at]) / degree_ref[block : block + 1, :]
        tiles_ref[block] = residual.astype(BF16)
    lane = iota2((K, BS), 1)
    side = jnp.where(lane == 0, quotient, 0.0)
    for at, value in enumerate(split3(top) + split3(bottom)):
        side = jnp.where(lane == 1 + at, value, side)
    tiles_ref[RB] = side.astype(BF16)
    wait_all(copies)


def make_image(halo_list, counts, halo_tiles, weights, own, basis, degree):
    return call(
        image_kernel,
        (pltpu.HBM(basis.shape, F32), shaped((RB + 1, K, BS), BF16), pltpu.HBM(halo_tiles.shape, BF16)),
        [SMEM, SMEM, VMEM, HBM, HBM, VMEM, VMEM],
        (HBM, VMEM, HBM),
        (
            pltpu.VMEM(basis.shape, F32),
            pltpu.SemaphoreType.DMA((3,)),
            pltpu.VMEM((RB + 1, K, BS), F32),
            HELD,
            GROUP_SEMS,
        ),
        flops=2 * SLOTS * K * BS * BS,
        moved=8000000,
    )(halo_list, counts, halo_tiles, in_hbm(weights), in_hbm(own), basis, degree)


def second_own_kernel(
    list_ref, count_ref, part_ref, table_ref, basis_part_ref, inverse_ref, weights_hbm, acc_ref, scaled_ref, quotient_ref,
    held, sems,
):
    start_groups(count_ref[0], weights_hbm, held, sems)
    acc_ref[...] = jnp.zeros_like(acc_ref)
    scaled_ref[...] = jnp.zeros_like(scaled_ref)
    table = table_ref[...].astype(F32)
    for owner in range(quotient_ref.shape[0]):
        quotient_ref[owner] = jnp.broadcast_to(table[:, owner : owner + 1], (K, BS))

    def load(block):
        scaled = scale_block(basis_part_ref[block], inverse_ref[pl.ds(block, 1), :])
        return jnp.concatenate([part_ref[block], scaled], axis=0)

    def add(row, block, product):
        acc_ref[row] = acc_ref[row] + (product[0:K] + quotient_ref[block >> 5] * product[K:])
        scaled_ref[row] = scaled_ref[row] + product[K:]

    work(count_ref[0], list_ref, weights_hbm, held, sems, load, add)


def second_own(own_list, counts, part_tiles, table, basis_part, inverse, weights, n_row):
    return call(
        second_own_kernel,
        (pltpu.HBM(ROWS.shape, F32), pltpu.HBM(ROWS.shape, F32)),
        [SMEM, SMEM, VMEM, VMEM, VMEM, VMEM, HBM],
        (VMEM, VMEM),
        (pltpu.VMEM((n_row, K, BS), F32), HELD, GROUP_SEMS),
        flops=4 * SLOTS * K * BS * BS,
        moved=10000000,
    )(own_list, counts, *map(in_hbm, (part_tiles, table, basis_part, inverse, weights)))


def spread_kernel(taken_ref, given_ref):
    total = taken_ref[0]
    for peer in range(1, taken_ref.shape[0]):
        total = total + taken_ref[peer]
    for peer in range(given_ref.shape[0]):
        given_ref[peer] = total


def add_and_repeat(taken, peers):
    return call(
        spread_kernel, shaped((peers,) + taken.shape[1:], F32), [VMEM], VMEM, moved=400000
    )(taken)


def square(value, wide_ref):
    rows, cols = value.shape
    wide_ref[...] = jnp.zeros_like(wide_ref)
    wide_ref[0:rows, 0:cols] = value
    return wide_ref[...]


def pack_grams(gram_b, gram_a, wide_ref):
    wide_a = square(gram_a, wide_ref)
    both = 0.5 * (wide_a + wide_a.T)
    wide_b = square(gram_b, wide_ref)
    row = iota2((BS, BS), 0)
    lane = iota2((BS, BS), 1)
    packed = jnp.where(row <= lane, wide_b, both)
    diagonal = jnp.sum(jnp.where(row == lane, both, 0.0), axis=1, keepdims=True)
    low, high = packed[0:24], pltpu.roll(packed[24:48], 48, 1)
    at = iota2((24, BS), 1)
    out = jnp.where(at < 48, low, high)
    out = jnp.where(at == 96, diagonal[0:24], out)
    return jnp.where(at == 97, diagonal[24:48], out)


def unpack_grams(packed, wide_ref):
    wide_ref[...] = jnp.zeros_like(wide_ref)
    at = iota2((24, BS), 1)
    wide_ref[0:24] = jnp.where(at < 48, packed, 0.0)
    wide_ref[24:48] = jnp.where(at < 48, pltpu.roll(packed, 80, 1), 0.0)
    wide = wide_ref[...]
    flipped = wide.T
    row = iota2((48, BS), 0)
    lane = iota2((48, BS), 1)
    wide, flipped = wide[0:48], flipped[0:48]
    diagonal = jnp.concatenate([packed[:, 96:97], packed[:, 97:98]], axis=0)
    gram_b = jnp.where(row <= lane, wide, flipped)
    gram_a = jnp.where(row == lane, diagonal, jnp.where(row > lane, wide, flipped))
    return gram_b, gram_a


def gram_kernel(
    list_ref, count_ref, halo_ref, weights_hbm, basis_halo_hbm, own_hbm, own_scaled_hbm, basis_hbm, image_hbm, degree_hbm,
    previous_hbm, previous_image_hbm, stacked, stacked_image, packed_ref, basis_halo_ref, acc_ref, scaled_ref, degree_ref,
    in_sems, held, sems, side_ref, quotient_ref, inverse_ref, wide_ref,
):
    early = [(basis_halo_hbm, basis_halo_ref), (own_hbm, acc_ref), (own_scaled_hbm, scaled_ref)]
    late = [
        (basis_hbm, stacked.at[0:16]),
        (previous_hbm, stacked.at[32:48]),
        (image_hbm, stacked_image.at[0:16]),
        (previous_image_hbm, stacked_image.at[32:48]),
        (degree_hbm, degree_ref),
    ]
    early = start_copies(early, in_sems)
    start_groups(count_ref[1], weights_hbm, held, sems)
    late = start_copies(late, in_sems, 3)
    peers = halo_ref.shape[0] // EXTRA
    total = jnp.zeros((K, BS), F32)
    for peer in range(peers):
        side = halo_ref[peer * EXTRA + SEND]
        side_ref[peer * K : (peer + 1) * K, :] = side
        total = total + side.astype(F32)
    side = side_ref[...]
    for j in range(SEND):
        spread = (iota2((BS, BS), 0) == j).astype(F32).astype(BF16)
        quotient_ref[j] = dot_nn(side, spread).reshape(peers, K, BS)
    lane = iota2((K, BS), 1)
    top = jnp.sum(jnp.where((lane >= 8) & (lane <= 10), total, 0.0), axis=1, keepdims=True)
    bottom = jnp.sum(jnp.where((lane >= 11) & (lane <= 13), total, 0.0), axis=1, keepdims=True)
    theta = top / bottom
    wait_all(early)
    for peer in range(peers):
        inverse = basis_halo_ref[peer * EXTRA + SEND].astype(F32)
        inverse_ref[peer * SEND : (peer + 1) * SEND, :] = inverse[0:SEND] + inverse[SEND:]

    def load(block):
        tile = block + (block >> 3)
        scaled = scale_block(basis_halo_ref[tile], inverse_ref[pl.ds(block, 1), :])
        return jnp.concatenate([halo_ref[tile], scaled], axis=0)

    def add(row, block, product):
        quotient = quotient_ref[block & 7, block >> 3]
        acc_ref[row] = acc_ref[row] + (product[0:K] + quotient * product[K:])
        scaled_ref[row] = scaled_ref[row] + product[K:]

    work(count_ref[1], list_ref, weights_hbm, held, sems, load, add)
    wait_all(late)
    for block in range(RB):
        at = columns(block)
        degree = degree_ref[block : block + 1, :]
        residual = (stacked_image[0:16, at] - theta * stacked[0:16, at]) / degree
        stacked[16:32, at] = residual
        stacked_image[16:32, at] = degree * residual - (acc_ref[block] - theta * scaled_ref[block])
    gram_b = dot_nt(stacked[...], stacked[...], HIGHEST)
    gram_a = dot_nt(stacked[...], stacked_image[...], HIGHEST)
    packed = pack_grams(gram_b, gram_a, wide_ref)
    for peer in range(packed_ref.shape[0]):
        packed_ref[peer] = packed


def make_grams(
    halo_list, counts, halo_tiles, weights, basis_halo, own, scaled, basis, image, degree, previous, previous_image, n_dom
):
    stack = shaped((3 * K, basis.shape[1]), F32)
    return call(
        gram_kernel,
        (stack, stack, shaped((n_dom, 24, BS), F32)),
        [SMEM, SMEM, VMEM] + [HBM] * 9,
        (VMEM, VMEM, VMEM),
        (
            pltpu.VMEM(basis_halo.shape, BF16),
            pltpu.VMEM((RB + 1, K, BS), F32),
            pltpu.VMEM((RB + 1, K, BS), F32),
            pltpu.VMEM(degree.shape, F32),
            pltpu.SemaphoreType.DMA((8,)),
            HELD,
            GROUP_SEMS,
            pltpu.VMEM((n_dom * K, BS), BF16),
            pltpu.VMEM((SEND, n_dom, K, BS), F32),
            pltpu.VMEM((n_dom * SEND, BS), F32),
            pltpu.VMEM((BS, BS), F32),
        ),
        flops=2 * SLOTS * K * BS * BS,
        moved=10000000,
    )(
        halo_list, counts, halo_tiles,
        *map(in_hbm, (weights, basis_halo, own, scaled, basis, image, degree, previous, previous_image)),
    )


def inverse_factor(gram, n):
    row = iota2((n, BS), 0)
    lane = iota2((n, BS), 1)
    work = jnp.where(lane < n, gram, jnp.where(lane == row + n, 1.0, 0.0))
    for first in range(0, n, 8):
        left = [jnp.broadcast_to(work[:, first + j : first + j + 1], (n, BS)) for j in range(8)]
        rows = [work[first + j : first + j + 1, :] for j in range(8)]
        for j in range(8):
            scale = lax.rsqrt(left[j][first + j : first + j + 1, :])
            rows[j] = rows[j] * scale
            left[j] = jnp.where(row > first + j, left[j] * scale, 0.0)
            for k in range(j + 1, 8):
                entry = left[j][first + k : first + k + 1, :]
                rows[k] = rows[k] - entry * rows[j]
                left[k] = left[k] - left[j] * entry
        for j in range(8):
            work = jnp.where(row == first + j, rows[j], work - left[j] * rows[j])
    return pltpu.roll(work, BS - n, 1)


def final_kernel(
    root_rows, taken_ref, stacked_ref, stacked_image_ref, new_basis_ref, new_image_ref, wide_ref
):
    packed = taken_ref[0]
    for peer in range(1, taken_ref.shape[0]):
        packed = packed + taken_ref[peer]
    gram_b, gram_a = unpack_grams(packed, wide_ref)
    inverse = inverse_factor(gram_b, 48)[:, 0:48]
    symmetric = gram_a[:, 0:48]
    reduced = dot_nt(dot_nn(inverse, symmetric, HIGHEST), inverse, HIGHEST)
    wide = square(reduced, wide_ref)
    reduced = 0.5 * (wide + wide.T)[0:48, 0:48]
    spread = jnp.max(jnp.sum(jnp.abs(reduced), axis=1, keepdims=True), axis=0, keepdims=True)
    row = iota2((48, 48), 0)
    lane = iota2((48, 48), 1)
    filter_mat = (jnp.where(row == lane, spread, 0.0) - reduced) / (2.0 * spread)
    turned = filter_mat[0:16, :]
    for repeat in range(3):
        turned = dot_nn(turned, filter_mat, HIGHEST)
    inner = dot_nt(turned, turned, HIGHEST)
    wide_ref[...] = jnp.zeros_like(wide_ref)
    wide_ref[0:16, 0:16] = inner
    sub_inverse = inverse_factor(wide_ref[0:16, :], 16)[:, 0:16]
    coeff = dot_nn(dot_nn(sub_inverse, turned, HIGHEST), inverse, HIGHEST) * root_rows
    new_basis_ref[...] = dot_nn(coeff, stacked_ref[...], HIGHEST)
    new_image_ref[...] = dot_nn(coeff, stacked_image_ref[...], HIGHEST)


def finish(root_rows, packed, stacked, stacked_image):
    shape = (K, stacked.shape[1])
    return call(
        functools.partial(final_kernel, root_rows),
        (shaped(shape, F32), shaped(shape, F32)),
        [VMEM] * 3,
        (VMEM, VMEM),
        (pltpu.VMEM((BS, BS), F32),),
        flops=1000000,
        moved=3000000,
    )(packed, stacked, stacked_image)


def to_all(value, axis):
    return lax.all_to_all(value, axis, split_axis=0, concat_axis=0, tiled=True)


def body(
    n_dom, n_row,
    basis, previous, previous_image, degree, coupling, slot_row, slot_column, send_lists, live_slots,
):
    part = n_row * RB
    place = lax.axis_index("row").astype(jnp.int32).reshape(1)
    send_list = send_lists.reshape(n_dom * SEND)
    degree = degree.reshape(RB, BS)
    own_list, halo_list, counts = make_lists(slot_row, slot_column, live_slots, part)

    gathered = gather_row(cast_tiles(in_hbm(basis), in_hbm(degree)), n_row)
    basis_part, inverse, chosen = first_select(gathered, place, send_list, n_row)
    halo_tiles = to_all(chosen, "dom")
    own, own_weights, halo_weights = first_own(own_list, halo_list, counts, basis_part, coupling)
    image, tiles, basis_halo = make_image(halo_list, counts, halo_tiles, halo_weights, own, basis, degree)

    gathered = gather_row(tiles, n_row)
    part_tiles, chosen, table = second_select(gathered, place, send_list, picks(send_list), n_row)
    halo_tiles = to_all(chosen, "dom")
    own, scaled = second_own(own_list, counts, part_tiles, table, basis_part, inverse, own_weights, n_row)
    stacked, stacked_image, packed = make_grams(
        halo_list, counts, halo_tiles, halo_weights, basis_halo, own, scaled, basis, image, degree, previous, previous_image,
        n_dom,
    )
    packed = to_all(add_and_repeat(to_all(packed, "dom"), n_row), "row")
    root_rows = math.sqrt(basis.shape[1] * n_dom * n_row)
    return finish(root_rows, packed, stacked, stacked_image)


def solution(mesh):
    split = P(None, ("dom", "row"))
    flat = P(("dom", "row"))
    return jax.shard_map(
        functools.partial(body, mesh.shape["dom"], mesh.shape["row"]),
        mesh=mesh,
        in_specs=(
            split, split, split, flat, P(("dom", "row"), None, None), flat, flat, P("dom", None, None), flat,
        ),
        out_specs=(split, split),
        check_vma=False,
    )
```

```python
import functools
import math

import jax
import jax.numpy as jnp
from jax import lax
from jax.experimental import pallas as pl
from jax.experimental.pallas import tpu as pltpu
from jax.sharding import PartitionSpec as P

K = 16
BS = 128
RB = 32
SLOTS = 256
SEND = 8
HALF = RB // 2
EXTRA = SEND + 1
GROUP = 32
LEN = SLOTS + GROUP
F32 = jnp.float32
BF16 = jnp.bfloat16
HIGHEST = lax.Precision.HIGHEST
MARGIN = 6 * 1024 * 1024
SMEM = pl.BlockSpec(memory_space=pltpu.SMEM)
HBM = pl.BlockSpec(memory_space=pl.ANY)
VMEM = pl.BlockSpec(memory_space=pltpu.VMEM)


def size(array):
    return math.prod(array.shape) * jnp.dtype(array.dtype).itemsize


def call(kernel, out_shape, in_specs, out_specs, scratch=(), flops=0, moved=0):
    def run(*args):
        arrays = list(args) + jax.tree.leaves(out_shape) + [held for held in scratch if jnp.issubdtype(held.dtype, jnp.floating)]
        return pl.pallas_call(
            kernel,
            out_shape=out_shape,
            in_specs=in_specs,
            out_specs=out_specs,
            scratch_shapes=scratch,
            compiler_params=pltpu.CompilerParams(vmem_limit_bytes=MARGIN + sum(map(size, arrays))),
            cost_estimate=pl.CostEstimate(flops=flops, bytes_accessed=moved, transcendentals=0),
        )(*args)

    return run


def shaped(shape, dtype):
    return jax.ShapeDtypeStruct(shape, dtype)


def in_hbm(value):
    return pltpu.with_memory_space_constraint(value, pltpu.HBM)


def start_copies(pairs, sems, first=0):
    copies = [pltpu.make_async_copy(source, target, sems.at[first + i]) for i, (source, target) in enumerate(pairs)]
    for copy in copies:
        copy.start()
    return copies


def wait_all(copies):
    for copy in copies:
        copy.wait()


def dot_nt(left, right, precision=None):
    return lax.dot_general(
        left, right, (((1,), (1,)), ((), ())), precision=precision, preferred_element_type=F32
    )


def dot_nn(left, right, precision=None):
    return lax.dot_general(
        left, right, (((1,), (0,)), ((), ())), precision=precision, preferred_element_type=F32
    )


def columns(block):
    return slice(block * BS, (block + 1) * BS)


def iota2(shape, axis):
    return lax.broadcasted_iota(jnp.int32, shape, axis)


def list_kernel(part, row_ref, column_ref, live_ref, own_ref, halo_ref, count_ref):
    live = live_ref[0]

    def step(quad, counts):
        n_own, n_halo = counts
        for j in range(4):
            slot = quad * 4 + j
            column = column_ref[slot]
            entry = slot + (row_ref[slot] << 16)
            own_ref[n_own] = entry + (column << 8)
            halo_ref[n_halo] = entry + ((column - part) << 8)
            used = slot < live
            is_own = used & (column < part)
            is_halo = used & (column >= part)
            n_own = n_own + is_own.astype(jnp.int32)
            n_halo = n_halo + is_halo.astype(jnp.int32)
        return n_own, n_halo

    n_own, n_halo = lax.fori_loop(0, lax.div(live + 3, 4), step, (jnp.int32(0), jnp.int32(0)))
    for ref, count in ((own_ref, n_own), (halo_ref, n_halo)):
        for extra in range(GROUP):
            ref[count + extra] = RB << 16
    count_ref[0] = n_own
    count_ref[1] = n_halo
    count_ref[2] = live


def make_lists(slot_row, slot_column, live_slots, part):
    return call(
        functools.partial(list_kernel, part),
        (shaped((LEN,), jnp.int32), shaped((LEN,), jnp.int32), shaped((3,), jnp.int32)),
        [SMEM, SMEM, SMEM],
        (SMEM, SMEM, SMEM),
        moved=20000,
    )(slot_row, slot_column, live_slots)


def split3(value):
    high = value.astype(BF16).astype(F32)
    rest = value - high
    middle = rest.astype(BF16).astype(F32)
    return high, middle, (rest - middle).astype(BF16).astype(F32)


def cast_kernel(field_hbm, tiles_ref, field_ref, sems):
    wait_all(start_copies([(field_hbm, field_ref)], sems))
    for block in range(RB):
        tiles_ref[block] = field_ref[:, columns(block)].astype(BF16)


def cast_tiles(field):
    return call(
        cast_kernel,
        shaped((RB, K, BS), BF16),
        [HBM],
        VMEM,
        (pltpu.VMEM(field.shape, F32), pltpu.SemaphoreType.DMA((1,))),
        moved=400000,
    )(field)


def gather_row(tiles, n_row):
    def shifted(value, shift):
        return lax.ppermute(value, "row", [(i, (i + shift) % n_row) for i in range(n_row)])

    pieces = [(0, tiles)]
    from_below = from_above = tiles
    for step in range(1, n_row // 2):
        from_below = shifted(from_below, 1)
        from_above = shifted(from_above, -1)
        pieces += [(-step, from_below), (step, from_above)]
    return pieces + [(n_row // 2, shifted(tiles, n_row // 2))]


def placed(offsets, pieces, n_row, place):
    return [(lax.rem(place + offset + n_row, n_row), piece) for offset, piece in zip(offsets, pieces)]


def fill_and_send(fill, tiles, chosen_ref, chosen_hbm, sems):
    peers = chosen_ref.shape[0] // tiles
    quarter = max(1, peers // 4)
    copies = []
    for at in range(peers // quarter):
        for peer in range(at * quarter, (at + 1) * quarter):
            fill(peer)
        span = pl.ds(at * quarter * tiles, quarter * tiles)
        copies.append(pltpu.make_async_copy(chosen_ref.at[span], chosen_hbm.at[span], sems.at[at]))
        copies[-1].start()
    wait_all(copies)


def first_select_kernel(offsets, n_row, place_ref, send_ref, *refs):
    pieces, (part_hbm, chosen_hbm, part_ref, chosen_ref, sems) = refs[:-5], refs[-5:]
    for owner, piece in placed(offsets, pieces, n_row, place_ref[0]):
        part_ref[pl.ds(owner * RB, RB)] = piece[...]
    copies = start_copies([(part_ref, part_hbm)], sems, 4)

    def fill(peer):
        for j in range(SEND):
            chosen_ref[peer * SEND + j] = part_ref[send_ref[peer * SEND + j]]

    fill_and_send(fill, SEND, chosen_ref, chosen_hbm, sems)
    wait_all(copies)


def first_select(gathered, place, send_list, n_row):
    part = n_row * RB
    count = send_list.shape[0]
    return call(
        functools.partial(first_select_kernel, [offset for offset, _ in gathered], n_row),
        (pltpu.HBM((part, K, BS), BF16), pltpu.HBM((count, K, BS), BF16)),
        [SMEM, SMEM] + [VMEM] * len(gathered),
        (HBM, HBM),
        (pltpu.VMEM((part, K, BS), BF16), pltpu.VMEM((count, K, BS), BF16), pltpu.SemaphoreType.DMA((5,))),
        moved=3000000,
    )(place, send_list, *[piece for _, piece in gathered])


def second_select_kernel(offsets, n_row, place_ref, send_ref, pick_ref, *refs):
    pieces, (part_hbm, chosen_hbm, table_hbm, inverse_hbm) = refs[:-10], refs[-10:-6]
    part_ref, chosen_ref, table_ref, inverse_ref, rows_ref, sems = refs[-6:]
    lane = iota2((K, BS), 1)
    table = jnp.zeros((K, BS), F32)
    side_sum = jnp.zeros((K, BS), F32)
    for owner, piece in placed(offsets, pieces, n_row, place_ref[0]):
        part_ref[pl.ds(owner * RB, RB)] = piece[0:RB]
        for half in range(2):
            at = pl.multiple_of(owner * RB + half * HALF, HALF)
            inverse_ref[pl.ds(at, HALF), :] = piece[RB + 1 + half].astype(F32)
        side = piece[RB].astype(F32)
        table = jnp.where(lane == owner, side[:, 0:1], table)
        side_sum = side_sum + side
    top = jnp.sum(jnp.where((lane >= 1) & (lane <= 3), side_sum, 0.0), axis=1, keepdims=True)
    bottom = jnp.sum(jnp.where((lane >= 4) & (lane <= 6), side_sum, 0.0), axis=1, keepdims=True)
    for at, value in enumerate(split3(top) + split3(bottom)):
        table = jnp.where(lane == 8 + at, value, table)
    table = table.astype(BF16)
    table_ref[...] = table
    copies = start_copies([(part_ref, part_hbm), (table_ref, table_hbm), (inverse_ref, inverse_hbm)], sems, 4)
    sides = dot_nn(table, pick_ref[...])

    def fill(peer):
        for j in range(SEND):
            block = send_ref[peer * SEND + j]
            chosen_ref[peer * EXTRA + j] = part_ref[block]
            rows_ref[j : j + 1, :] = inverse_ref[pl.ds(block, 1), :]
        side = sides[:, columns(peer)]
        folded = side[0:8] + pltpu.roll(side[8:16], 14, 1)
        chosen_ref[peer * EXTRA + SEND] = jnp.concatenate([rows_ref[...], folded], axis=0).astype(BF16)

    fill_and_send(fill, EXTRA, chosen_ref, chosen_hbm, sems)
    wait_all(copies)


def second_select(gathered, place, send_list, pick, n_row):
    part = n_row * RB
    peers = send_list.shape[0] // SEND
    return call(
        functools.partial(second_select_kernel, [offset for offset, _ in gathered], n_row),
        (
            pltpu.HBM((part, K, BS), BF16),
            pltpu.HBM((peers * EXTRA, K, BS), BF16),
            pltpu.HBM((K, BS), BF16),
            pltpu.HBM((part, BS), F32),
        ),
        [SMEM, SMEM] + [VMEM] * (len(gathered) + 1),
        (HBM, HBM, HBM, HBM),
        (
            pltpu.VMEM((part, K, BS), BF16),
            pltpu.VMEM((peers * EXTRA, K, BS), BF16),
            pltpu.VMEM((K, BS), BF16),
            pltpu.VMEM((part, BS), F32),
            pltpu.VMEM((SEND, BS), F32),
            pltpu.SemaphoreType.DMA((7,)),
        ),
        moved=3000000,
    )(place, send_list, pick, *[piece for _, piece in gathered])


def picks(send_list):
    peers = send_list.shape[0] // SEND
    owner = (send_list >> 5).reshape(peers, SEND)
    lane = jnp.broadcast_to(jnp.arange(BS, dtype=jnp.int32)[None, :], (peers, BS))
    target = jnp.where(lane < 14, lane, -1)
    target = jnp.concatenate([owner, target[:, SEND:]], axis=1).reshape(-1)
    return (jnp.arange(BS, dtype=jnp.int32)[:, None] == target[None, :]).astype(BF16)


def groups_of(count):
    return lax.div(count + GROUP - 1, GROUP)


def copy_group(source, target, sems, group):
    span = pl.ds(group * GROUP, GROUP)
    return pltpu.make_async_copy(source.at[span], target.at[span], sems.at[group])


def start_groups(count, source, target, sems):
    def start(group, carry):
        copy_group(source, target, sems, group).start()
        return carry

    lax.fori_loop(0, groups_of(count), start, 0)


def wait_groups(count, source, target, sems):
    def wait(group, carry):
        copy_group(source, target, sems, group).wait()
        return carry

    lax.fori_loop(0, groups_of(count), wait, 0)


def products_of(entries, weights, load):
    products = []
    for at in range(0, GROUP, 2):
        left = [load((entry >> 8) & 255) for entry in entries[at : at + 2]]
        product = dot_nn(jnp.concatenate(left, axis=0), jnp.concatenate(weights[at : at + 2], axis=1))
        rows = left[0].shape[0]
        products += [product[:rows, :BS], product[rows:, BS:]]
    return products


def work(count, list_ref, weights_hbm, held, sems, load, add):
    def step(group, carry):
        base = group * GROUP
        copy_group(weights_hbm, held, sems, group).wait()
        entries = [list_ref[base + j] for j in range(GROUP)]
        products = products_of(entries, [held[base + j] for j in range(GROUP)], load)
        for entry, product in zip(entries, products):
            add(entry >> 16, (entry >> 8) & 255, product)
        return carry

    lax.fori_loop(0, groups_of(count), step, 0)


WEIGHTS = pltpu.HBM((SLOTS, BS, BS), BF16)
HELD = pltpu.VMEM((SLOTS, BS, BS), BF16)
GROUP_SEMS = pltpu.SemaphoreType.DMA((SLOTS // GROUP,))
ROWS = shaped((RB + 1, K, BS), F32)


def scale_block(block, inverse):
    return (block.astype(F32) * inverse).astype(BF16)


def first_own_kernel(
    own_list, halo_list, count_ref, part_ref, coupling_ref, acc_ref, own_hbm, halo_hbm, held, own_held, halo_held, sems,
    own_sems, halo_sems,
):
    live = count_ref[2]
    start_groups(live, coupling_ref, held, sems)
    acc_ref[...] = jnp.zeros_like(acc_ref)
    wait_groups(live, coupling_ref, held, sems)

    def own_step(group, carry):
        base = group * GROUP
        entries = [own_list[base + j] for j in range(GROUP)]
        weights = [held[entry & 255].T for entry in entries]
        for j in range(GROUP):
            own_held[base + j] = weights[j]
        copy_group(own_held, own_hbm, own_sems, group).start()
        products = products_of(entries, weights, lambda block: part_ref[block])
        for entry, product in zip(entries, products):
            row = entry >> 16
            acc_ref[row] = acc_ref[row] + product
        return carry

    def halo_step(group, carry):
        base = group * GROUP
        for j in range(GROUP):
            halo_held[base + j] = held[halo_list[base + j] & 255].T
        copy_group(halo_held, halo_hbm, halo_sems, group).start()
        return carry

    lax.fori_loop(0, groups_of(count_ref[0]), own_step, 0)
    lax.fori_loop(0, groups_of(count_ref[1]), halo_step, 0)
    wait_groups(count_ref[0], own_held, own_hbm, own_sems)
    wait_groups(count_ref[1], halo_held, halo_hbm, halo_sems)


def first_own(own_list, halo_list, counts, part_tiles, coupling):
    return call(
        first_own_kernel,
        (pltpu.HBM(ROWS.shape, F32), WEIGHTS, WEIGHTS),
        [SMEM, SMEM, SMEM, VMEM, HBM],
        (VMEM, HBM, HBM),
        (HELD, HELD, HELD, GROUP_SEMS, GROUP_SEMS, GROUP_SEMS),
        flops=2 * SLOTS * K * BS * BS,
        moved=10000000,
    )(own_list, halo_list, counts, in_hbm(part_tiles), in_hbm(coupling))


def image_kernel(
    list_ref, count_ref, halo_ref, weights_hbm, own_hbm, basis_ref, degree_ref, image_hbm, tiles_ref, halo_hbm, image_ref,
    out_sems, acc_ref, held, sems,
):
    own = start_copies([(own_hbm, acc_ref)], out_sems, 2)
    start_groups(count_ref[1], weights_hbm, held, sems)
    copies = start_copies([(halo_ref, halo_hbm)], out_sems)
    wait_all(own)

    def load(block):
        return halo_ref[block]

    def add(row, block, product):
        acc_ref[row] = acc_ref[row] + product

    work(count_ref[1], list_ref, weights_hbm, held, sems, load, add)
    top = jnp.zeros((K, BS), F32)
    bottom = jnp.zeros((K, BS), F32)
    for block in range(RB):
        at = columns(block)
        basis = basis_ref[:, at]
        image = degree_ref[block : block + 1, :] * basis - acc_ref[block]
        image_ref[:, at] = image
        top = top + basis * image
        bottom = bottom + basis * basis
    copies += start_copies([(image_ref, image_hbm)], out_sems, 1)
    top = jnp.sum(top, axis=1, keepdims=True)
    bottom = jnp.sum(bottom, axis=1, keepdims=True)
    usable = bottom > 1e-30
    quotient = jnp.where(usable, top / jnp.where(usable, bottom, 1.0), 0.0).astype(BF16).astype(F32)
    for block in range(RB):
        at = columns(block)
        residual = (image_ref[:, at] - quotient * basis_ref[:, at]) / degree_ref[block : block + 1, :]
        tiles_ref[block] = residual.astype(BF16)
    lane = iota2((K, BS), 1)
    side = jnp.where(lane == 0, quotient, 0.0)
    for at, value in enumerate(split3(top) + split3(bottom)):
        side = jnp.where(lane == 1 + at, value, side)
    tiles_ref[RB] = side.astype(BF16)
    for half in range(2):
        tiles_ref[RB + 1 + half] = (1.0 / degree_ref[half * HALF : (half + 1) * HALF]).astype(BF16)
    wait_all(copies)


def make_image(halo_list, counts, halo_tiles, weights, own, basis, degree):
    return call(
        image_kernel,
        (pltpu.HBM(basis.shape, F32), shaped((RB + 3, K, BS), BF16), pltpu.HBM(halo_tiles.shape, BF16)),
        [SMEM, SMEM, VMEM, HBM, HBM, VMEM, VMEM],
        (HBM, VMEM, HBM),
        (
            pltpu.VMEM(basis.shape, F32),
            pltpu.SemaphoreType.DMA((3,)),
            pltpu.VMEM((RB + 1, K, BS), F32),
            HELD,
            GROUP_SEMS,
        ),
        flops=2 * SLOTS * K * BS * BS,
        moved=8000000,
    )(halo_list, counts, halo_tiles, in_hbm(weights), in_hbm(own), basis, degree)


def second_own_kernel(
    list_ref, count_ref, part_ref, table_ref, basis_part_ref, inverse_ref, weights_hbm, acc_ref, scaled_ref, quotient_ref,
    held, sems,
):
    start_groups(count_ref[0], weights_hbm, held, sems)
    acc_ref[...] = jnp.zeros_like(acc_ref)
    scaled_ref[...] = jnp.zeros_like(scaled_ref)
    table = table_ref[...].astype(F32)
    for owner in range(quotient_ref.shape[0]):
        quotient_ref[owner] = jnp.broadcast_to(table[:, owner : owner + 1], (K, BS))

    def load(block):
        scaled = scale_block(basis_part_ref[block], inverse_ref[pl.ds(block, 1), :])
        return jnp.concatenate([part_ref[block], scaled], axis=0)

    def add(row, block, product):
        acc_ref[row] = acc_ref[row] + (product[0:K] + quotient_ref[block >> 5] * product[K:])
        scaled_ref[row] = scaled_ref[row] + product[K:]

    work(count_ref[0], list_ref, weights_hbm, held, sems, load, add)


def second_own(own_list, counts, part_tiles, table, basis_part, inverse, weights, n_row):
    return call(
        second_own_kernel,
        (pltpu.HBM(ROWS.shape, F32), pltpu.HBM(ROWS.shape, F32)),
        [SMEM, SMEM, VMEM, VMEM, VMEM, VMEM, HBM],
        (VMEM, VMEM),
        (pltpu.VMEM((n_row, K, BS), F32), HELD, GROUP_SEMS),
        flops=4 * SLOTS * K * BS * BS,
        moved=10000000,
    )(own_list, counts, *map(in_hbm, (part_tiles, table, basis_part, inverse, weights)))


def spread_kernel(taken_ref, given_ref):
    total = taken_ref[0]
    for peer in range(1, taken_ref.shape[0]):
        total = total + taken_ref[peer]
    for peer in range(given_ref.shape[0]):
        given_ref[peer] = total


def add_and_repeat(taken, peers):
    return call(
        spread_kernel, shaped((peers,) + taken.shape[1:], F32), [VMEM], VMEM, moved=400000
    )(taken)


def square(value, wide_ref):
    rows, cols = value.shape
    wide_ref[...] = jnp.zeros_like(wide_ref)
    wide_ref[0:rows, 0:cols] = value
    return wide_ref[...]


def pack_grams(wide):
    row = iota2((BS, BS), 0)
    lane = iota2((BS, BS), 1)
    wide_b = jnp.where(lane < 48, wide, 0.0)
    wide_a = jnp.where(lane < 48, pltpu.roll(wide, BS - 48, 1), 0.0)
    both = 0.5 * (wide_a + wide_a.T)
    packed = jnp.where(row <= lane, wide_b, both)
    diagonal = jnp.sum(jnp.where(row == lane, both, 0.0), axis=1, keepdims=True)
    low, high = packed[0:24], pltpu.roll(packed[24:48], 48, 1)
    at = iota2((24, BS), 1)
    out = jnp.where(at < 48, low, high)
    out = jnp.where(at == 96, diagonal[0:24], out)
    return jnp.where(at == 97, diagonal[24:48], out)


def unpack_grams(packed, wide_ref):
    wide_ref[...] = jnp.zeros_like(wide_ref)
    at = iota2((24, BS), 1)
    wide_ref[0:24] = jnp.where(at < 48, packed, 0.0)
    wide_ref[24:48] = jnp.where(at < 48, pltpu.roll(packed, 80, 1), 0.0)
    wide = wide_ref[...]
    flipped = wide.T
    row = iota2((48, BS), 0)
    lane = iota2((48, BS), 1)
    wide, flipped = wide[0:48], flipped[0:48]
    diagonal = jnp.concatenate([packed[:, 96:97], packed[:, 97:98]], axis=0)
    gram_b = jnp.where(row <= lane, wide, flipped)
    gram_a = jnp.where(row == lane, diagonal, jnp.where(row > lane, wide, flipped))
    return gram_b, gram_a


def gram_kernel(
    list_ref, count_ref, halo_ref, weights_hbm, basis_halo_hbm, own_hbm, own_scaled_hbm, basis_hbm, image_hbm, degree_hbm,
    previous_hbm, previous_image_hbm, stack, packed_ref, basis_halo_ref, acc_ref, scaled_ref, degree_ref,
    in_sems, held, sems, side_ref, quotient_ref, inverse_ref, wide_ref,
):
    early = [(basis_halo_hbm, basis_halo_ref), (own_hbm, acc_ref), (own_scaled_hbm, scaled_ref)]
    late = [
        (basis_hbm, stack.at[0:16]),
        (previous_hbm, stack.at[32:48]),
        (image_hbm, stack.at[48:64]),
        (previous_image_hbm, stack.at[80:96]),
        (degree_hbm, degree_ref),
    ]
    early = start_copies(early, in_sems)
    start_groups(count_ref[1], weights_hbm, held, sems)
    late = start_copies(late, in_sems, 3)
    peers = halo_ref.shape[0] // EXTRA
    lane = iota2((K, BS), 1)
    total = jnp.zeros((K, BS), F32)
    for peer in range(peers):
        tile = halo_ref[peer * EXTRA + SEND].astype(F32)
        inverse_ref[peer * SEND : (peer + 1) * SEND, :] = tile[0:8]
        unfolded = [tile[8:16], pltpu.roll(tile[8:16], BS - 14, 1)]
        side = jnp.where(lane < 14, jnp.concatenate(unfolded, axis=0), 0.0)
        side_ref[peer * K : (peer + 1) * K, :] = side.astype(BF16)
        total = total + side
    side = side_ref[...]
    for j in range(SEND):
        spread = (iota2((BS, BS), 0) == j).astype(F32).astype(BF16)
        quotient_ref[j] = dot_nn(side, spread).reshape(peers, K, BS)
    top = jnp.sum(jnp.where((lane >= 8) & (lane <= 10), total, 0.0), axis=1, keepdims=True)
    bottom = jnp.sum(jnp.where((lane >= 11) & (lane <= 13), total, 0.0), axis=1, keepdims=True)
    theta = top / bottom
    wait_all(early)

    def load(block):
        scaled = scale_block(basis_halo_ref[block], inverse_ref[pl.ds(block, 1), :])
        return jnp.concatenate([halo_ref[block + (block >> 3)], scaled], axis=0)

    def add(row, block, product):
        quotient = quotient_ref[block & 7, block >> 3]
        acc_ref[row] = acc_ref[row] + (product[0:K] + quotient * product[K:])
        scaled_ref[row] = scaled_ref[row] + product[K:]

    work(count_ref[1], list_ref, weights_hbm, held, sems, load, add)
    wait_all(late)
    for block in range(RB):
        at = columns(block)
        degree = degree_ref[block : block + 1, :]
        residual = (stack[48:64, at] - theta * stack[0:16, at]) / degree
        stack[16:32, at] = residual
        stack[64:80, at] = degree * residual - (acc_ref[block] - theta * scaled_ref[block])
    packed = pack_grams(square(dot_nt(stack[0:48], stack[...], HIGHEST), wide_ref))
    for peer in range(packed_ref.shape[0]):
        packed_ref[peer] = packed


def make_grams(
    halo_list, counts, halo_tiles, weights, basis_halo, own, scaled, basis, image, degree, previous, previous_image, n_dom
):
    return call(
        gram_kernel,
        (shaped((6 * K, basis.shape[1]), F32), shaped((n_dom, 24, BS), F32)),
        [SMEM, SMEM, VMEM] + [HBM] * 9,
        (VMEM, VMEM),
        (
            pltpu.VMEM(basis_halo.shape, BF16),
            pltpu.VMEM((RB + 1, K, BS), F32),
            pltpu.VMEM((RB + 1, K, BS), F32),
            pltpu.VMEM(degree.shape, F32),
            pltpu.SemaphoreType.DMA((8,)),
            HELD,
            GROUP_SEMS,
            pltpu.VMEM((n_dom * K, BS), BF16),
            pltpu.VMEM((SEND, n_dom, K, BS), F32),
            pltpu.VMEM((n_dom * SEND, BS), F32),
            pltpu.VMEM((BS, BS), F32),
        ),
        flops=2 * SLOTS * K * BS * BS,
        moved=10000000,
    )(
        halo_list, counts, halo_tiles,
        *map(in_hbm, (weights, basis_halo, own, scaled, basis, image, degree, previous, previous_image)),
    )


def inverse_factor(gram, n):
    row = iota2((n, BS), 0)
    lane = iota2((n, BS), 1)
    work = jnp.where(lane < n, gram, jnp.where(lane == row + n, 1.0, 0.0))
    for first in range(0, n, 8):
        left = [jnp.broadcast_to(work[:, first + j : first + j + 1], (n, BS)) for j in range(8)]
        rows = [work[first + j : first + j + 1, :] for j in range(8)]
        for j in range(8):
            scale = lax.rsqrt(left[j][first + j : first + j + 1, :])
            rows[j] = rows[j] * scale
            left[j] = jnp.where(row > first + j, left[j] * scale, 0.0)
            for k in range(j + 1, 8):
                entry = left[j][first + k : first + k + 1, :]
                rows[k] = rows[k] - entry * rows[j]
                left[k] = left[k] - left[j] * entry
        for j in range(8):
            work = jnp.where(row == first + j, rows[j], work - left[j] * rows[j])
    return pltpu.roll(work, BS - n, 1)


def final_kernel(
    root_rows, taken_ref, stack_ref, new_basis_ref, new_image_ref, wide_ref
):
    packed = taken_ref[0]
    for peer in range(1, taken_ref.shape[0]):
        packed = packed + taken_ref[peer]
    gram_b, gram_a = unpack_grams(packed, wide_ref)
    inverse = inverse_factor(gram_b, 48)[:, 0:48]
    symmetric = gram_a[:, 0:48]
    reduced = dot_nt(dot_nn(inverse, symmetric, HIGHEST), inverse, HIGHEST)
    wide = square(reduced, wide_ref)
    reduced = 0.5 * (wide + wide.T)[0:48, 0:48]
    spread = jnp.max(jnp.sum(jnp.abs(reduced), axis=1, keepdims=True), axis=0, keepdims=True)
    row = iota2((48, 48), 0)
    lane = iota2((48, 48), 1)
    filter_mat = (jnp.where(row == lane, spread, 0.0) - reduced) / (2.0 * spread)
    turned = filter_mat[0:16, :]
    for repeat in range(3):
        turned = dot_nn(turned, filter_mat, HIGHEST)
    inner = dot_nt(turned, turned, HIGHEST)
    wide_ref[...] = jnp.zeros_like(wide_ref)
    wide_ref[0:16, 0:16] = inner
    sub_inverse = inverse_factor(wide_ref[0:16, :], 16)[:, 0:16]
    coeff = dot_nn(dot_nn(sub_inverse, turned, HIGHEST), inverse, HIGHEST) * root_rows
    new_basis_ref[...] = dot_nn(coeff, stack_ref[0:48], HIGHEST)
    new_image_ref[...] = dot_nn(coeff, stack_ref[48:96], HIGHEST)


def finish(root_rows, packed, stack):
    shape = (K, stack.shape[1])
    return call(
        functools.partial(final_kernel, root_rows),
        (shaped(shape, F32), shaped(shape, F32)),
        [VMEM] * 2,
        (VMEM, VMEM),
        (pltpu.VMEM((BS, BS), F32),),
        flops=1000000,
        moved=3000000,
    )(packed, stack)


def to_all(value, axis):
    return lax.all_to_all(value, axis, split_axis=0, concat_axis=0, tiled=True)


def body(
    n_dom, n_row,
    basis, previous, previous_image, degree, coupling, slot_row, slot_column, send_lists, live_slots,
):
    part = n_row * RB
    place = lax.axis_index("row").astype(jnp.int32).reshape(1)
    send_list = send_lists.reshape(n_dom * SEND)
    degree = degree.reshape(RB, BS)
    own_list, halo_list, counts = make_lists(slot_row, slot_column, live_slots, part)

    gathered = gather_row(cast_tiles(in_hbm(basis)), n_row)
    basis_part, chosen = first_select(gathered, place, send_list, n_row)
    halo_tiles = to_all(chosen, "dom")
    own, own_weights, halo_weights = first_own(own_list, halo_list, counts, basis_part, coupling)
    image, tiles, basis_halo = make_image(halo_list, counts, halo_tiles, halo_weights, own, basis, degree)

    gathered = gather_row(tiles, n_row)
    part_tiles, chosen, table, inverse = second_select(gathered, place, send_list, picks(send_list), n_row)
    halo_tiles = to_all(chosen, "dom")
    own, scaled = second_own(own_list, counts, part_tiles, table, basis_part, inverse, own_weights, n_row)
    stack, packed = make_grams(
        halo_list, counts, halo_tiles, halo_weights, basis_halo, own, scaled, basis, image, degree, previous, previous_image,
        n_dom,
    )
    packed = to_all(add_and_repeat(to_all(packed, "dom"), n_row), "row")
    root_rows = math.sqrt(basis.shape[1] * n_dom * n_row)
    return finish(root_rows, packed, stack)


def solution(mesh):
    split = P(None, ("dom", "row"))
    flat = P(("dom", "row"))
    return jax.shard_map(
        functools.partial(body, mesh.shape["dom"], mesh.shape["row"]),
        mesh=mesh,
        in_specs=(
            split, split, split, flat, P(("dom", "row"), None, None), flat, flat, P("dom", None, None), flat,
        ),
        out_specs=(split, split),
        check_vma=False,
    )
```

```python
import functools
import math

import jax
import jax.numpy as jnp
from jax import lax
from jax.experimental import pallas as pl
from jax.experimental.pallas import tpu as pltpu
from jax.sharding import PartitionSpec as P

K = 16
BS = 128
RB = 32
SLOTS = 256
SEND = 8
HALF = RB // 2
EXTRA = SEND + 1
GROUP = 32
LEN = SLOTS + GROUP
F32 = jnp.float32
BF16 = jnp.bfloat16
HIGHEST = lax.Precision.HIGHEST
MARGIN = 6 * 1024 * 1024
SMEM = pl.BlockSpec(memory_space=pltpu.SMEM)
HBM = pl.BlockSpec(memory_space=pl.ANY)
VMEM = pl.BlockSpec(memory_space=pltpu.VMEM)


def size(array):
    return math.prod(array.shape) * jnp.dtype(array.dtype).itemsize


def call(kernel, out_shape, in_specs, out_specs, scratch=(), flops=0, moved=0):
    def run(*args):
        arrays = list(args) + jax.tree.leaves(out_shape) + [held for held in scratch if jnp.issubdtype(held.dtype, jnp.floating)]
        return pl.pallas_call(
            kernel,
            out_shape=out_shape,
            in_specs=in_specs,
            out_specs=out_specs,
            scratch_shapes=scratch,
            compiler_params=pltpu.CompilerParams(vmem_limit_bytes=MARGIN + sum(map(size, arrays))),
            cost_estimate=pl.CostEstimate(flops=flops, bytes_accessed=moved, transcendentals=0),
        )(*args)

    return run


def shaped(shape, dtype):
    return jax.ShapeDtypeStruct(shape, dtype)


def in_hbm(value):
    return pltpu.with_memory_space_constraint(value, pltpu.HBM)


def start_copies(pairs, sems, first=0):
    copies = [pltpu.make_async_copy(source, target, sems.at[first + i]) for i, (source, target) in enumerate(pairs)]
    for copy in copies:
        copy.start()
    return copies


def wait_all(copies):
    for copy in copies:
        copy.wait()


def dot_nt(left, right, precision=None):
    return lax.dot_general(
        left, right, (((1,), (1,)), ((), ())), precision=precision, preferred_element_type=F32
    )


def dot_nn(left, right, precision=None):
    return lax.dot_general(
        left, right, (((1,), (0,)), ((), ())), precision=precision, preferred_element_type=F32
    )


def columns(block):
    return slice(block * BS, (block + 1) * BS)


def iota2(shape, axis):
    return lax.broadcasted_iota(jnp.int32, shape, axis)


def list_kernel(part, row_ref, column_ref, live_ref, own_ref, halo_ref, count_ref):
    live = live_ref[0]

    def step(quad, counts):
        n_own, n_halo = counts
        for j in range(4):
            slot = quad * 4 + j
            column = column_ref[slot]
            entry = slot + (row_ref[slot] << 16)
            own_ref[n_own] = entry + (column << 8)
            halo_ref[n_halo] = entry + ((column - part) << 8)
            used = slot < live
            is_own = used & (column < part)
            is_halo = used & (column >= part)
            n_own = n_own + is_own.astype(jnp.int32)
            n_halo = n_halo + is_halo.astype(jnp.int32)
        return n_own, n_halo

    n_own, n_halo = lax.fori_loop(0, lax.div(live + 3, 4), step, (jnp.int32(0), jnp.int32(0)))
    for ref, count in ((own_ref, n_own), (halo_ref, n_halo)):
        for extra in range(GROUP):
            ref[count + extra] = RB << 16
    count_ref[0] = n_own
    count_ref[1] = n_halo
    count_ref[2] = live


def make_lists(slot_row, slot_column, live_slots, part):
    return call(
        functools.partial(list_kernel, part),
        (shaped((LEN,), jnp.int32), shaped((LEN,), jnp.int32), shaped((3,), jnp.int32)),
        [SMEM, SMEM, SMEM],
        (SMEM, SMEM, SMEM),
        moved=20000,
    )(slot_row, slot_column, live_slots)


def split3(value):
    high = value.astype(BF16).astype(F32)
    rest = value - high
    middle = rest.astype(BF16).astype(F32)
    return high, middle, (rest - middle).astype(BF16).astype(F32)


def cast_kernel(field_hbm, tiles_ref, field_ref, sems):
    wait_all(start_copies([(field_hbm, field_ref)], sems))
    for block in range(RB):
        tiles_ref[block] = field_ref[:, columns(block)].astype(BF16)


def cast_tiles(field):
    return call(
        cast_kernel,
        shaped((RB, K, BS), BF16),
        [HBM],
        VMEM,
        (pltpu.VMEM(field.shape, F32), pltpu.SemaphoreType.DMA((1,))),
        moved=400000,
    )(field)


def gather_row(tiles, n_row):
    def shifted(value, shift):
        return lax.ppermute(value, "row", [(i, (i + shift) % n_row) for i in range(n_row)])

    pieces = [(0, tiles)]
    from_below = from_above = tiles
    for step in range(1, n_row // 2):
        from_below = shifted(from_below, 1)
        from_above = shifted(from_above, -1)
        pieces += [(-step, from_below), (step, from_above)]
    return pieces + [(n_row // 2, shifted(tiles, n_row // 2))]


def placed(offsets, pieces, n_row, place):
    return [(lax.rem(place + offset + n_row, n_row), piece) for offset, piece in zip(offsets, pieces)]


def fill_and_send(fill, tiles, chosen_ref, chosen_hbm, sems, others):
    peers = chosen_ref.shape[0] // tiles
    quarter = max(1, peers // 4)
    copies = []
    for at in range(peers // quarter):
        for peer in range(at * quarter, (at + 1) * quarter):
            fill(peer)
        span = pl.ds(at * quarter * tiles, quarter * tiles)
        copies.append(pltpu.make_async_copy(chosen_ref.at[span], chosen_hbm.at[span], sems.at[at]))
        copies[-1].start()
        if at == 0:
            copies += start_copies(others, sems, 4)
    wait_all(copies)


def first_select_kernel(offsets, n_row, place_ref, send_ref, *refs):
    pieces, (part_hbm, chosen_hbm, part_ref, chosen_ref, sems) = refs[:-5], refs[-5:]
    for owner, piece in placed(offsets, pieces, n_row, place_ref[0]):
        part_ref[pl.ds(owner * RB, RB)] = piece[...]

    def fill(peer):
        for j in range(SEND):
            chosen_ref[peer * SEND + j] = part_ref[send_ref[peer * SEND + j]]

    fill_and_send(fill, SEND, chosen_ref, chosen_hbm, sems, [(part_ref, part_hbm)])


def first_select(gathered, place, send_list, n_row):
    part = n_row * RB
    count = send_list.shape[0]
    return call(
        functools.partial(first_select_kernel, [offset for offset, _ in gathered], n_row),
        (pltpu.HBM((part, K, BS), BF16), pltpu.HBM((count, K, BS), BF16)),
        [SMEM, SMEM] + [VMEM] * len(gathered),
        (HBM, HBM),
        (pltpu.VMEM((part, K, BS), BF16), pltpu.VMEM((count, K, BS), BF16), pltpu.SemaphoreType.DMA((5,))),
        moved=3000000,
    )(place, send_list, *[piece for _, piece in gathered])


def second_select_kernel(offsets, n_row, place_ref, send_ref, pick_ref, *refs):
    pieces, (part_hbm, chosen_hbm, table_hbm, inverse_hbm) = refs[:-10], refs[-10:-6]
    part_ref, chosen_ref, table_ref, inverse_ref, rows_ref, sems = refs[-6:]
    lane = iota2((K, BS), 1)
    table = jnp.zeros((K, BS), F32)
    side_sum = jnp.zeros((K, BS), F32)
    for owner, piece in placed(offsets, pieces, n_row, place_ref[0]):
        part_ref[pl.ds(owner * RB, RB)] = piece[0:RB]
        for half in range(2):
            at = pl.multiple_of(owner * RB + half * HALF, HALF)
            inverse_ref[pl.ds(at, HALF), :] = piece[RB + 1 + half].astype(F32)
        side = piece[RB].astype(F32)
        table = jnp.where(lane == owner, side[:, 0:1], table)
        side_sum = side_sum + side
    top = jnp.sum(jnp.where((lane >= 1) & (lane <= 3), side_sum, 0.0), axis=1, keepdims=True)
    bottom = jnp.sum(jnp.where((lane >= 4) & (lane <= 6), side_sum, 0.0), axis=1, keepdims=True)
    for at, value in enumerate(split3(top) + split3(bottom)):
        table = jnp.where(lane == 8 + at, value, table)
    table = table.astype(BF16)
    table_ref[...] = table
    sides = dot_nn(table, pick_ref[...])

    def fill(peer):
        for j in range(SEND):
            block = send_ref[peer * SEND + j]
            chosen_ref[peer * EXTRA + j] = part_ref[block]
            rows_ref[j : j + 1, :] = inverse_ref[pl.ds(block, 1), :]
        side = sides[:, columns(peer)]
        folded = side[0:8] + pltpu.roll(side[8:16], 14, 1)
        chosen_ref[peer * EXTRA + SEND] = jnp.concatenate([rows_ref[...], folded], axis=0).astype(BF16)

    others = [(part_ref, part_hbm), (table_ref, table_hbm), (inverse_ref, inverse_hbm)]
    fill_and_send(fill, EXTRA, chosen_ref, chosen_hbm, sems, others)


def second_select(gathered, place, send_list, pick, n_row):
    part = n_row * RB
    peers = send_list.shape[0] // SEND
    return call(
        functools.partial(second_select_kernel, [offset for offset, _ in gathered], n_row),
        (
            pltpu.HBM((part, K, BS), BF16),
            pltpu.HBM((peers * EXTRA, K, BS), BF16),
            pltpu.HBM((K, BS), BF16),
            pltpu.HBM((part, BS), F32),
        ),
        [SMEM, SMEM] + [VMEM] * (len(gathered) + 1),
        (HBM, HBM, HBM, HBM),
        (
            pltpu.VMEM((part, K, BS), BF16),
            pltpu.VMEM((peers * EXTRA, K, BS), BF16),
            pltpu.VMEM((K, BS), BF16),
            pltpu.VMEM((part, BS), F32),
            pltpu.VMEM((SEND, BS), F32),
            pltpu.SemaphoreType.DMA((7,)),
        ),
        moved=3000000,
    )(place, send_list, pick, *[piece for _, piece in gathered])


def picks(send_list):
    peers = send_list.shape[0] // SEND
    owner = (send_list >> 5).reshape(peers, SEND)
    lane = jnp.broadcast_to(jnp.arange(BS, dtype=jnp.int32)[None, :], (peers, BS))
    target = jnp.where(lane < 14, lane, -1)
    target = jnp.concatenate([owner, target[:, SEND:]], axis=1).reshape(-1)
    return (jnp.arange(BS, dtype=jnp.int32)[:, None] == target[None, :]).astype(BF16)


def groups_of(count):
    return lax.div(count + GROUP - 1, GROUP)


def copy_group(source, target, sems, group):
    span = pl.ds(group * GROUP, GROUP)
    return pltpu.make_async_copy(source.at[span], target.at[span], sems.at[group])


def start_groups(count, source, target, sems):
    def start(group, carry):
        copy_group(source, target, sems, group).start()
        return carry

    lax.fori_loop(0, groups_of(count), start, 0)


def wait_groups(count, source, target, sems):
    def wait(group, carry):
        copy_group(source, target, sems, group).wait()
        return carry

    lax.fori_loop(0, groups_of(count), wait, 0)


def products_of(entries, weights, load):
    products = []
    for at in range(0, GROUP, 2):
        left = [load((entry >> 8) & 255) for entry in entries[at : at + 2]]
        product = dot_nn(jnp.concatenate(left, axis=0), jnp.concatenate(weights[at : at + 2], axis=1))
        rows = left[0].shape[0]
        products += [product[:rows, :BS], product[rows:, BS:]]
    return products


def work(count, list_ref, weights_hbm, held, sems, load, add):
    def step(group, carry):
        base = group * GROUP
        copy_group(weights_hbm, held, sems, group).wait()
        entries = [list_ref[base + j] for j in range(GROUP)]
        products = products_of(entries, [held[base + j] for j in range(GROUP)], load)
        for entry, product in zip(entries, products):
            add(entry >> 16, (entry >> 8) & 255, product)
        return carry

    lax.fori_loop(0, groups_of(count), step, 0)


WEIGHTS = pltpu.HBM((SLOTS, BS, BS), BF16)
HELD = pltpu.VMEM((SLOTS, BS, BS), BF16)
GROUP_SEMS = pltpu.SemaphoreType.DMA((SLOTS // GROUP,))
ROWS = shaped((RB + 1, K, BS), F32)


def scale_block(block, inverse):
    return (block.astype(F32) * inverse).astype(BF16)


def first_own_kernel(
    own_list, halo_list, count_ref, part_ref, coupling_ref, acc_ref, own_hbm, halo_hbm, held, own_held, halo_held, sems,
    own_sems, halo_sems,
):
    live = count_ref[2]
    start_groups(live, coupling_ref, held, sems)
    acc_ref[...] = jnp.zeros_like(acc_ref)
    wait_groups(live, coupling_ref, held, sems)

    def own_step(group, carry):
        base = group * GROUP
        entries = [own_list[base + j] for j in range(GROUP)]
        weights = [held[entry & 255].T for entry in entries]
        for j in range(GROUP):
            own_held[base + j] = weights[j]
        copy_group(own_held, own_hbm, own_sems, group).start()
        products = products_of(entries, weights, lambda block: part_ref[block])
        for entry, product in zip(entries, products):
            row = entry >> 16
            acc_ref[row] = acc_ref[row] + product
        return carry

    def halo_step(group, carry):
        base = group * GROUP
        for j in range(GROUP):
            halo_held[base + j] = held[halo_list[base + j] & 255].T
        copy_group(halo_held, halo_hbm, halo_sems, group).start()
        return carry

    lax.fori_loop(0, groups_of(count_ref[0]), own_step, 0)
    lax.fori_loop(0, groups_of(count_ref[1]), halo_step, 0)
    wait_groups(count_ref[0], own_held, own_hbm, own_sems)
    wait_groups(count_ref[1], halo_held, halo_hbm, halo_sems)


def first_own(own_list, halo_list, counts, part_tiles, coupling):
    return call(
        first_own_kernel,
        (pltpu.HBM(ROWS.shape, F32), WEIGHTS, WEIGHTS),
        [SMEM, SMEM, SMEM, VMEM, HBM],
        (VMEM, HBM, HBM),
        (HELD, HELD, HELD, GROUP_SEMS, GROUP_SEMS, GROUP_SEMS),
        flops=2 * SLOTS * K * BS * BS,
        moved=10000000,
    )(own_list, halo_list, counts, in_hbm(part_tiles), in_hbm(coupling))


def image_kernel(
    list_ref, count_ref, halo_ref, weights_hbm, own_hbm, basis_ref, degree_ref, image_hbm, tiles_ref, halo_hbm, image_ref,
    out_sems, own_ref, acc_ref, held, sems,
):
    start_groups(count_ref[1], weights_hbm, held, sems)
    own = start_copies([(own_hbm, own_ref)], out_sems, 2)
    copies = start_copies([(halo_ref, halo_hbm)], out_sems)
    acc_ref[...] = jnp.zeros_like(acc_ref)

    def load(block):
        return halo_ref[block]

    def add(row, block, product):
        acc_ref[row] = acc_ref[row] + product

    work(count_ref[1], list_ref, weights_hbm, held, sems, load, add)
    wait_all(own)
    top = jnp.zeros((K, BS), F32)
    bottom = jnp.zeros((K, BS), F32)
    for block in range(RB):
        at = columns(block)
        basis = basis_ref[:, at]
        image = degree_ref[block : block + 1, :] * basis - (own_ref[block] + acc_ref[block])
        image_ref[:, at] = image
        top = top + basis * image
        bottom = bottom + basis * basis
    copies += start_copies([(image_ref, image_hbm)], out_sems, 1)
    top = jnp.sum(top, axis=1, keepdims=True)
    bottom = jnp.sum(bottom, axis=1, keepdims=True)
    usable = bottom > 1e-30
    quotient = jnp.where(usable, top / jnp.where(usable, bottom, 1.0), 0.0).astype(BF16).astype(F32)
    for block in range(RB):
        at = columns(block)
        residual = (image_ref[:, at] - quotient * basis_ref[:, at]) / degree_ref[block : block + 1, :]
        tiles_ref[block] = residual.astype(BF16)
    lane = iota2((K, BS), 1)
    side = jnp.where(lane == 0, quotient, 0.0)
    for at, value in enumerate(split3(top) + split3(bottom)):
        side = jnp.where(lane == 1 + at, value, side)
    tiles_ref[RB] = side.astype(BF16)
    for half in range(2):
        tiles_ref[RB + 1 + half] = (1.0 / degree_ref[half * HALF : (half + 1) * HALF]).astype(BF16)
    wait_all(copies)


def make_image(halo_list, counts, halo_tiles, weights, own, basis, degree):
    return call(
        image_kernel,
        (pltpu.HBM(basis.shape, F32), shaped((RB + 3, K, BS), BF16), pltpu.HBM(halo_tiles.shape, BF16)),
        [SMEM, SMEM, VMEM, HBM, HBM, VMEM, VMEM],
        (HBM, VMEM, HBM),
        (
            pltpu.VMEM(basis.shape, F32),
            pltpu.SemaphoreType.DMA((3,)),
            pltpu.VMEM((RB + 1, K, BS), F32),
            pltpu.VMEM((RB + 1, K, BS), F32),
            HELD,
            GROUP_SEMS,
        ),
        flops=2 * SLOTS * K * BS * BS,
        moved=8000000,
    )(halo_list, counts, halo_tiles, in_hbm(weights), in_hbm(own), basis, degree)


def second_own_kernel(
    list_ref, count_ref, part_ref, table_ref, basis_part_ref, inverse_ref, weights_hbm, acc_ref, scaled_ref, quotient_ref,
    held, sems,
):
    start_groups(count_ref[0], weights_hbm, held, sems)
    acc_ref[...] = jnp.zeros_like(acc_ref)
    scaled_ref[...] = jnp.zeros_like(scaled_ref)
    table = table_ref[...].astype(F32)
    for owner in range(quotient_ref.shape[0]):
        quotient_ref[owner] = jnp.broadcast_to(table[:, owner : owner + 1], (K, BS))

    def load(block):
        scaled = scale_block(basis_part_ref[block], inverse_ref[pl.ds(block, 1), :])
        return jnp.concatenate([part_ref[block], scaled], axis=0)

    def add(row, block, product):
        acc_ref[row] = acc_ref[row] + (product[0:K] + quotient_ref[block >> 5] * product[K:])
        scaled_ref[row] = scaled_ref[row] + product[K:]

    work(count_ref[0], list_ref, weights_hbm, held, sems, load, add)


def second_own(own_list, counts, part_tiles, table, basis_part, inverse, weights, n_row):
    return call(
        second_own_kernel,
        (pltpu.HBM(ROWS.shape, F32), pltpu.HBM(ROWS.shape, F32)),
        [SMEM, SMEM, VMEM, VMEM, VMEM, VMEM, HBM],
        (VMEM, VMEM),
        (pltpu.VMEM((n_row, K, BS), F32), HELD, GROUP_SEMS),
        flops=4 * SLOTS * K * BS * BS,
        moved=10000000,
    )(own_list, counts, *map(in_hbm, (part_tiles, table, basis_part, inverse, weights)))


def spread_kernel(taken_ref, given_ref):
    total = taken_ref[0]
    for peer in range(1, taken_ref.shape[0]):
        total = total + taken_ref[peer]
    for peer in range(given_ref.shape[0]):
        given_ref[peer] = total


def add_and_repeat(taken, peers):
    return call(
        spread_kernel, shaped((peers,) + taken.shape[1:], F32), [VMEM], VMEM, moved=400000
    )(taken)


def square(value, wide_ref):
    rows, cols = value.shape
    wide_ref[...] = jnp.zeros_like(wide_ref)
    wide_ref[0:rows, 0:cols] = value
    return wide_ref[...]


def pack_grams(wide):
    row = iota2((BS, BS), 0)
    lane = iota2((BS, BS), 1)
    wide_b = jnp.where(lane < 48, wide, 0.0)
    wide_a = jnp.where(lane < 48, pltpu.roll(wide, BS - 48, 1), 0.0)
    both = 0.5 * (wide_a + wide_a.T)
    packed = jnp.where(row <= lane, wide_b, both)
    diagonal = jnp.sum(jnp.where(row == lane, both, 0.0), axis=1, keepdims=True)
    low, high = packed[0:24], pltpu.roll(packed[24:48], 48, 1)
    at = iota2((24, BS), 1)
    out = jnp.where(at < 48, low, high)
    out = jnp.where(at == 96, diagonal[0:24], out)
    return jnp.where(at == 97, diagonal[24:48], out)


def unpack_grams(packed, wide_ref):
    wide_ref[...] = jnp.zeros_like(wide_ref)
    at = iota2((24, BS), 1)
    wide_ref[0:24] = jnp.where(at < 48, packed, 0.0)
    wide_ref[24:48] = jnp.where(at < 48, pltpu.roll(packed, 80, 1), 0.0)
    wide = wide_ref[...]
    flipped = wide.T
    row = iota2((48, BS), 0)
    lane = iota2((48, BS), 1)
    wide, flipped = wide[0:48], flipped[0:48]
    diagonal = jnp.concatenate([packed[:, 96:97], packed[:, 97:98]], axis=0)
    gram_b = jnp.where(row <= lane, wide, flipped)
    gram_a = jnp.where(row == lane, diagonal, jnp.where(row > lane, wide, flipped))
    return gram_b, gram_a


def gram_kernel(
    list_ref, count_ref, halo_ref, weights_hbm, basis_halo_hbm, own_hbm, own_scaled_hbm, basis_hbm, image_hbm, degree_hbm,
    previous_hbm, previous_image_hbm, stack, packed_ref, basis_halo_ref, own_ref, own_scaled_ref, acc_ref,
    scaled_ref, degree_ref,
    in_sems, held, sems, side_ref, quotient_ref, inverse_ref, wide_ref,
):
    early = [(basis_halo_hbm, basis_halo_ref)]
    late = [
        (own_hbm, own_ref),
        (own_scaled_hbm, own_scaled_ref),
        (basis_hbm, stack.at[0:16]),
        (previous_hbm, stack.at[32:48]),
        (image_hbm, stack.at[48:64]),
        (previous_image_hbm, stack.at[80:96]),
        (degree_hbm, degree_ref),
    ]
    early = start_copies(early, in_sems)
    start_groups(count_ref[1], weights_hbm, held, sems)
    late = start_copies(late, in_sems, 1)
    acc_ref[...] = jnp.zeros_like(acc_ref)
    scaled_ref[...] = jnp.zeros_like(scaled_ref)
    peers = halo_ref.shape[0] // EXTRA
    lane = iota2((K, BS), 1)
    total = jnp.zeros((K, BS), F32)
    for peer in range(peers):
        tile = halo_ref[peer * EXTRA + SEND].astype(F32)
        inverse_ref[peer * SEND : (peer + 1) * SEND, :] = tile[0:8]
        unfolded = [tile[8:16], pltpu.roll(tile[8:16], BS - 14, 1)]
        side = jnp.where(lane < 14, jnp.concatenate(unfolded, axis=0), 0.0)
        side_ref[peer * K : (peer + 1) * K, :] = side.astype(BF16)
        total = total + side
    side = side_ref[...]
    for j in range(SEND):
        spread = (iota2((BS, BS), 0) == j).astype(F32).astype(BF16)
        quotient_ref[j] = dot_nn(side, spread).reshape(peers, K, BS)
    top = jnp.sum(jnp.where((lane >= 8) & (lane <= 10), total, 0.0), axis=1, keepdims=True)
    bottom = jnp.sum(jnp.where((lane >= 11) & (lane <= 13), total, 0.0), axis=1, keepdims=True)
    theta = top / bottom
    wait_all(early)

    def load(block):
        scaled = scale_block(basis_halo_ref[block], inverse_ref[pl.ds(block, 1), :])
        return jnp.concatenate([halo_ref[block + (block >> 3)], scaled], axis=0)

    def add(row, block, product):
        quotient = quotient_ref[block & 7, block >> 3]
        acc_ref[row] = acc_ref[row] + (product[0:K] + quotient * product[K:])
        scaled_ref[row] = scaled_ref[row] + product[K:]

    work(count_ref[1], list_ref, weights_hbm, held, sems, load, add)
    wait_all(late)
    for block in range(RB):
        at = columns(block)
        degree = degree_ref[block : block + 1, :]
        residual = (stack[48:64, at] - theta * stack[0:16, at]) / degree
        stack[16:32, at] = residual
        stack[64:80, at] = degree * residual - (
            own_ref[block] + acc_ref[block] - theta * (own_scaled_ref[block] + scaled_ref[block])
        )
    packed = pack_grams(square(dot_nt(stack[0:48], stack[...], HIGHEST), wide_ref))
    for peer in range(packed_ref.shape[0]):
        packed_ref[peer] = packed


def make_grams(
    halo_list, counts, halo_tiles, weights, basis_halo, own, scaled, basis, image, degree, previous, previous_image, n_dom
):
    return call(
        gram_kernel,
        (shaped((6 * K, basis.shape[1]), F32), shaped((n_dom, 24, BS), F32)),
        [SMEM, SMEM, VMEM] + [HBM] * 9,
        (VMEM, VMEM),
        (
            pltpu.VMEM(basis_halo.shape, BF16),
            pltpu.VMEM((RB + 1, K, BS), F32),
            pltpu.VMEM((RB + 1, K, BS), F32),
            pltpu.VMEM((RB + 1, K, BS), F32),
            pltpu.VMEM((RB + 1, K, BS), F32),
            pltpu.VMEM(degree.shape, F32),
            pltpu.SemaphoreType.DMA((8,)),
            HELD,
            GROUP_SEMS,
            pltpu.VMEM((n_dom * K, BS), BF16),
            pltpu.VMEM((SEND, n_dom, K, BS), F32),
            pltpu.VMEM((n_dom * SEND, BS), F32),
            pltpu.VMEM((BS, BS), F32),
        ),
        flops=2 * SLOTS * K * BS * BS,
        moved=10000000,
    )(
        halo_list, counts, halo_tiles,
        *map(in_hbm, (weights, basis_halo, own, scaled, basis, image, degree, previous, previous_image)),
    )


def inverse_factor(gram, n):
    row = iota2((n, BS), 0)
    lane = iota2((n, BS), 1)
    work = jnp.where(lane < n, gram, jnp.where(lane == row + n, 1.0, 0.0))
    for first in range(0, n, 8):
        left = [jnp.broadcast_to(work[:, first + j : first + j + 1], (n, BS)) for j in range(8)]
        rows = [work[first + j : first + j + 1, :] for j in range(8)]
        for j in range(8):
            scale = lax.rsqrt(left[j][first + j : first + j + 1, :])
            rows[j] = rows[j] * scale
            left[j] = jnp.where(row > first + j, left[j] * scale, 0.0)
            for k in range(j + 1, 8):
                entry = left[j][first + k : first + k + 1, :]
                rows[k] = rows[k] - entry * rows[j]
                left[k] = left[k] - left[j] * entry
        for j in range(8):
            work = jnp.where(row == first + j, rows[j], work - left[j] * rows[j])
    return pltpu.roll(work, BS - n, 1)


def final_kernel(
    root_rows, taken_ref, stack_ref, new_basis_hbm, new_image_hbm, wide_ref, new_basis_ref, new_image_ref, sems
):
    packed = taken_ref[0]
    for peer in range(1, taken_ref.shape[0]):
        packed = packed + taken_ref[peer]
    gram_b, gram_a = unpack_grams(packed, wide_ref)
    inverse = inverse_factor(gram_b, 48)[:, 0:48]
    symmetric = gram_a[:, 0:48]
    reduced = dot_nt(dot_nn(inverse, symmetric, HIGHEST), inverse, HIGHEST)
    wide = square(reduced, wide_ref)
    reduced = 0.5 * (wide + wide.T)[0:48, 0:48]
    spread = jnp.max(jnp.sum(jnp.abs(reduced), axis=1, keepdims=True), axis=0, keepdims=True)
    row = iota2((48, 48), 0)
    lane = iota2((48, 48), 1)
    filter_mat = (jnp.where(row == lane, spread, 0.0) - reduced) / (2.0 * spread)
    squared = dot_nn(filter_mat, filter_mat, HIGHEST)
    turned = dot_nn(squared[0:16, :], squared, HIGHEST)
    back = dot_nn(turned, inverse, HIGHEST)
    inner = dot_nt(turned, turned, HIGHEST)
    wide_ref[...] = jnp.zeros_like(wide_ref)
    wide_ref[0:16, 0:16] = inner
    sub_inverse = inverse_factor(wide_ref[0:16, :], 16)[:, 0:16]
    coeff = dot_nn(sub_inverse, back, HIGHEST) * root_rows
    copies = []
    half = stack_ref.shape[1] // 2
    for rows, out_ref, out_hbm in ((0, new_basis_ref, new_basis_hbm), (48, new_image_ref, new_image_hbm)):
        for start in (0, half):
            span = slice(start, start + half)
            out_ref[:, span] = dot_nn(coeff, stack_ref[rows : rows + 48, span], HIGHEST)
            span = pl.ds(start, half)
            copies += start_copies([(out_ref.at[:, span], out_hbm.at[:, span])], sems, len(copies))
    wait_all(copies)


def finish(root_rows, packed, stack):
    shape = (K, stack.shape[1])
    return call(
        functools.partial(final_kernel, root_rows),
        (pltpu.HBM(shape, F32), pltpu.HBM(shape, F32)),
        [VMEM] * 2,
        (HBM, HBM),
        (
            pltpu.VMEM((BS, BS), F32),
            pltpu.VMEM(shape, F32),
            pltpu.VMEM(shape, F32),
            pltpu.SemaphoreType.DMA((4,)),
        ),
        flops=1000000,
        moved=3000000,
    )(packed, stack)


def to_all(value, axis):
    return lax.all_to_all(value, axis, split_axis=0, concat_axis=0, tiled=True)


def body(
    n_dom, n_row,
    basis, previous, previous_image, degree, coupling, slot_row, slot_column, send_lists, live_slots,
):
    part = n_row * RB
    place = lax.axis_index("row").astype(jnp.int32).reshape(1)
    send_list = send_lists.reshape(n_dom * SEND)
    degree = degree.reshape(RB, BS)
    own_list, halo_list, counts = make_lists(slot_row, slot_column, live_slots, part)

    gathered = gather_row(cast_tiles(in_hbm(basis)), n_row)
    basis_part, chosen = first_select(gathered, place, send_list, n_row)
    halo_tiles = to_all(chosen, "dom")
    own, own_weights, halo_weights = first_own(own_list, halo_list, counts, basis_part, coupling)
    image, tiles, basis_halo = make_image(halo_list, counts, halo_tiles, halo_weights, own, basis, degree)

    gathered = gather_row(tiles, n_row)
    part_tiles, chosen, table, inverse = second_select(gathered, place, send_list, picks(send_list), n_row)
    halo_tiles = to_all(chosen, "dom")
    own, scaled = second_own(own_list, counts, part_tiles, table, basis_part, inverse, own_weights, n_row)
    stack, packed = make_grams(
        halo_list, counts, halo_tiles, halo_weights, basis_halo, own, scaled, basis, image, degree, previous, previous_image,
        n_dom,
    )
    packed = to_all(add_and_repeat(to_all(packed, "dom"), n_row), "row")
    root_rows = math.sqrt(basis.shape[1] * n_dom * n_row)
    return finish(root_rows, packed, stack)


def solution(mesh):
    split = P(None, ("dom", "row"))
    flat = P(("dom", "row"))
    return jax.shard_map(
        functools.partial(body, mesh.shape["dom"], mesh.shape["row"]),
        mesh=mesh,
        in_specs=(
            split, split, split, flat, P(("dom", "row"), None, None), flat, flat, P("dom", None, None), flat,
        ),
        out_specs=(split, split),
        check_vma=False,
    )
```
